32 devices in a mesh: section: 2 (over core), row: 4 (over y, x), col: 4 (over z).
Axes of the slice: x: 2, y: 2, z: 4, core: 2. Of those that a mesh axis runs over, the one named last changes fastest.
Arguments:
- section_input: bfloat16 [64, 61440], P('row', ('section', 'col')), may hold values from -6 to 6
- cache_three: bfloat16 [64, 30720], P('row', ('section', 'col')), may hold values from -6 to 6
- gain_three: float32 [192], replicated, may hold values from 0.25 to 1.75
- bias_three: float32 [192], replicated, may hold values from -2 to 2
- weight_three: bfloat16 [27, 36864], replicated, may hold values from -0.078125 to 0.078125
- weight_up: bfloat16 [9, 18432], replicated, may hold values from -0.15625 to 0.15625
- bias_up: float32 [96], replicated, may hold values from -2 to 2
- cache_four: bfloat16 [128, 30720], P('row', ('section', 'col')), may hold values from -6 to 6
- gain_four: float32 [96], replicated, may hold values from 0.25 to 1.75
- weight_four: bfloat16 [27, 9216], replicated, may hold values from -0.125 to 0.125
- bias_four: float32 [96], replicated, may hold values from -2 to 2
Outputs:
- frame_out: bfloat16 [128, 61440], P('row', ('section', 'col'))
The draws below stay inside these ranges and needn't reach their ends.
All inputs are finite; a program needn't handle non-finite values.
Results may differ from the reference program's by a relative error of at most 0.0085.
Values may be sent and summed in bfloat16 or wider, within the bound.
No kernel may reach another device: no remote copies, remote signals or barrier semaphores. Data moves between devices by JAX's collectives and lax.ppermute only.
A program may use at most 64 MiB of HBM per device.

```python
import jax
import jax.numpy as jnp
from jax import lax

C3 = 192
C4 = 96
FRAMES = 4
H3 = 64
W3 = 80
H4 = 128
W4 = 160


def steps_of(stream_key, dims, split, least, high):
    level = 1.0
    for position, shards_of in split:
        steps = jax.random.uniform(jax.random.fold_in(jax.random.fold_in(stream_key, 6), position), (shards_of,), jnp.float32, least / len(split), high / len(split))
        level = level * jnp.repeat(jnp.exp(steps), dims[position] // shards_of).reshape((-1,) + (1,) * (len(dims) - 1 - position))
    return level


def centred(key, extent, spread, reach, pieces=(), held_as=jnp.bfloat16):
    drawn = spread * jax.random.normal(key, extent, jnp.float32)
    if pieces:
        drawn = drawn * steps_of(key, extent, pieces, -0.22, 0.18)
    return jnp.clip(drawn, -reach, reach).astype(held_as)


def setup_inputs(seed: int = 0) -> dict:
    splits = jax.random.split(jax.random.key(seed), 12)
    section_input = centred(splits[0], (H3, W3 * FRAMES * C3), 1.0, 6.0, ((0, 4), (1, 8)))
    cache_three = centred(splits[1], (H3, W3 * 2 * C3), 1.0, 6.0, ((0, 4), (1, 8)))
    gain_three = jnp.clip(1.0 + 0.15 * jax.random.normal(splits[2], (C3,), jnp.float32), 0.25, 1.75)
    bias_three = centred(splits[3], (C3,), 0.3, 2.0, (), jnp.float32)
    weight_three = centred(splits[4], (27, C3 * C3), (27 * C3) ** -0.5, 0.078125)
    weight_up = centred(splits[5], (9, C4 * C3), (9 * C3) ** -0.5, 0.15625)
    bias_up = centred(splits[6], (C4,), 0.3, 2.0, (), jnp.float32)
    cache_four = centred(splits[7], (H4, W4 * 2 * C4), 1.0, 6.0, ((0, 4), (1, 8)))
    gain_four = jnp.clip(1.0 + 0.15 * jax.random.normal(splits[8], (C4,), jnp.float32), 0.25, 1.75)
    weight_four = centred(splits[9], (27, C4 * C4), (27 * C4) ** -0.5, 0.125)
    bias_four = centred(splits[10], (C4,), 0.3, 2.0, (), jnp.float32)
    return {"section_input": section_input, "cache_three": cache_three, "gain_three": gain_three, "bias_three": bias_three, "weight_three": weight_three, "weight_up": weight_up, "bias_up": bias_up, "cache_four": cache_four, "gain_four": gain_four, "weight_four": weight_four, "bias_four": bias_four}


EPSILON = 1e-06

def norm_act(values, gain):
    widened = values.astype(jnp.float32)
    meansq = lax.optimization_barrier(jnp.mean(widened * widened, axis=-1, keepdims=True))
    scaled = widened * lax.rsqrt(meansq + EPSILON) * gain
    return jax.nn.silu(scaled).astype(jnp.bfloat16)

def causal_kernel(flat_weight, in_ch):
    out_ch = flat_weight.shape[1] // in_ch
    shaped = flat_weight.reshape(3, 3, 3, out_ch, in_ch).transpose(1, 2, 0, 4, 3)
    return shaped.reshape(3, 3, 3 * in_ch, out_ch)

def spatial_kernel(flat_weight, in_ch):
    out_ch = flat_weight.shape[1] // in_ch
    return flat_weight.reshape(3, 3, out_ch, in_ch).transpose(0, 1, 3, 2)

def run_conv(batch, kernel):
    return lax.conv_general_dilated(batch, kernel, (1, 1), 'VALID', dimension_numbers=('NHWC', 'HWIO', 'NHWC'), preferred_element_type=jnp.float32)

def causal_frames(stacked, kernel, in_ch, count):
    padded = jnp.pad(stacked, ((1, 1), (1, 1), (0, 0)))
    outputs = []
    for frame_pos in range(count):
        window = padded[:, :, frame_pos * in_ch:(frame_pos + 3) * in_ch]
        outputs.append(run_conv(window[None], kernel)[0])
    return jnp.stack(outputs)

def reference(section_input, cache_three, gain_three, bias_three, weight_three, weight_up, bias_up, cache_four, gain_four, weight_four, bias_four):
    features = section_input.reshape(H3, W3, FRAMES, C3)
    active_three = norm_act(features, gain_three).reshape(H3, W3, FRAMES * C3)
    stacked = jnp.concatenate([cache_three.reshape(H3, W3, 2 * C3), active_three], axis=2)
    conv_three = causal_frames(stacked, causal_kernel(weight_three, C3), C3, FRAMES) + bias_three
    result_three = (features.transpose(2, 0, 1, 3).astype(jnp.float32) + conv_three).astype(jnp.bfloat16)
    up_kernel = spatial_kernel(weight_up, C3)
    four_inputs = []
    for frame_pos in range(FRAMES):
        upsampled = jnp.repeat(jnp.repeat(result_three[frame_pos], 2, axis=0), 2, axis=1)
        padded = jnp.pad(upsampled, ((1, 1), (1, 1), (0, 0)))
        four_inputs.append((run_conv(padded[None], up_kernel)[0] + bias_up).astype(jnp.bfloat16))
    section_four_in = jnp.stack(four_inputs)
    active_four = norm_act(section_four_in, gain_four).transpose(1, 2, 0, 3).reshape(H4, W4, FRAMES * C4)
    stacked_four = jnp.concatenate([cache_four.reshape(H4, W4, 2 * C4), active_four], axis=2)
    conv_four = causal_frames(stacked_four, causal_kernel(weight_four, C4), C4, FRAMES) + bias_four
    result = (section_four_in.astype(jnp.float32) + conv_four).astype(jnp.bfloat16)
    return result.transpose(1, 2, 0, 3).reshape(H4, W4 * FRAMES * C4)
```

```python
import jax
import jax.numpy as jnp
from jax import lax
from jax.experimental import pallas as pl
from jax.experimental.pallas import tpu as pltpu
from jax.sharding import PartitionSpec as P

EPSILON = 1e-06
BF16 = jnp.bfloat16
F32 = jnp.float32

ROWS = 16
COLS = 10
C3 = 192
C4 = 96
FRAMES = 4
WIDE = COLS + 4
MID = COLS + 2
EXT = 24
FINE = 2 * COLS + 2
FROWS = 2 * ROWS
FEXT = 40
XW = COLS * FRAMES * C3
PW = COLS * 2 * C3
QW = 2 * COLS * 2 * C4
COLX = FRAMES * C3
COLP = 2 * C3
COLQ = 2 * C4


def nt_dot(lhs, rhs):
    return lax.dot_general(lhs, rhs, (((1,), (1,)), ((), ())), preferred_element_type=F32)


def silu(value):
    return value / (1.0 + jnp.exp(-value))


def lane_mask(rows, below):
    return lax.broadcasted_iota(jnp.int32, (rows, 128), 1) < below


def split_pair(v0, v1, v2):
    low = lane_mask(v0.shape[0], 64)
    r1 = pltpu.roll(v1, 64, 1)
    r2 = pltpu.roll(v2, 64, 1)
    zero = jnp.zeros_like(v1)
    return (v0, jnp.where(low, v1, zero)), (jnp.where(low, r1, r2), jnp.where(low, r2, zero))


def norm_pair(v0, v1, v2, gains):
    low = lane_mask(v0.shape[0], 64)
    sq1 = v1 * v1
    zero = jnp.zeros_like(v1)
    sum_a = jnp.sum(v0 * v0 + jnp.where(low, sq1, zero), axis=1, keepdims=True)
    sum_b = jnp.sum(v2 * v2 + jnp.where(low, zero, sq1), axis=1, keepdims=True)
    inv_a = lax.rsqrt(sum_a * (1.0 / C3) + EPSILON)
    inv_b = lax.rsqrt(sum_b * (1.0 / C3) + EPSILON)
    return (
        silu(v0 * inv_a * gains[0]),
        silu(v1 * jnp.where(low, inv_a, inv_b) * gains[1]),
        silu(v2 * inv_b * gains[2]),
    )


def main_kernel(
    x_ref, p_ref, q_ref, even_row, odd_row, even_col, odd_col,
    g3_ref, b3_ref, w3_ref, wu_ref, bu_ref, g4_ref, w4_ref, b4_ref,
    out_ref,
    raw, act, act_d, halo_d, res, res_d, res_h, wup, z4, s4, act4_d, w4p,
    *, row_count, col_count, col_size,
):
    row = lax.axis_index("row")
    col = lax.axis_index("section") * col_size + lax.axis_index("col")
    row_odd = lax.rem(row, 2) == 1
    col_odd = lax.rem(col, 2) == 1
    first_row, last_row = row == 0, row == row_count - 1
    first_col, last_col = col == 0, col == col_count - 1

    def wide(value):
        return value.astype(F32)

    above = jnp.where(row_odd, wide(even_row[...]), wide(odd_row[...]))
    below = jnp.where(row_odd, wide(odd_row[...]), wide(even_row[...]))
    left = jnp.where(col_odd, wide(even_col[...]), wide(odd_col[...]))
    right = jnp.where(col_odd, wide(odd_col[...]), wide(even_col[...]))

    g3 = g3_ref[...]
    gains = (
        g3[:, 0:128],
        jnp.concatenate([g3[:, 128:192], g3[:, 0:64]], axis=1),
        g3[:, 64:192],
    )

    def put_pair(frame, jj, tiles):
        for half, pair in enumerate(split_pair(*tiles)):
            base = ((frame + half) * WIDE + jj) * EXT
            act[0, base : base + EXT, :] = pair[0]
            act[1, base : base + EXT, :] = pair[1]

    for jj in range(WIDE):
        base = jj * EXT
        side, lane = (left, jj) if jj < 2 else (right, jj - WIDE + 2)
        for q in range(9):
            if 2 <= jj < WIDE - 2:
                j = jj - 2
                if q < 6:
                    src, at = x_ref, j * COLX + q * 128
                    strip_at = at
                else:
                    src, at = p_ref, j * COLP + (q - 6) * 128
                    strip_at = XW + at
                raw[q, base : base + 2, :] = above[:, strip_at : strip_at + 128]
                raw[q, base + 2 : base + 18, :] = wide(src[:, at : at + 128])
                raw[q, base + 18 : base + 20, :] = below[:, strip_at : strip_at + 128]
            else:
                at = lane * COLX + q * 128 if q < 6 else 2 * COLX + lane * COLP + (q - 6) * 128
                raw[q, base : base + 20, :] = side[:, at : at + 128]
        put_pair(0, jj, [raw[6 + q, base : base + EXT, :] for q in range(3)])
        for pair in range(2):
            tiles = [raw[3 * pair + q, base : base + EXT, :] for q in range(3)]
            put_pair(2 + 2 * pair, jj, norm_pair(*tiles, gains))

    for slab in range(6 * WIDE):
        for dy in range(3):
            at = slab * EXT + 1 + dy
            both = jnp.concatenate([act[0, at : at + ROWS, :], act[1, at : at + ROWS, :]], axis=1)
            act_d[dy, slab * ROWS : (slab + 1) * ROWS, :] = both.astype(BF16)
    for place, ext in enumerate((0, 1, 2, 17, 18, 19)):
        for frame in range(6):
            rows = pl.ds(frame * WIDE * EXT + ext, 16, stride=EXT)
            both = jnp.concatenate([act[0, rows, :], act[1, rows, :]], axis=1)
            halo_d[place, frame * 16 : (frame + 1) * 16, :] = both.astype(BF16)

    center = None
    edges = [None, None, None]
    for dy in range(3):
        for dx in range(3):
            for t in range(3):
                parts = []
                for k in range(FRAMES):
                    at = ((k + t) * WIDE + dx) * ROWS
                    parts.append(act_d[dy, at : at + MID * ROWS, 0:C3])
                for side in range(2):
                    parts.append(halo_d[3 * side + dy, t * 16 : (t + FRAMES) * 16, 0:C3])
                got = nt_dot(jnp.concatenate(parts, axis=0), w3_ref[9 * t + 3 * dy + dx])
                mid = FRAMES * MID * ROWS
                center = got[:mid] if center is None else center + got[:mid]
                edges[dx] = got[mid:] if edges[dx] is None else edges[dx] + got[mid:]

    b3 = b3_ref[...]

    def keep(inside, value):
        return jnp.where(inside, value, jnp.zeros_like(value))

    def rounded(value):
        return value.astype(BF16).astype(F32)

    def put_res(rows, value):
        res[0, rows, :] = value[:, 0:128]
        res[1, rows, 0:64] = value[:, 128:192]

    for jm in range(MID):
        for pair in range(2):
            at = (jm + 1) * EXT + 2
            tiles = [raw[3 * pair + q, at : at + ROWS, :] for q in range(3)]
            for half, skip in enumerate(split_pair(*tiles)):
                k = 2 * pair + half
                slab = k * MID + jm
                value = center[slab * ROWS : (slab + 1) * ROWS] + b3
                value = rounded(value + jnp.concatenate([skip[0], skip[1][:, 0:64]], axis=1))
                if jm == 0:
                    value = keep(jnp.logical_not(first_col), value)
                if jm == MID - 1:
                    value = keep(jnp.logical_not(last_col), value)
                put_res(pl.ds(slab * EXT + 1, ROWS), value)
    column = lax.broadcasted_iota(jnp.int32, (MID, 1), 0)
    cols_in = jnp.logical_and(
        jnp.logical_or(column > 0, jnp.logical_not(first_col)),
        jnp.logical_or(column < MID - 1, jnp.logical_not(last_col)),
    )
    for side in range(2):
        rows_in = jnp.logical_not(last_row if side else first_row)
        ext = 18 if side else 1
        for pair in range(2):
            tiles = [raw[3 * pair + q, pl.ds(EXT + ext, MID, stride=EXT), :] for q in range(3)]
            for half, skip in enumerate(split_pair(*tiles)):
                k = 2 * pair + half
                at = (side * FRAMES + k) * 16
                value = b3 + edges[0][at : at + MID] + edges[1][at + 1 : at + 1 + MID]
                value = value + edges[2][at + 2 : at + 2 + MID]
                value = rounded(value + jnp.concatenate([skip[0], skip[1][:, 0:64]], axis=1))
                value = keep(jnp.logical_and(cols_in, rows_in), value)
                put_res(pl.ds(k * MID * EXT + (17 if side else 0), MID, stride=EXT), value)

    for slab in range(FRAMES * MID):
        for di in range(3):
            at = slab * EXT + di
            both = jnp.concatenate([res[0, at : at + ROWS, :], res[1, at : at + ROWS, :]], axis=1)
            res_d[di, slab * ROWS : (slab + 1) * ROWS, :] = both.astype(BF16)
    for place, ext in enumerate((0, 1, 16, 17)):
        for k in range(FRAMES):
            rows = pl.ds(k * MID * EXT + ext, 16, stride=EXT)
            both = jnp.concatenate([res[0, rows, :], res[1, rows, :]], axis=1)
            res_h[place, k * 16 : (k + 1) * 16, :] = both.astype(BF16)

    taps = {}

    def tap(dy, dx):
        if (dy, dx) not in taps:
            taps[dy, dx] = wide(wu_ref[3 * dy + dx])
        return taps[dy, dx]

    spans = {(0, 0): (0,), (0, 1): (1, 2), (1, 1): (0, 1), (1, 2): (2,)}
    for a in range(2):
        for di in (a, a + 1):
            for b in range(2):
                for dj in (b, b + 1):
                    total = None
                    for dy in spans[a, di]:
                        for dx in spans[b, dj]:
                            one = tap(dy, dx)
                            total = one if total is None else total + one
                    both = jnp.concatenate([total, jnp.zeros((32, C3), F32)], axis=0)
                    slot = 2 * a + b
                    wup[3 * di + dj, slot * 128 : (slot + 1) * 128, 0:C3] = both.astype(BF16)

    b4in = jnp.concatenate([bu_ref[...], jnp.zeros((1, 32), F32)], axis=1)
    g4 = jnp.concatenate([g4_ref[...], jnp.zeros((1, 32), F32)], axis=1)

    def act_four(value):
        total = jnp.sum(value * value, axis=1, keepdims=True)
        return silu(value * lax.rsqrt(total * (1.0 / C4) + EPSILON) * g4)

    span = COLS + 1
    for a in range(2):
        for b in range(2):
            slot = 2 * a + b
            total = None
            rim = None
            for di in (a, a + 1):
                for dj in (b, b + 1):
                    kernel = wup[3 * di + dj, slot * 128 : (slot + 1) * 128, 0:C3]
                    parts = [
                        res_d[di, (k * MID + dj - b) * ROWS : (k * MID + dj - b + span) * ROWS, 0:C3]
                        for k in range(FRAMES)
                    ]
                    parts.append(res_h[(di - 1) if a else (2 + di), :, 0:C3])
                    got = nt_dot(jnp.concatenate(parts, axis=0), kernel)
                    mid = FRAMES * span * ROWS
                    total = got[:mid] if total is None else total + got[:mid]
                    starts = [mid + k * 16 + dj - b for k in range(FRAMES)]
                    part = [got[at : at + span] for at in starts]
                    rim = part if rim is None else [p + r for p, r in zip(part, rim)]
            for k in range(FRAMES):
                for j in range(span):
                    at = (k * span + j) * ROWS
                    fx = 2 * j if b else 2 * j + 1
                    value = rounded(total[at : at + ROWS] + b4in)
                    if 1 <= fx <= 2 * COLS:
                        s4[k, pl.ds((fx - 1) * FROWS + a, ROWS, stride=2), :] = value
                    value = act_four(value)
                    if fx == 0:
                        value = keep(jnp.logical_not(first_col), value)
                    if fx == FINE - 1:
                        value = keep(jnp.logical_not(last_col), value)
                    z4[2 + k, pl.ds(fx * FEXT + 1 + a, ROWS, stride=2), :] = value
                value = act_four(rounded(rim[k] + b4in))
                index = lax.broadcasted_iota(jnp.int32, (span, 1), 0)
                if b:
                    inside = jnp.logical_or(index > 0, jnp.logical_not(first_col))
                else:
                    inside = jnp.logical_or(index < span - 1, jnp.logical_not(last_col))
                rows_in = jnp.logical_not(first_row if a else last_row)
                value = keep(jnp.logical_and(inside, rows_in), value)
                start = (0 if b else FEXT) + (0 if a else FROWS + 1)
                z4[2 + k, pl.ds(start, span, stride=2 * FEXT), :] = value

    def put_cached(fx, row0, tiles, rows, pick):
        joined = jnp.concatenate(tiles, axis=1)
        for t in range(2):
            at = pick + t * C4
            value = joined[:, at : at + C4]
            value = jnp.concatenate([value, jnp.zeros((rows, 32), F32)], axis=1)
            z4[t, fx * FEXT + row0 : fx * FEXT + row0 + rows, :] = value

    for fx in range(1, FINE - 1):
        at = (fx - 1) * COLQ
        start = at // 128 * 128
        pick = at - start
        lanes = slice(start, start + 256)
        put_cached(fx, 1, [wide(q_ref[:, lanes])], FROWS, pick)
        strip = slice(XW + PW + start, XW + PW + start + 256)
        put_cached(fx, 0, [above[1:2, strip]], 1, pick)
        put_cached(fx, FROWS + 1, [below[0:1, strip]], 1, pick)
    qat = 2 * COLX + 2 * COLP
    for fx, side in ((0, left), (FINE - 1, right)):
        lanes = side[:, qat : qat + 384]
        put_cached(fx, 0, [lanes[1:2]], 1, 0)
        put_cached(fx, 1, [lanes[2:18]], ROWS, 0)
        put_cached(fx, 1 + ROWS, [lanes[2:18]], ROWS, COLQ)
        put_cached(fx, FROWS + 1, [lanes[18:19]], 1, 0)

    for fx in range(FINE):
        for dy in range(3):
            at = fx * FEXT + dy
            both = jnp.concatenate([z4[f, at : at + FROWS, :] for f in range(6)], axis=1)
            act4_d[dy, fx * FROWS : (fx + 1) * FROWS, :] = both.astype(BF16)

    pad = jnp.zeros((C4, 32), BF16)
    none = jnp.zeros((C4, 128), BF16)
    for place in range(9):
        kernels = [jnp.concatenate([w4_ref[9 * t + place], pad], axis=1) for t in range(3)]
        w4p[place, 0:C4, :] = jnp.concatenate(kernels + [none], axis=1)
        w4p[place, C4 : 2 * C4, :] = jnp.concatenate([none] + kernels, axis=1)
    total = None
    size = 2 * COLS * FROWS
    for dy in range(3):
        for dx in range(3):
            at = dx * FROWS
            parts = [act4_d[dy, at : at + size, 256 * p : 256 * p + 512] for p in range(2)]
            got = nt_dot(jnp.concatenate(parts, axis=0), w4p[3 * dy + dx])
            total = got if total is None else total + got

    b4 = b4_ref[...]
    bias = jnp.concatenate([b4, b4], axis=1)
    first = lane_mask(FROWS, C4)
    low = lane_mask(FROWS, 64)
    for fx in range(2 * COLS):
        tiles = []
        for pair in range(2):
            at = pair * size + fx * FROWS
            got = total[at : at + FROWS] + bias
            keep_a = s4[2 * pair, fx * FROWS : (fx + 1) * FROWS, :]
            keep_b = pltpu.roll(s4[2 * pair + 1, fx * FROWS : (fx + 1) * FROWS, :], C4, 1)
            skip = jnp.concatenate([jnp.where(first, keep_a, keep_b), keep_b[:, 0:64]], axis=1)
            tiles.append(got + skip)
        out_ref[:, fx * 384 : (fx + 1) * 384] = jnp.concatenate(tiles, axis=1).astype(BF16)


def swap_pairs(count, start):
    out = []
    for low in range(start, count - 1, 2):
        out += [(low, low + 1), (low + 1, low)]
    return out


def swaps(axis, count, index, low, high):
    odd = index % 2 == 1
    even_swap = lax.ppermute(jnp.where(odd, low, high), axis, swap_pairs(count, 0))
    odd_swap = lax.ppermute(jnp.where(odd, high, low), axis, swap_pairs(count, 1))
    return odd, even_swap, odd_swap


def shards(
    section_input,
    cache_three,
    gain_three,
    bias_three,
    weight_three,
    weight_up,
    bias_up,
    cache_four,
    gain_four,
    weight_four,
    bias_four,
):
    row_count = lax.axis_size("row")
    col_size = lax.axis_size("col")
    col_count = lax.axis_size("section") * col_size
    row = lax.axis_index("row")
    col = lax.axis_index("section") * col_size + lax.axis_index("col")

    def row_strip(part):
        return jnp.concatenate([section_input[part], cache_three[part], cache_four[part]], axis=1)

    row_odd, even_row, odd_row = swaps(
        "row", row_count, row, row_strip(slice(0, 2)), row_strip(slice(-2, None))
    )
    above = jnp.where(row_odd, even_row, odd_row)
    below = jnp.where(row_odd, odd_row, even_row)

    def col_strip(high):
        def edge(block, start, width, lanes):
            at = start + (width - lanes if high else 0)
            return block[:, at : at + lanes]

        center = [
            edge(section_input, 0, XW, 2 * COLX),
            edge(cache_three, 0, PW, 2 * COLP),
            edge(cache_four[:ROWS], 0, QW, COLQ),
            edge(cache_four[ROWS:], 0, QW, COLQ),
        ]
        parts = [jnp.concatenate(center, axis=1)]
        for strip in (above, below):
            corner = [
                edge(strip, 0, XW, 2 * COLX),
                edge(strip, XW, PW, 2 * COLP),
                edge(strip, XW + PW, QW, COLQ),
                jnp.zeros((2, COLQ), BF16),
            ]
            parts.append(jnp.concatenate(corner, axis=1))
        return jnp.concatenate([parts[1], parts[0], parts[2]], axis=0)

    _, even_col, odd_col = swaps(
        ("section", "col"), col_count, col, col_strip(False), col_strip(True)
    )

    w3 = weight_three.reshape(27, C3, C3)
    wu = weight_up.reshape(9, C4, C3)
    w4 = weight_four.reshape(27, C4, C4)

    def run(*operands):
        def kernel(*refs):
            main_kernel(*refs, row_count=row_count, col_count=col_count, col_size=col_size)

        return pl.pallas_call(
            kernel,
            out_shape=jax.ShapeDtypeStruct((FROWS, 2 * COLS * FRAMES * C4), BF16),
            in_specs=[pl.BlockSpec(memory_space=pltpu.VMEM)] * len(operands),
            out_specs=pl.BlockSpec(memory_space=pltpu.VMEM),
            scratch_shapes=[
                pltpu.VMEM((9, 16 * EXT, 128), F32),
                pltpu.VMEM((2, (6 * WIDE + 2) * EXT, 128), F32),
                pltpu.VMEM((3, 6 * WIDE * ROWS, 256), BF16),
                pltpu.VMEM((6, 6 * 16, 256), BF16),
                pltpu.VMEM((2, (FRAMES * MID + 4) * EXT, 128), F32),
                pltpu.VMEM((3, FRAMES * MID * ROWS, 256), BF16),
                pltpu.VMEM((4, FRAMES * 16, 256), BF16),
                pltpu.VMEM((9, 512, 256), BF16),
                pltpu.VMEM((6, FINE * FEXT, 128), F32),
                pltpu.VMEM((FRAMES, 2 * COLS * FROWS, 128), F32),
                pltpu.VMEM((3, FINE * FROWS, 768), BF16),
                pltpu.VMEM((9, 2 * C4, 512), BF16),
            ],
            compiler_params=pltpu.CompilerParams(vmem_limit_bytes=56 * 1024 * 1024),
        )(*operands)

    return run(
        section_input, cache_three, cache_four, even_row, odd_row, even_col, odd_col,
        gain_three.reshape(1, C3), bias_three.reshape(1, C3), w3, wu, bias_up.reshape(1, C4),
        gain_four.reshape(1, C4), w4, bias_four.reshape(1, C4),
    )


def solution(mesh):
    tiled = P("row", ("section", "col"))
    return jax.shard_map(
        shards,
        mesh=mesh,
        in_specs=(tiled, tiled, P(), P(), P(), P(), P(), tiled, P(), P(), P()),
        out_specs=tiled,
        check_vma=False,
    )
```

```python
import jax
import jax.numpy as jnp
from jax import lax
from jax.experimental import pallas as pl
from jax.experimental.pallas import tpu as pltpu
from jax.sharding import PartitionSpec as P

EPSILON = 1e-06
BF16 = jnp.bfloat16
F32 = jnp.float32

ROWS = 16
COLS = 10
C3 = 192
C4 = 96
FRAMES = 4
WIDE = COLS + 4
MID = COLS + 2
CHUNKS = 4
EXT = 24
FINE = 2 * COLS + 2
FROWS = 2 * ROWS
FEXT = 40
XW = COLS * FRAMES * C3
PW = COLS * 2 * C3
QW = 2 * COLS * 2 * C4
COLX = FRAMES * C3
COLP = 2 * C3
COLQ = 2 * C4
QAT = 2 * COLX + 2 * COLP


def nt_dot(lhs, rhs):
    return lax.dot_general(lhs, rhs, (((1,), (1,)), ((), ())), preferred_element_type=F32)


def silu(value):
    half = 0.5 * value
    return half + half * jnp.tanh(half)


def lane_mask(rows, below):
    return lax.broadcasted_iota(jnp.int32, (rows, 128), 1) < below


def split_pair(v0, v1, v2):
    low = lane_mask(v0.shape[0], 64)
    r1 = pltpu.roll(v1, 64, 1)
    r2 = pltpu.roll(v2, 64, 1)
    zero = jnp.zeros_like(v1)
    return (v0, jnp.where(low, v1, zero)), (jnp.where(low, r1, r2), jnp.where(low, r2, zero))


def norm_pair(v0, v1, v2, gains):
    low = lane_mask(v0.shape[0], 64)
    sq1 = v1 * v1
    zero = jnp.zeros_like(v1)
    sum_a = jnp.sum(v0 * v0 + jnp.where(low, sq1, zero), axis=1, keepdims=True)
    sum_b = jnp.sum(v2 * v2 + jnp.where(low, zero, sq1), axis=1, keepdims=True)
    inv_a = lax.rsqrt(sum_a * (1.0 / C3) + EPSILON)
    inv_b = lax.rsqrt(sum_b * (1.0 / C3) + EPSILON)
    return (
        silu(v0 * inv_a * gains[0]),
        silu(v1 * jnp.where(low, inv_a, inv_b) * gains[1]),
        silu(v2 * inv_b * gains[2]),
    )


def weave(*streams):
    lists = []
    for stream in streams:
        lists.append(list(stream))
    order = []
    for place, steps in enumerate(lists):
        order += [((n + 0.5) / len(steps), place, step) for n, step in enumerate(steps)]
    for _, _, step in sorted(order, key=lambda entry: entry[:2]):
        step()


def up_slots():
    slots = {}
    count = 0
    for di in range(3):
        for dj in range(3):
            phases = [(a, b) for a in range(2) for b in range(2) if 0 <= di - a < 2 and 0 <= dj - b < 2]
            slots[di, dj] = (count, phases)
            count += len(phases)
    return slots


def main_kernel(
    x_ref, p_ref, q_ref, even_row, odd_row, even_col, odd_col,
    g3_ref, b3_ref, w3_ref, wu_ref, bu_ref, g4_ref, w4_ref, b4_ref,
    out_ref,
    raw0, raw1, raw2, act0, act1, act2, actd0, actd1, actd2, halo0, halo1, halo2,
    res0, res1, resd0, resd1, resh0, resh1, z0, z1, z2, s0, s1, fine0, fine1, fine2,
    *, row_count, col_count, col_size,
):
    raw, act, act_d, halo_d = (raw0, raw1, raw2), (act0, act1, act2), (actd0, actd1, actd2), (halo0, halo1, halo2)
    res, res_d, res_h = (res0, res1), (resd0, resd1), (resh0, resh1)
    z4, s4, act4_d = (z0, z1, z2), (s0, s1), (fine0, fine1, fine2)
    row = lax.axis_index("row")
    col = lax.axis_index("section") * col_size + lax.axis_index("col")
    row_odd = lax.rem(row, 2) == 1
    col_odd = lax.rem(col, 2) == 1
    first_row, last_row = row == 0, row == row_count - 1
    first_col, last_col = col == 0, col == col_count - 1

    def wide(value):
        return value.astype(F32)

    def pick(flag, one, other, *index):
        return wide(jnp.where(flag, one[index], other[index]))

    def above(lanes):
        return pick(row_odd, even_row, odd_row, slice(0, 2), lanes)

    def below(lanes):
        return pick(row_odd, odd_row, even_row, slice(0, 2), lanes)

    def left(lanes):
        return pick(col_odd, even_col, odd_col, slice(0, ROWS + 4), lanes)

    def right(lanes):
        return pick(col_odd, odd_col, even_col, slice(0, ROWS + 4), lanes)

    def keep(inside, value):
        return jnp.where(inside, value, jnp.zeros_like(value))

    def rounded(value):
        return value.astype(BF16).astype(F32)

    def pair_of(ref, *index):
        return jnp.concatenate([ref[(0,) + index], ref[(1,) + index]], axis=1).astype(BF16)

    g3 = g3_ref[...]
    gains = (
        g3[:, 0:128],
        jnp.concatenate([g3[:, 128:192], g3[:, 0:64]], axis=1),
        g3[:, 64:192],
    )

    def load_column(group, jj):
        base = jj * EXT
        for q in range(3):
            if 2 <= jj < WIDE - 2:
                at = (jj - 2) * COLX + (3 * (group - 1) + q) * 128
                if group == 0:
                    at = (jj - 2) * COLP + q * 128
                src, strip_at = (x_ref, at) if group else (p_ref, XW + at)
                strip = slice(strip_at, strip_at + 128)
                raw[group][q, base : base + 16, :] = wide(src[:, at : at + 128])
                raw[group][q, base + 16 : base + 18, :] = above(strip)
                raw[group][q, base + 18 : base + 20, :] = below(strip)
            else:
                side, lane = (left, jj) if jj < 2 else (right, jj - WIDE + 2)
                at = lane * COLX + (3 * (group - 1) + q) * 128
                if group == 0:
                    at = 2 * COLX + lane * COLP + q * 128
                raw[group][q, base : base + 20, :] = side(slice(at, at + 128))
        tiles = [raw[group][q, base : base + EXT, :] for q in range(3)]
        if group:
            tiles = norm_pair(*tiles, gains)
        for half, pair in enumerate(split_pair(*tiles)):
            at = (half * WIDE + jj) * EXT
            for q in range(2):
                act[group][q, at : at + 2, :] = pair[q][16:18]
                act[group][q, at + 2 : at + 18, :] = pair[q][0:16]
                act[group][q, at + 18 : at + 20, :] = pair[q][18:20]

    def shift_column(group, jj):
        for half in range(2):
            slab = half * WIDE + jj
            for dy in range(3):
                rows = slice(slab * EXT + 1 + dy, slab * EXT + 1 + dy + ROWS)
                act_d[group][dy, slab * ROWS : (slab + 1) * ROWS, :] = pair_of(act[group], rows, slice(None))

    def gather_rows(group, place):
        ext = (0, 1, 2, 17, 18, 19)[place]
        for half in range(2):
            rows = pl.ds(half * WIDE * EXT + ext, 16, stride=EXT)
            halo_d[group][place, half * 16 : (half + 1) * 16, :] = pair_of(act[group], rows, slice(None))

    def coarse_steps(group):
        for jj in range(WIDE):
            yield lambda jj=jj: (load_column(group, jj), shift_column(group, jj))
        for place in range(6):
            yield lambda place=place: gather_rows(group, place)

    mid = 2 * MID * ROWS
    center = [None, None]
    edges = [[None] * 3, [None] * 3]

    def conv_three(p, dy, dx, t):
        parts = []
        halos = []
        for k in range(2):
            group, half = p + (k + t) // 2, (k + t) % 2
            at = (half * WIDE + dx) * ROWS
            parts.append(act_d[group][dy, at : at + MID * ROWS, 0:C3])
            for side in range(2):
                halos.append(halo_d[group][3 * side + dy, half * 16 : (half + 1) * 16, 0:C3])
        kernel = w3_ref[9 * t + 3 * dy + dx, :, 0:C3]
        got = nt_dot(jnp.concatenate(parts + halos, axis=0), kernel)
        center[p] = got[:mid] if center[p] is None else center[p] + got[:mid]
        edges[p][dx] = got[mid:] if edges[p][dx] is None else edges[p][dx] + got[mid:]

    def conv_three_steps(p):
        for dy in range(3):
            for dx in range(3):
                for t in range(3):
                    yield lambda dy=dy, dx=dx, t=t: conv_three(p, dy, dx, t)

    b3 = b3_ref[...]
    column = lax.broadcasted_iota(jnp.int32, (MID, 1), 0)
    cols_in = jnp.logical_and(
        jnp.logical_or(column > 0, jnp.logical_not(first_col)),
        jnp.logical_or(column < MID - 1, jnp.logical_not(last_col)),
    )

    def put_res(p, rows, value):
        res[p][0, rows, :] = value[:, 0:128]
        res[p][1, rows, 0:64] = value[:, 128:192]

    def result_column(p, jm):
        at = (jm + 1) * EXT
        tiles = [raw[p + 1][q, at : at + ROWS, :] for q in range(3)]
        for k, skip in enumerate(split_pair(*tiles)):
            slab = k * MID + jm
            value = center[p][slab * ROWS : (slab + 1) * ROWS] + b3
            value = rounded(value + jnp.concatenate([skip[0], skip[1][:, 0:64]], axis=1))
            if jm == 0:
                value = keep(jnp.logical_not(first_col), value)
            if jm == MID - 1:
                value = keep(jnp.logical_not(last_col), value)
            put_res(p, pl.ds(slab * EXT + 1, ROWS), value)

    def result_rows(p, side):
        rows_in = jnp.logical_not(last_row if side else first_row)
        ext = 18 if side else 17
        tiles = [raw[p + 1][q, pl.ds(EXT + ext, MID, stride=EXT), :] for q in range(3)]
        for k, skip in enumerate(split_pair(*tiles)):
            at = (2 * k + side) * 16
            value = b3 + edges[p][0][at : at + MID] + edges[p][1][at + 1 : at + 1 + MID]
            value = value + edges[p][2][at + 2 : at + 2 + MID]
            value = rounded(value + jnp.concatenate([skip[0], skip[1][:, 0:64]], axis=1))
            value = keep(jnp.logical_and(cols_in, rows_in), value)
            put_res(p, pl.ds(k * MID * EXT + (17 if side else 0), MID, stride=EXT), value)

    def shift_result(p, jm):
        for k in range(2):
            slab = k * MID + jm
            for di in range(3):
                rows = slice(slab * EXT + di, slab * EXT + di + ROWS)
                res_d[p][di, slab * ROWS : (slab + 1) * ROWS, :] = pair_of(res[p], rows, slice(None))

    def gather_result(p, place):
        ext = (0, 1, 16, 17)[place]
        for k in range(2):
            rows = pl.ds(k * MID * EXT + ext, 16, stride=EXT)
            res_h[p][place, k * 16 : (k + 1) * 16, :] = pair_of(res[p], rows, slice(None))

    def result_steps(p):
        for side in range(2):
            yield lambda side=side: result_rows(p, side)
        for jm in range(MID):
            yield lambda jm=jm: (result_column(p, jm), shift_result(p, jm))
        for place in range(4):
            yield lambda place=place: gather_result(p, place)

    span = COLS + 1
    slots = up_slots()
    total = [{}, {}]
    rim = [{}, {}]

    def conv_up(p, di, dj):
        start, phases = slots[di, dj]
        low = min(dj - b for _, b in phases)
        wide_cols = span + max(dj - b for _, b in phases) - low
        sides = sorted({a for a, _ in phases})
        parts = []
        for k in range(2):
            at = (k * MID + low) * ROWS
            parts.append(res_d[p][di, at : at + wide_cols * ROWS, 0:C3])
        for a in sides:
            parts.append(res_h[p][(di - 1) if a else (2 + di), :, 0:C3])
        kernel = wu_ref[start * 128 : (start + len(phases)) * 128, 0:C3]
        got = nt_dot(jnp.concatenate(parts, axis=0), kernel)
        for n, (a, b) in enumerate(phases):
            lanes = slice(n * 128, (n + 1) * 128)
            for k in range(2):
                at = (k * wide_cols + dj - b - low) * ROWS
                value = got[at : at + span * ROWS, lanes]
                at = 2 * wide_cols * ROWS + sides.index(a) * 32 + k * 16 + dj - b
                edge = got[at : at + span, lanes]
                if (a, b, k) in total[p]:
                    value = value + total[p][a, b, k]
                    edge = edge + rim[p][a, b, k]
                total[p][a, b, k] = value
                rim[p][a, b, k] = edge

    def conv_up_steps(p):
        for di in range(3):
            for dj in range(3):
                yield lambda di=di, dj=dj: conv_up(p, di, dj)

    bias_up = jnp.concatenate([bu_ref[...], jnp.zeros((1, 32), F32)], axis=1)
    g4 = jnp.concatenate([g4_ref[...], jnp.zeros((1, 32), F32)], axis=1)

    def act_four(value):
        square = jnp.sum(value * value, axis=1, keepdims=True)
        return silu(value * lax.rsqrt(square * (1.0 / C4) + EPSILON) * g4)

    def fine_rows(p, a, b, k):
        value = act_four(rounded(rim[p][a, b, k] + bias_up))
        index = lax.broadcasted_iota(jnp.int32, (span, 1), 0)
        if b:
            inside = jnp.logical_or(index > 0, jnp.logical_not(first_col))
        else:
            inside = jnp.logical_or(index < span - 1, jnp.logical_not(last_col))
        value = keep(jnp.logical_and(inside, jnp.logical_not(first_row if a else last_row)), value)
        start = (0 if b else FEXT) + (0 if a else FROWS + 1)
        z4[p + 1][k, pl.ds(start, span, stride=2 * FEXT), :] = value

    def fine_column(p, b, j):
        fx = 2 * j if b else 2 * j + 1
        for k in range(2):
            for a in range(2):
                value = rounded(total[p][a, b, k][j * ROWS : (j + 1) * ROWS] + bias_up)
                if 1 <= fx <= 2 * COLS:
                    s4[p][k, pl.ds((fx - 1) * FROWS + a, ROWS, stride=2), :] = value
                value = act_four(value)
                if fx == 0:
                    value = keep(jnp.logical_not(first_col), value)
                if fx == FINE - 1:
                    value = keep(jnp.logical_not(last_col), value)
                z4[p + 1][k, pl.ds(fx * FEXT + 1 + a, ROWS, stride=2), :] = value
        shift_fine(p + 1, fx)

    def shift_fine(group, fx):
        for dy in range(3):
            rows = slice(fx * FEXT + dy, fx * FEXT + dy + FROWS)
            act4_d[group][dy, fx * FROWS : (fx + 1) * FROWS, :] = pair_of(z4[group], rows, slice(None))

    def fine_steps(p):
        for a in range(2):
            for b in range(2):
                for k in range(2):
                    yield lambda a=a, b=b, k=k: fine_rows(p, a, b, k)
        for j in range(span):
            for b in (1, 0):
                yield lambda b=b, j=j: fine_column(p, b, j)

    def put_cached(fx, row0, joined, first):
        rows = joined.shape[0]
        for t in range(2):
            at = first + t * C4
            value = jnp.concatenate([joined[:, at : at + C4], jnp.zeros((rows, 32), F32)], axis=1)
            z4[0][t, fx * FEXT + row0 : fx * FEXT + row0 + rows, :] = value

    def cached_column(fx):
        if 0 < fx < FINE - 1:
            at = (fx - 1) * COLQ
            start = at // 128 * 128
            first = at - start
            strip = slice(XW + PW + start, XW + PW + start + 256)
            put_cached(fx, 1, wide(q_ref[:, start : start + 256]), first)
            put_cached(fx, 0, above(strip)[1:2], first)
            put_cached(fx, FROWS + 1, below(strip)[0:1], first)
        else:
            lanes = (right if fx else left)(slice(QAT, QAT + 384))
            put_cached(fx, 0, lanes[17:18], 0)
            put_cached(fx, 1, lanes[0:16], 0)
            put_cached(fx, 1 + ROWS, lanes[0:16], COLQ)
            put_cached(fx, FROWS + 1, lanes[18:19], 0)
        shift_fine(0, fx)

    def cached_steps():
        for fx in range(FINE):
            yield lambda fx=fx: cached_column(fx)

    size = 2 * COLS * FROWS
    done = [None, None]

    def conv_four(p, dy, dx):
        at = dx * FROWS
        parts = [act4_d[group][dy, at : at + size, :] for group in (p, p + 1)]
        got = nt_dot(jnp.concatenate(parts, axis=1), w4_ref[3 * dy + dx])
        done[p] = got if done[p] is None else done[p] + got

    def conv_four_steps(p):
        for dy in range(3):
            for dx in range(3):
                yield lambda dy=dy, dx=dx: conv_four(p, dy, dx)

    b4 = b4_ref[...]
    bias_four = jnp.concatenate([b4, b4], axis=1)
    first = lane_mask(FROWS, C4)

    def out_column(p, fx):
        rows = slice(fx * FROWS, (fx + 1) * FROWS)
        other = pltpu.roll(s4[p][1, rows, :], C4, 1)
        skip = jnp.concatenate([jnp.where(first, s4[p][0, rows, :], other), other[:, 0:64]], axis=1)
        value = (done[p][rows] + bias_four + skip).astype(BF16)
        out_ref[:, fx * 384 + p * 192 : fx * 384 + (p + 1) * 192] = value

    def out_steps(p):
        for fx in range(2 * COLS):
            yield lambda fx=fx: out_column(p, fx)

    weave(coarse_steps(0), coarse_steps(1))
    weave(conv_three_steps(0), coarse_steps(2), cached_steps())
    later = list(conv_three_steps(1))
    weave(later[:13], result_steps(0))
    weave(conv_up_steps(0))
    weave(later[13:], fine_steps(0))
    later = list(conv_four_steps(0))
    weave(later[:4], result_steps(1))
    weave(conv_up_steps(1))
    weave(later[4:], fine_steps(1))
    weave(conv_four_steps(1), out_steps(0))
    weave(out_steps(1))


def prep_three_kernel(source_ref, out_ref, flat_ref, parts, mixed, sems):
    low = lane_mask(C3 // 2, 64)
    zero = jnp.zeros((C3 // 2, 128), F32)
    size = source_ref.shape[1] // CHUNKS
    copies = []
    for chunk in range(CHUNKS):
        lanes = pl.ds(chunk * size, size)
        copies.append(
            pltpu.make_async_copy(source_ref.at[:, lanes], flat_ref.at[:, lanes], sems.at[chunk])
        )
        copies[-1].start()
    for pair in range(C3 // 2):
        if pair % (C3 // 2 // CHUNKS) == 0:
            copies[pair // (C3 // 2 // CHUNKS)].wait()
        for q in range(3):
            at = (3 * pair + q) * 128
            parts[q, pair * 32 : pair * 32 + 27, :] = flat_ref[:, at : at + 128].astype(F32)
    for tap in range(27):
        v0, v1, v2 = [parts[q, pl.ds(tap, C3 // 2, stride=32), :] for q in range(3)]
        r1, r2 = pltpu.roll(v1, 64, 1), pltpu.roll(v2, 64, 1)
        slot = tap % 2
        mixed[slot, 0, pl.ds(0, C3 // 2, stride=2), :] = v0
        mixed[slot, 1, pl.ds(0, C3 // 2, stride=2), :] = jnp.where(low, v1, zero)
        mixed[slot, 0, pl.ds(1, C3 // 2, stride=2), :] = jnp.where(low, r1, r2)
        mixed[slot, 1, pl.ds(1, C3 // 2, stride=2), :] = jnp.where(low, r2, zero)
        both = jnp.concatenate([mixed[slot, 0], mixed[slot, 1]], axis=1)
        out_ref[tap] = both.astype(BF16)


def prep_four_kernel(up_ref, four_ref, up_out, four_out, parts_u, mixed_u, parts_f, mixed_f):
    half = C4 // 2
    low = lane_mask(half, 64)
    zero = jnp.zeros((half, 128), F32)
    for pair in range(half):
        for q in range(3):
            at = (3 * pair + q) * 128
            parts_u[q, pair * 16 : pair * 16 + 9, :] = up_ref[:, at : at + 128].astype(F32)
    for tap in range(9):
        v0, v1, v2 = [parts_u[q, pl.ds(tap, half, stride=16), :] for q in range(3)]
        r1, r2 = pltpu.roll(v1, 64, 1), pltpu.roll(v2, 64, 1)
        mixed_u[tap, 0, pl.ds(0, half, stride=2), :] = v0
        mixed_u[tap, 1, pl.ds(0, half, stride=2), :] = jnp.where(low, v1, zero)
        mixed_u[tap, 0, pl.ds(1, half, stride=2), :] = jnp.where(low, r1, r2)
        mixed_u[tap, 1, pl.ds(1, half, stride=2), :] = jnp.where(low, r2, zero)
    spans = {(0, 0): (0,), (0, 1): (1, 2), (1, 0): (0, 1), (1, 1): (2,)}
    rest = jnp.zeros((32, 256), BF16)
    for (di, dj), (start, phases) in up_slots().items():
        for n, (a, b) in enumerate(phases):
            tiles = []
            for q in range(2):
                total = None
                for dy in spans[a, di - a]:
                    for dx in spans[b, dj - b]:
                        one = mixed_u[3 * dy + dx, q]
                        total = one if total is None else total + one
                tiles.append(total)
            at = (start + n) * 128
            up_out[at : at + C4, :] = jnp.concatenate(tiles, axis=1).astype(BF16)
            up_out[at + C4 : at + 128, :] = rest
    quarter = C4 // 4
    lane = lax.broadcasted_iota(jnp.int32, (quarter, 128), 1)
    empty = jnp.zeros((quarter, 128), F32)
    for four in range(quarter):
        for q in range(3):
            at = (3 * four + q) * 128
            parts_f[q, four * 32 : four * 32 + 27, :] = four_ref[:, at : at + 128].astype(F32)
    none = jnp.zeros((C4, 128), BF16)
    for place in range(9):
        four_out[place, 0:C4, 384:512] = none
        four_out[place, C4 : 2 * C4, 0:128] = none
        for t in range(3):
            rows = pl.ds(9 * t + place, quarter, stride=32)
            v0, v1, v2 = [parts_f[q, rows, :] for q in range(3)]
            second = jnp.where(lane < 32, pltpu.roll(v0, 32, 1), pltpu.roll(v1, 32, 1))
            third = jnp.where(lane < 64, pltpu.roll(v1, 64, 1), pltpu.roll(v2, 64, 1))
            slot = t % 2
            for m, value in enumerate((v0, second, third, pltpu.roll(v2, 96, 1))):
                rows = pl.ds(m, quarter, stride=4)
                mixed_f[slot, rows, :] = jnp.where(lane < C4, value, empty)
            kernel = mixed_f[slot].astype(BF16)
            four_out[place, 0:C4, t * 128 : (t + 1) * 128] = kernel
            four_out[place, C4 : 2 * C4, (t + 1) * 128 : (t + 2) * 128] = kernel


def row_strips(refs, low_flag, out_ref):
    at = 0
    for ref in refs:
        rows, width = ref.shape
        out_ref[:, at : at + width] = jnp.where(low_flag, ref[0:2, :], ref[rows - 2 : rows, :])
        at += width


def row_strips_kernel(x_ref, p_ref, q_ref, even_ref, odd_ref, x_own, p_own, q_own, sems):
    own = (x_own, p_own, q_own)
    copies = [
        pltpu.make_async_copy(source, target, sems.at[n])
        for n, (source, target) in enumerate(zip((x_ref, p_ref, q_ref), own))
    ]
    for copy in copies:
        copy.start()
    for copy in copies:
        copy.wait()
    row_odd = lax.rem(lax.axis_index("row"), 2) == 1
    row_strips(own, row_odd, even_ref)
    row_strips(own, jnp.logical_not(row_odd), odd_ref)


def col_strips_kernel(x_ref, p_ref, q_ref, even_row, odd_row, _, out_ref, *, col_size, parity):
    row_odd = lax.rem(lax.axis_index("row"), 2) == 1
    col = lax.axis_index("section") * col_size + lax.axis_index("col")
    take_low = lax.rem(col, 2) == parity
    strips = (
        jnp.where(row_odd, even_row[...], odd_row[...]),
        jnp.where(row_odd, odd_row[...], even_row[...]),
    )

    def put(rows, at, low, high):
        out_ref[rows, at : at + low.shape[1]] = jnp.where(take_low, low, high)

    start = 0
    for ref, at, width, lanes in (
        (x_ref, 0, XW, 2 * COLX), (p_ref, 2 * COLX, PW, 2 * COLP), (q_ref, QAT, QW, COLQ)
    ):
        high = width - lanes
        if ref is q_ref:
            for half in range(2):
                rows = slice(half * ROWS, (half + 1) * ROWS)
                put(slice(0, ROWS), at + half * lanes, ref[rows, 0:lanes], ref[rows, high:width])
        else:
            put(slice(0, ROWS), at, ref[:, 0:lanes], ref[:, high:width])
        for place, strip in enumerate(strips):
            rows = slice(ROWS + 2 * place, ROWS + 2 * place + 2)
            put(rows, at, strip[:, start : start + lanes], strip[:, start + high : start + width])
            if ref is q_ref:
                out_ref[rows, at + lanes : at + 2 * lanes] = jnp.zeros((2, lanes), BF16)
        start += width


def call(kernel, operands, outputs, scratch, megabytes, moved=0, unread=0, space=pl.ANY):
    cost = pl.CostEstimate(flops=moved, bytes_accessed=moved, transcendentals=0) if moved else None
    vmem = pl.BlockSpec(memory_space=pltpu.VMEM)
    shapes = [jax.ShapeDtypeStruct(shape, BF16) for shape in outputs]
    got = pl.pallas_call(
        kernel,
        out_shape=shapes,
        in_specs=[vmem] * (len(operands) - unread) + [pl.BlockSpec(memory_space=space)] * unread,
        out_specs=[vmem] * len(outputs),
        scratch_shapes=scratch,
        cost_estimate=cost,
        compiler_params=pltpu.CompilerParams(vmem_limit_bytes=megabytes * 1024 * 1024),
    )(*operands)
    return got[0] if len(outputs) == 1 else got


def swap_pairs(count, start):
    out = []
    for low in range(start, count - 1, 2):
        out += [(low, low + 1), (low + 1, low)]
    return out


def shards(
    section_input,
    cache_three,
    gain_three,
    bias_three,
    weight_three,
    weight_up,
    bias_up,
    cache_four,
    gain_four,
    weight_four,
    bias_four,
):
    row_count = lax.axis_size("row")
    col_size = lax.axis_size("col")
    col_count = lax.axis_size("section") * col_size
    tile = (section_input, cache_three, cache_four)

    row_strip = (2, XW + PW + QW)
    own = [pltpu.VMEM(block.shape, BF16) for block in tile]
    even_strip, odd_strip = call(
        row_strips_kernel,
        tile,
        [row_strip] * 2,
        [*own, pltpu.SemaphoreType.DMA((3,))],
        62, unread=3, space=pltpu.HBM,
    )
    even_row = lax.ppermute(even_strip, "row", swap_pairs(row_count, 0))
    odd_row = lax.ppermute(odd_strip, "row", swap_pairs(row_count, 1))

    w3 = call(
        prep_three_kernel,
        (weight_three,),
        [(27, C3, 256)],
        [
            pltpu.VMEM(weight_three.shape, BF16),
            pltpu.VMEM((3, 32 * C3 // 2, 128), F32),
            pltpu.VMEM((2, 2, C3, 128), F32),
            pltpu.SemaphoreType.DMA((CHUNKS,)),
        ],
        16, 8_000_000, unread=1, space=pltpu.HBM,
    )
    wu, w4 = call(
        prep_four_kernel,
        (weight_up, weight_four),
        [(16 * 128, 256), (9, 2 * C4, 512)],
        [
            pltpu.VMEM((3, 16 * C4 // 2, 128), F32),
            pltpu.VMEM((9, 2, C4, 128), F32),
            pltpu.VMEM((3, 32 * C4 // 4, 128), F32),
            pltpu.VMEM((2, C4, 128), F32),
        ],
        16, 8_000_000,
    )

    col_strip = (ROWS + 4, QAT + 2 * COLQ)

    def swap_columns(parity):
        def col_kernel(*refs):
            col_strips_kernel(*refs, col_size=col_size, parity=1 - parity)

        strip = call(col_kernel, (*tile, even_row, odd_row, w3), [col_strip], [], 4, unread=1)
        return lax.ppermute(strip, ("section", "col"), swap_pairs(col_count, parity))

    even_col = swap_columns(0)
    odd_col = swap_columns(1)

    def kernel(*refs):
        main_kernel(*refs, row_count=row_count, col_count=col_count, col_size=col_size)

    operands = (
        *tile, even_row, odd_row, even_col, odd_col,
        gain_three.reshape(1, C3), bias_three.reshape(1, C3), w3, wu, bias_up.reshape(1, C4),
        gain_four.reshape(1, C4), w4, bias_four.reshape(1, C4),
    )
    scratch = [pltpu.VMEM((3, 16 * EXT, 128), F32)] * 3
    scratch += [pltpu.VMEM((2, (2 * WIDE + 2) * EXT, 128), F32)] * 3
    scratch += [pltpu.VMEM((3, 2 * WIDE * ROWS, 256), BF16)] * 3
    scratch += [pltpu.VMEM((6, 2 * 16, 256), BF16)] * 3
    scratch += [pltpu.VMEM((2, (2 * MID + 4) * EXT, 128), F32)] * 2
    scratch += [pltpu.VMEM((3, 2 * MID * ROWS, 256), BF16)] * 2
    scratch += [pltpu.VMEM((4, 2 * 16, 256), BF16)] * 2
    scratch += [pltpu.VMEM((2, FINE * FEXT, 128), F32)] * 3
    scratch += [pltpu.VMEM((2, 2 * COLS * FROWS, 128), F32)] * 2
    scratch += [pltpu.VMEM((3, FINE * FROWS, 256), BF16)] * 3
    return call(kernel, operands, [(FROWS, 2 * COLS * FRAMES * C4)], scratch, 32)


def solution(mesh):
    tiled = P("row", ("section", "col"))
    return jax.shard_map(
        shards,
        mesh=mesh,
        in_specs=(tiled, tiled, P(), P(), P(), P(), P(), tiled, P(), P(), P()),
        out_specs=tiled,
        check_vma=False,
    )
```

```python
import jax
import jax.numpy as jnp
from jax import lax
from jax.experimental import pallas as pl
from jax.experimental.pallas import tpu as pltpu
from jax.sharding import PartitionSpec as P

EPSILON = 1e-06
BF16 = jnp.bfloat16
F32 = jnp.float32

ROWS = 16
COLS = 10
C3 = 192
C4 = 96
FRAMES = 4
WIDE = COLS + 4
MID = COLS + 2
EXT = 24
FINE = 2 * COLS + 2
FROWS = 2 * ROWS
FEXT = 40
XW = COLS * FRAMES * C3
PW = COLS * 2 * C3
QW = 2 * COLS * 2 * C4
COLX = FRAMES * C3
COLP = 2 * C3
COLQ = 2 * C4
QAT = 2 * COLX + 2 * COLP


def nt_dot(lhs, rhs):
    return lax.dot_general(lhs, rhs, (((1,), (1,)), ((), ())), preferred_element_type=F32)


def silu(value):
    half = 0.5 * value
    return half + half * jnp.tanh(half)


def lane_mask(rows, below):
    return lax.broadcasted_iota(jnp.int32, (rows, 128), 1) < below


def split_pair(v0, v1, v2):
    low = lane_mask(v0.shape[0], 64)
    r1 = pltpu.roll(v1, 64, 1)
    r2 = pltpu.roll(v2, 64, 1)
    zero = jnp.zeros_like(v1)
    return (v0, jnp.where(low, v1, zero)), (jnp.where(low, r1, r2), jnp.where(low, r2, zero))


def norm_pair(v0, v1, v2, gains):
    low = lane_mask(v0.shape[0], 64)
    sq1 = v1 * v1
    zero = jnp.zeros_like(v1)
    sum_a = jnp.sum(v0 * v0 + jnp.where(low, sq1, zero), axis=1, keepdims=True)
    sum_b = jnp.sum(v2 * v2 + jnp.where(low, zero, sq1), axis=1, keepdims=True)
    inv_a = lax.rsqrt(sum_a * (1.0 / C3) + EPSILON)
    inv_b = lax.rsqrt(sum_b * (1.0 / C3) + EPSILON)
    return (
        silu(v0 * inv_a * gains[0]),
        silu(v1 * jnp.where(low, inv_a, inv_b) * gains[1]),
        silu(v2 * inv_b * gains[2]),
    )


def weave(*streams):
    lists = []
    for stream in streams:
        lists.append(list(stream))
    order = []
    for place, steps in enumerate(lists):
        order += [((n + 0.5) / len(steps), place, step) for n, step in enumerate(steps)]
    for _, _, step in sorted(order, key=lambda entry: entry[:2]):
        step()


def up_slots():
    slots = {}
    count = 0
    for di in range(3):
        for dj in range(3):
            phases = [(a, b) for a in range(2) for b in range(2) if 0 <= di - a < 2 and 0 <= dj - b < 2]
            slots[di, dj] = (count, phases)
            count += len(phases)
    return slots


def main_kernel(
    x_ref, p_ref, q_ref, odd_row, even_row, even_col, odd_col,
    g3_ref, b3_ref, w3_ref, wu_ref, bu_ref, g4_ref, w4_ref, b4_ref,
    out_ref,
    raw0, raw1, raw2, act0, act1, act2, actd0, actd1, actd2, halo0, halo1, halo2,
    res0, res1, resd0, resd1, resh0, resh1, z0, z1, z2, s0, s1, fine0, fine1, fine2,
    *, row_count, col_count, col_size,
):
    raw, act, act_d, halo_d = (raw0, raw1, raw2), (act0, act1, act2), (actd0, actd1, actd2), (halo0, halo1, halo2)
    res, res_d, res_h = (res0, res1), (resd0, resd1), (resh0, resh1)
    z4, s4, act4_d = (z0, z1, z2), (s0, s1), (fine0, fine1, fine2)
    row = lax.axis_index("row")
    col = lax.axis_index("section") * col_size + lax.axis_index("col")
    row_odd = lax.rem(row, 2) == 1
    col_odd = lax.rem(col, 2) == 1
    first_row, last_row = row == 0, row == row_count - 1
    first_col, last_col = col == 0, col == col_count - 1

    def wide(value):
        return value.astype(F32)

    def pick(flag, one, other, *index):
        return wide(jnp.where(flag, one[index], other[index]))

    def above(lanes):
        return pick(row_odd, even_row, odd_row, slice(0, 2), lanes)

    def below(lanes):
        return pick(row_odd, odd_row, even_row, slice(0, 2), lanes)

    def left(lanes):
        return pick(col_odd, even_col, odd_col, slice(0, ROWS + 4), lanes)

    def right(lanes):
        return pick(col_odd, odd_col, even_col, slice(0, ROWS + 4), lanes)

    def keep(inside, value):
        return jnp.where(inside, value, jnp.zeros_like(value))

    def rounded(value):
        return value.astype(BF16).astype(F32)

    def pair_of(ref, *index):
        return jnp.concatenate([ref[(0,) + index], ref[(1,) + index]], axis=1).astype(BF16)

    g3 = g3_ref[...]
    gains = (
        g3[:, 0:128],
        jnp.concatenate([g3[:, 128:192], g3[:, 0:64]], axis=1),
        g3[:, 64:192],
    )

    def load_column(group, jj):
        base = jj * EXT
        for q in range(3):
            if 2 <= jj < WIDE - 2:
                at = (jj - 2) * COLX + (3 * (group - 1) + q) * 128
                if group == 0:
                    at = (jj - 2) * COLP + q * 128
                src, strip_at = (x_ref, at) if group else (p_ref, XW + at)
                strip = slice(strip_at, strip_at + 128)
                raw[group][q, base : base + 16, :] = wide(src[:, at : at + 128])
                raw[group][q, base + 16 : base + 18, :] = above(strip)
                raw[group][q, base + 18 : base + 20, :] = below(strip)
            else:
                side, lane = (left, jj) if jj < 2 else (right, jj - WIDE + 2)
                at = lane * COLX + (3 * (group - 1) + q) * 128
                if group == 0:
                    at = 2 * COLX + lane * COLP + q * 128
                raw[group][q, base : base + 20, :] = side(slice(at, at + 128))
        tiles = [raw[group][q, base : base + EXT, :] for q in range(3)]
        if group:
            tiles = norm_pair(*tiles, gains)
        for half, pair in enumerate(split_pair(*tiles)):
            at = (half * WIDE + jj) * EXT
            for q in range(2):
                act[group][q, at : at + 2, :] = pair[q][16:18]
                act[group][q, at + 2 : at + 18, :] = pair[q][0:16]
                act[group][q, at + 18 : at + 20, :] = pair[q][18:20]

    def shift_column(group, jj):
        for half in range(2):
            slab = half * WIDE + jj
            for dy in range(3):
                rows = slice(slab * EXT + 1 + dy, slab * EXT + 1 + dy + ROWS)
                act_d[group][dy, slab * ROWS : (slab + 1) * ROWS, :] = pair_of(act[group], rows, slice(None))

    def gather_rows(group, place):
        ext = (0, 1, 2, 17, 18, 19)[place]
        for half in range(2):
            rows = pl.ds(half * WIDE * EXT + ext, 16, stride=EXT)
            halo_d[group][place, half * 16 : (half + 1) * 16, :] = pair_of(act[group], rows, slice(None))

    def coarse_steps(group):
        for jj in range(WIDE):
            yield lambda jj=jj: (load_column(group, jj), shift_column(group, jj))
        for place in range(6):
            yield lambda place=place: gather_rows(group, place)

    mid = 2 * MID * ROWS
    center = [None, None]
    edges = [[None] * 3, [None] * 3]

    def conv_three(p, dy, dx, t):
        parts = []
        halos = []
        for k in range(2):
            group, half = p + (k + t) // 2, (k + t) % 2
            at = (half * WIDE + dx) * ROWS
            parts.append(act_d[group][dy, at : at + MID * ROWS, 0:C3])
            for side in range(2):
                halos.append(halo_d[group][3 * side + dy, half * 16 : (half + 1) * 16, 0:C3])
        kernel = w3_ref[9 * t + 3 * dy + dx, :, 0:C3]
        got = nt_dot(jnp.concatenate(parts + halos, axis=0), kernel)
        center[p] = got[:mid] if center[p] is None else center[p] + got[:mid]
        edges[p][dx] = got[mid:] if edges[p][dx] is None else edges[p][dx] + got[mid:]

    def conv_three_steps(p):
        for dy in range(3):
            for dx in range(3):
                for t in range(3):
                    yield lambda dy=dy, dx=dx, t=t: conv_three(p, dy, dx, t)

    b3 = b3_ref[...]
    column = lax.broadcasted_iota(jnp.int32, (MID, 1), 0)
    cols_in = jnp.logical_and(
        jnp.logical_or(column > 0, jnp.logical_not(first_col)),
        jnp.logical_or(column < MID - 1, jnp.logical_not(last_col)),
    )

    def put_res(p, rows, value):
        res[p][0, rows, :] = value[:, 0:128]
        res[p][1, rows, 0:64] = value[:, 128:192]

    def result_column(p, jm):
        at = (jm + 1) * EXT
        tiles = [raw[p + 1][q, at : at + ROWS, :] for q in range(3)]
        for k, skip in enumerate(split_pair(*tiles)):
            slab = k * MID + jm
            value = center[p][slab * ROWS : (slab + 1) * ROWS] + b3
            value = rounded(value + jnp.concatenate([skip[0], skip[1][:, 0:64]], axis=1))
            if jm == 0:
                value = keep(jnp.logical_not(first_col), value)
            if jm == MID - 1:
                value = keep(jnp.logical_not(last_col), value)
            put_res(p, pl.ds(slab * EXT + 1, ROWS), value)

    def result_rows(p, side):
        rows_in = jnp.logical_not(last_row if side else first_row)
        ext = 18 if side else 17
        tiles = [raw[p + 1][q, pl.ds(EXT + ext, MID, stride=EXT), :] for q in range(3)]
        for k, skip in enumerate(split_pair(*tiles)):
            at = (2 * k + side) * 16
            value = b3 + edges[p][0][at : at + MID] + edges[p][1][at + 1 : at + 1 + MID]
            value = value + edges[p][2][at + 2 : at + 2 + MID]
            value = rounded(value + jnp.concatenate([skip[0], skip[1][:, 0:64]], axis=1))
            value = keep(jnp.logical_and(cols_in, rows_in), value)
            put_res(p, pl.ds(k * MID * EXT + (17 if side else 0), MID, stride=EXT), value)

    def shift_result(p, jm):
        for k in range(2):
            slab = k * MID + jm
            for di in range(3):
                rows = slice(slab * EXT + di, slab * EXT + di + ROWS)
                res_d[p][di, slab * ROWS : (slab + 1) * ROWS, :] = pair_of(res[p], rows, slice(None))

    def gather_result(p, place):
        ext = (0, 1, 16, 17)[place]
        for k in range(2):
            rows = pl.ds(k * MID * EXT + ext, 16, stride=EXT)
            res_h[p][place, k * 16 : (k + 1) * 16, :] = pair_of(res[p], rows, slice(None))

    def result_steps(p):
        for side in range(2):
            yield lambda side=side: result_rows(p, side)
        for jm in range(MID):
            yield lambda jm=jm: (result_column(p, jm), shift_result(p, jm))
        for place in range(4):
            yield lambda place=place: gather_result(p, place)

    span = COLS + 1
    slots = up_slots()
    total = [{}, {}]
    rim = [{}, {}]

    def conv_up(p, di, dj):
        start, phases = slots[di, dj]
        low = min(dj - b for _, b in phases)
        wide_cols = span + max(dj - b for _, b in phases) - low
        sides = sorted({a for a, _ in phases})
        parts = []
        for k in range(2):
            at = (k * MID + low) * ROWS
            parts.append(res_d[p][di, at : at + wide_cols * ROWS, 0:C3])
        for a in sides:
            parts.append(res_h[p][(di - 1) if a else (2 + di), :, 0:C3])
        kernel = wu_ref[start * 128 : (start + len(phases)) * 128, 0:C3]
        got = nt_dot(jnp.concatenate(parts, axis=0), kernel)
        for n, (a, b) in enumerate(phases):
            lanes = slice(n * 128, (n + 1) * 128)
            for k in range(2):
                at = (k * wide_cols + dj - b - low) * ROWS
                value = got[at : at + span * ROWS, lanes]
                at = 2 * wide_cols * ROWS + sides.index(a) * 32 + k * 16 + dj - b
                edge = got[at : at + span, lanes]
                if (a, b, k) in total[p]:
                    value = value + total[p][a, b, k]
                    edge = edge + rim[p][a, b, k]
                total[p][a, b, k] = value
                rim[p][a, b, k] = edge

    def conv_up_steps(p):
        for di in range(3):
            for dj in range(3):
                yield lambda di=di, dj=dj: conv_up(p, di, dj)

    bias_up = jnp.concatenate([bu_ref[...], jnp.zeros((1, 32), F32)], axis=1)
    g4 = jnp.concatenate([g4_ref[...], jnp.zeros((1, 32), F32)], axis=1)

    def act_four(value):
        square = jnp.sum(value * value, axis=1, keepdims=True)
        return silu(value * lax.rsqrt(square * (1.0 / C4) + EPSILON) * g4)

    def fine_rows(p, a, b, k):
        value = act_four(rounded(rim[p][a, b, k] + bias_up))
        index = lax.broadcasted_iota(jnp.int32, (span, 1), 0)
        if b:
            inside = jnp.logical_or(index > 0, jnp.logical_not(first_col))
        else:
            inside = jnp.logical_or(index < span - 1, jnp.logical_not(last_col))
        value = keep(jnp.logical_and(inside, jnp.logical_not(first_row if a else last_row)), value)
        start = (0 if b else FEXT) + (0 if a else FROWS + 1)
        z4[p + 1][k, pl.ds(start, span, stride=2 * FEXT), :] = value

    def fine_column(p, b, j):
        fx = 2 * j if b else 2 * j + 1
        for k in range(2):
            for a in range(2):
                value = rounded(total[p][a, b, k][j * ROWS : (j + 1) * ROWS] + bias_up)
                if 1 <= fx <= 2 * COLS:
                    s4[p][k, pl.ds((fx - 1) * FROWS + a, ROWS, stride=2), :] = value
                value = act_four(value)
                if fx == 0:
                    value = keep(jnp.logical_not(first_col), value)
                if fx == FINE - 1:
                    value = keep(jnp.logical_not(last_col), value)
                z4[p + 1][k, pl.ds(fx * FEXT + 1 + a, ROWS, stride=2), :] = value
        shift_fine(p + 1, fx)

    def shift_fine(group, fx):
        for dy in range(3):
            rows = slice(fx * FEXT + dy, fx * FEXT + dy + FROWS)
            act4_d[group][dy, fx * FROWS : (fx + 1) * FROWS, :] = pair_of(z4[group], rows, slice(None))

    def fine_steps(p):
        for a in range(2):
            for b in range(2):
                for k in range(2):
                    yield lambda a=a, b=b, k=k: fine_rows(p, a, b, k)
        for j in range(span):
            for b in (1, 0):
                yield lambda b=b, j=j: fine_column(p, b, j)

    def put_cached(fx, row0, joined, first):
        rows = joined.shape[0]
        for t in range(2):
            at = first + t * C4
            value = jnp.concatenate([joined[:, at : at + C4], jnp.zeros((rows, 32), F32)], axis=1)
            z4[0][t, fx * FEXT + row0 : fx * FEXT + row0 + rows, :] = value

    def cached_column(fx):
        if 0 < fx < FINE - 1:
            at = (fx - 1) * COLQ
            start = at // 128 * 128
            first = at - start
            strip = slice(XW + PW + start, XW + PW + start + 256)
            put_cached(fx, 1, wide(q_ref[:, start : start + 256]), first)
            put_cached(fx, 0, above(strip)[1:2], first)
            put_cached(fx, FROWS + 1, below(strip)[0:1], first)
        else:
            lanes = (right if fx else left)(slice(QAT, QAT + 384))
            put_cached(fx, 0, lanes[17:18], 0)
            put_cached(fx, 1, lanes[0:16], 0)
            put_cached(fx, 1 + ROWS, lanes[0:16], COLQ)
            put_cached(fx, FROWS + 1, lanes[18:19], 0)
        shift_fine(0, fx)

    def cached_steps():
        for fx in range(FINE):
            yield lambda fx=fx: cached_column(fx)

    size = 2 * COLS * FROWS
    done = [None, None]

    def conv_four(p, dy, dx):
        at = dx * FROWS
        parts = [act4_d[group][dy, at : at + size, :] for group in (p, p + 1)]
        got = nt_dot(jnp.concatenate(parts, axis=1), w4_ref[3 * dy + dx])
        done[p] = got if done[p] is None else done[p] + got

    def conv_four_steps(p):
        for dy in range(3):
            for dx in range(3):
                yield lambda dy=dy, dx=dx: conv_four(p, dy, dx)

    b4 = b4_ref[...]
    bias_four = jnp.concatenate([b4, b4], axis=1)
    first = lane_mask(FROWS, C4)

    def out_column(p, fx):
        rows = slice(fx * FROWS, (fx + 1) * FROWS)
        other = pltpu.roll(s4[p][1, rows, :], C4, 1)
        skip = jnp.concatenate([jnp.where(first, s4[p][0, rows, :], other), other[:, 0:64]], axis=1)
        value = (done[p][rows] + bias_four + skip).astype(BF16)
        out_ref[:, fx * 384 + p * 192 : fx * 384 + (p + 1) * 192] = value

    def out_steps(p):
        for fx in range(2 * COLS):
            yield lambda fx=fx: out_column(p, fx)

    weave(coarse_steps(0), coarse_steps(1))
    weave(conv_three_steps(0), coarse_steps(2), cached_steps())
    later = list(conv_three_steps(1))
    weave(later[:13], result_steps(0))
    weave(conv_up_steps(0))
    weave(later[13:], fine_steps(0))
    later = list(conv_four_steps(0))
    weave(later[:4], result_steps(1))
    weave(conv_up_steps(1))
    weave(later[4:], fine_steps(1))
    weave(conv_four_steps(1), out_steps(0))
    weave(out_steps(1))


def split_pairs(flat_ref, parts, pairs, taps, stride):
    low = lane_mask(taps, 64)
    zero = jnp.zeros((taps, 128), F32)
    for pair in pairs:
        v0, v1, v2 = [flat_ref[:, (3 * pair + q) * 128 : (3 * pair + q + 1) * 128].astype(F32) for q in range(3)]
        r1, r2 = pltpu.roll(v1, 64, 1), pltpu.roll(v2, 64, 1)
        at = 2 * pair * stride
        parts[0, at : at + taps, :] = v0
        parts[1, at : at + taps, :] = jnp.where(low, v1, zero)
        parts[0, at + stride : at + stride + taps, :] = jnp.where(low, r1, r2)
        parts[1, at + stride : at + stride + taps, :] = jnp.where(low, r2, zero)


def prep_three_kernel(flat_ref, out_ref, parts):
    split_pairs(flat_ref, parts, range(C3 // 2), 27, 40)
    for tap in range(27):
        both = [parts[q, pl.ds(tap, C3, stride=40), :] for q in range(2)]
        out_ref[tap] = jnp.concatenate(both, axis=1).astype(BF16)


def prep_four_kernel(up_ref, four_ref, up_out, four_out, parts_u, parts_f):
    split_pairs(up_ref, parts_u, range(C4 // 2), 9, 24)
    taps = {}
    for tap in range(9):
        for q in range(2):
            taps[tap, q] = parts_u[q, pl.ds(tap, C4, stride=24), :]
    spans = {(0, 0): (0,), (0, 1): (1, 2), (1, 0): (0, 1), (1, 1): (2,)}
    rest = jnp.zeros((32, 256), BF16)
    for (di, dj), (start, phases) in up_slots().items():
        for n, (a, b) in enumerate(phases):
            tiles = []
            for q in range(2):
                total = None
                for dy in spans[a, di - a]:
                    for dx in spans[b, dj - b]:
                        one = taps[3 * dy + dx, q]
                        total = one if total is None else total + one
                tiles.append(total)
            at = (start + n) * 128
            up_out[at : at + C4, :] = jnp.concatenate(tiles, axis=1).astype(BF16)
            up_out[at + C4 : at + 128, :] = rest
    lane = lax.broadcasted_iota(jnp.int32, (27, 128), 1)
    empty = jnp.zeros((27, 128), F32)
    for four in range(C4 // 4):
        at = 3 * four * 128
        v0, v1, v2 = [four_ref[:, at + q * 128 : at + (q + 1) * 128].astype(F32) for q in range(3)]
        second = jnp.where(lane < 32, pltpu.roll(v0, 32, 1), pltpu.roll(v1, 32, 1))
        third = jnp.where(lane < 64, pltpu.roll(v1, 64, 1), pltpu.roll(v2, 64, 1))
        for m, value in enumerate((v0, second, third, pltpu.roll(v2, 96, 1))):
            at = (4 * four + m) * 40
            parts_f[at : at + 27, :] = jnp.where(lane < C4, value, empty)
    none = jnp.zeros((C4, 128), BF16)
    for place in range(9):
        four_out[place, 0:C4, 384:512] = none
        four_out[place, C4 : 2 * C4, 0:128] = none
        for t in range(3):
            kernel = parts_f[pl.ds(9 * t + place, C4, stride=40), :].astype(BF16)
            four_out[place, 0:C4, t * 128 : (t + 1) * 128] = kernel
            four_out[place, C4 : 2 * C4, (t + 1) * 128 : (t + 2) * 128] = kernel


def row_strips(refs, low_flag, out_ref):
    at = 0
    for ref in refs:
        rows, width = ref.shape
        out_ref[:, at : at + width] = jnp.where(low_flag, ref[0:2, :], ref[rows - 2 : rows, :])
        at += width


def row_strips_kernel(x_ref, p_ref, q_ref, even_ref, odd_ref, x_own, p_own, q_own, sems):
    own = (x_own, p_own, q_own)
    copies = [
        pltpu.make_async_copy(source, target, sems.at[n])
        for n, (source, target) in enumerate(zip((x_ref, p_ref, q_ref), own))
    ]
    for copy in copies:
        copy.start()
    for copy in copies:
        copy.wait()
    row_odd = lax.rem(lax.axis_index("row"), 2) == 1
    row_strips(own, row_odd, even_ref)
    row_strips(own, jnp.logical_not(row_odd), odd_ref)


def col_strips_kernel(x_ref, p_ref, q_ref, odd_row, even_row, _, out_ref, *, col_size, parity):
    row_odd = lax.rem(lax.axis_index("row"), 2) == 1
    col = lax.axis_index("section") * col_size + lax.axis_index("col")
    take_low = lax.rem(col, 2) == parity
    strips = (
        jnp.where(row_odd, even_row[...], odd_row[...]),
        jnp.where(row_odd, odd_row[...], even_row[...]),
    )

    def put(rows, at, low, high):
        out_ref[rows, at : at + low.shape[1]] = jnp.where(take_low, low, high)

    start = 0
    for ref, at, width, lanes in (
        (x_ref, 0, XW, 2 * COLX), (p_ref, 2 * COLX, PW, 2 * COLP), (q_ref, QAT, QW, COLQ)
    ):
        high = width - lanes
        if ref is q_ref:
            for half in range(2):
                rows = slice(half * ROWS, (half + 1) * ROWS)
                put(slice(0, ROWS), at + half * lanes, ref[rows, 0:lanes], ref[rows, high:width])
        else:
            put(slice(0, ROWS), at, ref[:, 0:lanes], ref[:, high:width])
        for place, strip in enumerate(strips):
            rows = slice(ROWS + 2 * place, ROWS + 2 * place + 2)
            put(rows, at, strip[:, start : start + lanes], strip[:, start + high : start + width])
            if ref is q_ref:
                out_ref[rows, at + lanes : at + 2 * lanes] = jnp.zeros((2, lanes), BF16)
        start += width


def call(kernel, operands, outputs, scratch, megabytes, moved=0, unread=0, space=pl.ANY):
    cost = pl.CostEstimate(flops=moved, bytes_accessed=moved, transcendentals=0) if moved else None
    vmem = pl.BlockSpec(memory_space=pltpu.VMEM)
    shapes = [jax.ShapeDtypeStruct(shape, BF16) for shape in outputs]
    got = pl.pallas_call(
        kernel,
        out_shape=shapes,
        in_specs=[vmem] * (len(operands) - unread) + [pl.BlockSpec(memory_space=space)] * unread,
        out_specs=[vmem] * len(outputs),
        scratch_shapes=scratch,
        cost_estimate=cost,
        compiler_params=pltpu.CompilerParams(vmem_limit_bytes=megabytes * 1024 * 1024),
    )(*operands)
    return got[0] if len(outputs) == 1 else got


def swap_pairs(count, start):
    out = []
    for low in range(start, count - 1, 2):
        out += [(low, low + 1), (low + 1, low)]
    return out


def shards(
    section_input,
    cache_three,
    gain_three,
    bias_three,
    weight_three,
    weight_up,
    bias_up,
    cache_four,
    gain_four,
    weight_four,
    bias_four,
):
    row_count = lax.axis_size("row")
    col_size = lax.axis_size("col")
    col_count = lax.axis_size("section") * col_size
    tile = (section_input, cache_three, cache_four)

    row_strip = (2, XW + PW + QW)
    own = [pltpu.VMEM(block.shape, BF16) for block in tile]
    even_strip, odd_strip = call(
        row_strips_kernel,
        tile,
        [row_strip] * 2,
        [*own, pltpu.SemaphoreType.DMA((3,))],
        62, unread=3, space=pltpu.HBM,
    )
    even_row = lax.ppermute(even_strip, "row", swap_pairs(row_count, 0))
    odd_row = lax.ppermute(odd_strip, "row", swap_pairs(row_count, 1))

    w3 = call(
        prep_three_kernel,
        (weight_three,),
        [(27, C3, 256)],
        [pltpu.VMEM((2, 40 * C3, 128), F32)],
        16, 8_000_000,
    )
    wu, w4 = call(
        prep_four_kernel,
        (weight_up, weight_four),
        [(16 * 128, 256), (9, 2 * C4, 512)],
        [
            pltpu.VMEM((2, 24 * C4, 128), F32),
            pltpu.VMEM((40 * C4, 128), F32),
        ],
        16, 8_000_000,
    )

    col_strip = (ROWS + 4, QAT + 2 * COLQ)

    def swap_columns(parity):
        def col_kernel(*refs):
            col_strips_kernel(*refs, col_size=col_size, parity=1 - parity)

        strip = call(col_kernel, (*tile, odd_row, even_row, w3), [col_strip], [], 4, unread=1)
        return lax.ppermute(strip, ("section", "col"), swap_pairs(col_count, parity))

    even_col = swap_columns(0)
    odd_col = swap_columns(1)

    def kernel(*refs):
        main_kernel(*refs, row_count=row_count, col_count=col_count, col_size=col_size)

    operands = (
        *tile, odd_row, even_row, even_col, odd_col,
        gain_three.reshape(1, C3), bias_three.reshape(1, C3), w3, wu, bias_up.reshape(1, C4),
        gain_four.reshape(1, C4), w4, bias_four.reshape(1, C4),
    )
    scratch = [pltpu.VMEM((3, 16 * EXT, 128), F32)] * 3
    scratch += [pltpu.VMEM((2, (2 * WIDE + 2) * EXT, 128), F32)] * 3
    scratch += [pltpu.VMEM((3, 2 * WIDE * ROWS, 256), BF16)] * 3
    scratch += [pltpu.VMEM((6, 2 * 16, 256), BF16)] * 3
    scratch += [pltpu.VMEM((2, (2 * MID + 4) * EXT, 128), F32)] * 2
    scratch += [pltpu.VMEM((3, 2 * MID * ROWS, 256), BF16)] * 2
    scratch += [pltpu.VMEM((4, 2 * 16, 256), BF16)] * 2
    scratch += [pltpu.VMEM((2, FINE * FEXT, 128), F32)] * 3
    scratch += [pltpu.VMEM((2, 2 * COLS * FROWS, 128), F32)] * 2
    scratch += [pltpu.VMEM((3, FINE * FROWS, 256), BF16)] * 3
    return call(kernel, operands, [(FROWS, 2 * COLS * FRAMES * C4)], scratch, 32)


def solution(mesh):
    tiled = P("row", ("section", "col"))
    return jax.shard_map(
        shards,
        mesh=mesh,
        in_specs=(tiled, tiled, P(), P(), P(), P(), P(), tiled, P(), P(), P()),
        out_specs=tiled,
        check_vma=False,
    )
```

```python
import jax
import jax.numpy as jnp
from jax import lax
from jax.experimental import pallas as pl
from jax.experimental.pallas import tpu as pltpu
from jax.sharding import PartitionSpec as P

EPSILON = 1e-06
BF16 = jnp.bfloat16
F32 = jnp.float32

ROWS = 16
COLS = 10
C3 = 192
C4 = 96
FRAMES = 4
WIDE = COLS + 4
MID = COLS + 2
EXT = 24
FINE = 2 * COLS + 2
FROWS = 2 * ROWS
FEXT = 40
XW = COLS * FRAMES * C3
PW = COLS * 2 * C3
QW = 2 * COLS * 2 * C4
COLX = FRAMES * C3
COLP = 2 * C3
COLQ = 2 * C4
QAT = 2 * COLX + 2 * COLP


def nt_dot(lhs, rhs):
    return lax.dot_general(lhs, rhs, (((1,), (1,)), ((), ())), preferred_element_type=F32)


def silu(value):
    half = 0.5 * value
    return half + half * jnp.tanh(half)


def lane_mask(rows, below):
    return lax.broadcasted_iota(jnp.int32, (rows, 128), 1) < below


def split_pair(v0, v1, v2):
    low = lane_mask(v0.shape[0], 64)
    r1 = pltpu.roll(v1, 64, 1)
    r2 = pltpu.roll(v2, 64, 1)
    zero = jnp.zeros_like(v1)
    return (v0, jnp.where(low, v1, zero)), (jnp.where(low, r1, r2), jnp.where(low, r2, zero))


def norm_pair(v0, v1, v2, gains):
    low = lane_mask(v0.shape[0], 64)
    sq1 = v1 * v1
    zero = jnp.zeros_like(v1)
    sum_a = jnp.sum(v0 * v0 + jnp.where(low, sq1, zero), axis=1, keepdims=True)
    sum_b = jnp.sum(v2 * v2 + jnp.where(low, zero, sq1), axis=1, keepdims=True)
    inv_a = lax.rsqrt(sum_a * (1.0 / C3) + EPSILON)
    inv_b = lax.rsqrt(sum_b * (1.0 / C3) + EPSILON)
    return (
        silu(v0 * inv_a * gains[0]),
        silu(v1 * jnp.where(low, inv_a, inv_b) * gains[1]),
        silu(v2 * inv_b * gains[2]),
    )


def weave(*streams):
    lists = []
    for stream in streams:
        lists.append(list(stream))
    order = []
    for place, steps in enumerate(lists):
        order += [((n + 0.5) / len(steps), place, step) for n, step in enumerate(steps)]
    for _, _, step in sorted(order, key=lambda entry: entry[:2]):
        step()


def main_kernel(
    x_ref, p_ref, q_ref, odd_row, even_row, even_col, odd_col,
    g3_ref, b3_ref, w3_ref, wu_ref, bu_ref, g4_ref, w4_ref, b4_ref,
    out_ref,
    raw0, raw1, raw2, act0, act1, act2, actd0, actd1, actd2, halo0, halo1, halo2,
    res0, res1, resd0, resd1, resh0, resh1, z0, z1, z2, s0, s1, fine0, fine1, fine2,
    *, row_count, col_count, col_size,
):
    raw, act, act_d, halo_d = (raw0, raw1, raw2), (act0, act1, act2), (actd0, actd1, actd2), (halo0, halo1, halo2)
    res, res_d, res_h = (res0, res1), (resd0, resd1), (resh0, resh1)
    z4, s4, act4_d = (z0, z1, z2), (s0, s1), (fine0, fine1, fine2)
    row = lax.axis_index("row")
    col = lax.axis_index("section") * col_size + lax.axis_index("col")
    row_odd = lax.rem(row, 2) == 1
    col_odd = lax.rem(col, 2) == 1
    first_row, last_row = row == 0, row == row_count - 1
    first_col, last_col = col == 0, col == col_count - 1

    def wide(value):
        return value.astype(F32)

    def pick(flag, one, other, *index):
        return wide(jnp.where(flag, one[index], other[index]))

    def above(lanes):
        return pick(row_odd, even_row, odd_row, slice(0, 2), lanes)

    def below(lanes):
        return pick(row_odd, odd_row, even_row, slice(0, 2), lanes)

    def left(lanes):
        return pick(col_odd, even_col, odd_col, slice(0, ROWS + 4), lanes)

    def right(lanes):
        return pick(col_odd, odd_col, even_col, slice(0, ROWS + 4), lanes)

    def keep(inside, value):
        return jnp.where(inside, value, jnp.zeros_like(value))

    def rounded(value):
        return value.astype(BF16).astype(F32)

    def pair_of(ref, *index):
        return jnp.concatenate([ref[(0,) + index], ref[(1,) + index]], axis=1).astype(BF16)

    g3 = g3_ref[...]
    gains = (
        g3[:, 0:128],
        jnp.concatenate([g3[:, 128:192], g3[:, 0:64]], axis=1),
        g3[:, 64:192],
    )

    def load_column(group, jj):
        base = jj * EXT
        for q in range(3):
            if 2 <= jj < WIDE - 2:
                at = (jj - 2) * COLX + (3 * (group - 1) + q) * 128
                if group == 0:
                    at = (jj - 2) * COLP + q * 128
                src, strip_at = (x_ref, at) if group else (p_ref, XW + at)
                strip = slice(strip_at, strip_at + 128)
                raw[group][q, base : base + 16, :] = wide(src[:, at : at + 128])
                raw[group][q, base + 16 : base + 18, :] = above(strip)
                raw[group][q, base + 18 : base + 20, :] = below(strip)
            else:
                side, lane = (left, jj) if jj < 2 else (right, jj - WIDE + 2)
                at = lane * COLX + (3 * (group - 1) + q) * 128
                if group == 0:
                    at = 2 * COLX + lane * COLP + q * 128
                raw[group][q, base : base + 20, :] = side(slice(at, at + 128))
        tiles = [raw[group][q, base : base + EXT, :] for q in range(3)]
        if group:
            tiles = norm_pair(*tiles, gains)
        for half, pair in enumerate(split_pair(*tiles)):
            at = (half * WIDE + jj) * EXT
            for q in range(2):
                act[group][q, at : at + 2, :] = pair[q][16:18]
                act[group][q, at + 2 : at + 18, :] = pair[q][0:16]
                act[group][q, at + 18 : at + 20, :] = pair[q][18:20]

    def shift_column(group, jj):
        for half in range(2):
            slab = half * WIDE + jj
            for dy in range(3):
                rows = slice(slab * EXT + 1 + dy, slab * EXT + 1 + dy + ROWS)
                act_d[group][dy, slab * ROWS : (slab + 1) * ROWS, :] = pair_of(act[group], rows, slice(None))

    def gather_rows(group, place):
        dx, ext = place // 6, (0, 1, 2, 17, 18, 19)[place % 6]
        for half in range(2):
            rows = pl.ds((half * WIDE + dx) * EXT + ext, 16, stride=EXT)
            halo_d[group][place, half * 16 : (half + 1) * 16, :] = pair_of(act[group], rows, slice(None))

    def coarse_steps(group):
        for jj in range(WIDE):
            yield lambda jj=jj: (load_column(group, jj), shift_column(group, jj))
        for place in range(18):
            yield lambda place=place: gather_rows(group, place)

    mid = MID * ROWS
    center = [[None, None], [None, None]]

    def conv_three(p, k):
        kernels = []
        pieces = []
        for dy in range(3):
            for dx in range(3):
                kernels.append(w3_ref[3 * dy + dx])
                for t in range(3):
                    parts = []
                    group, half = p + (k + t) // 2, (k + t) % 2
                    at = (half * WIDE + dx) * ROWS
                    parts.append(act_d[group][dy, at : at + MID * ROWS, :])
                    for side in range(2):
                        place = 6 * dx + 3 * side + dy
                        parts.append(halo_d[group][place, half * 16 : (half + 1) * 16, :])
                    pieces.append(jnp.concatenate(parts, axis=0))
        got = nt_dot(jnp.concatenate(pieces, axis=1), jnp.concatenate(kernels, axis=1))
        center[p][k] = got

    def conv_three_steps(p):
        for k in range(2):
            yield lambda k=k: conv_three(p, k)

    b3 = b3_ref[...]
    column = lax.broadcasted_iota(jnp.int32, (MID, 1), 0)
    cols_in = jnp.logical_and(
        jnp.logical_or(column > 0, jnp.logical_not(first_col)),
        jnp.logical_or(column < MID - 1, jnp.logical_not(last_col)),
    )

    def put_res(p, rows, value):
        res[p][0, rows, :] = value[:, 0:128]
        rest = jnp.zeros((value.shape[0], 64), F32)
        res[p][1, rows, :] = jnp.concatenate([value[:, 128:192], rest], axis=1)

    def result_column(p, jm):
        at = (jm + 1) * EXT
        tiles = [raw[p + 1][q, at : at + ROWS, :] for q in range(3)]
        for k, skip in enumerate(split_pair(*tiles)):
            slab = k * MID + jm
            value = center[p][k][jm * ROWS : (jm + 1) * ROWS] + b3
            value = rounded(value + jnp.concatenate([skip[0], skip[1][:, 0:64]], axis=1))
            if jm == 0:
                value = keep(jnp.logical_not(first_col), value)
            if jm == MID - 1:
                value = keep(jnp.logical_not(last_col), value)
            put_res(p, pl.ds(slab * EXT + 1, ROWS), value)

    def result_rows(p, side):
        rows_in = jnp.logical_not(last_row if side else first_row)
        ext = 18 if side else 17
        tiles = [raw[p + 1][q, pl.ds(EXT + ext, MID, stride=EXT), :] for q in range(3)]
        for k, skip in enumerate(split_pair(*tiles)):
            at = mid + side * 16
            value = center[p][k][at : at + MID] + b3
            value = rounded(value + jnp.concatenate([skip[0], skip[1][:, 0:64]], axis=1))
            value = keep(jnp.logical_and(cols_in, rows_in), value)
            put_res(p, pl.ds(k * MID * EXT + (17 if side else 0), MID, stride=EXT), value)

    def shift_result(p, jm):
        for k in range(2):
            slab = k * MID + jm
            for r in range(2):
                rows = slice(slab * EXT + r, slab * EXT + r + ROWS)
                res_d[p][r, slab * ROWS : (slab + 1) * ROWS, :] = pair_of(res[p], rows, slice(None))

    def gather_result(p, place):
        r, c = divmod(place, 2)
        for k in range(2):
            rows = pl.ds((k * MID + c) * EXT + ROWS + r, 16, stride=EXT)
            res_h[p][place, k * 16 : (k + 1) * 16, :] = pair_of(res[p], rows, slice(None))

    def result_steps(p):
        for side in range(2):
            yield lambda side=side: result_rows(p, side)
        for jm in range(MID):
            yield lambda jm=jm: (result_column(p, jm), shift_result(p, jm))
        for place in range(4):
            yield lambda place=place: gather_result(p, place)

    span = COLS + 1
    total = [[None, None], [None, None]]

    def conv_up(p, k):
        pieces = []
        for r in range(2):
            for c in range(2):
                at = (k * MID + c) * ROWS
                own = res_d[p][r, at : at + span * ROWS, :]
                last = res_h[p][2 * r + c, k * 16 : (k + 1) * 16, :]
                pieces.append(jnp.concatenate([own, last], axis=0))
        total[p][k] = nt_dot(jnp.concatenate(pieces, axis=1), wu_ref[...])

    def conv_up_steps(p):
        for k in range(2):
            yield lambda k=k: conv_up(p, k)

    bias_up = jnp.concatenate([bu_ref[...], jnp.zeros((1, 32), F32)], axis=1)
    g4 = jnp.concatenate([g4_ref[...], jnp.zeros((1, 32), F32)], axis=1)

    def act_four(value):
        square = jnp.sum(value * value, axis=1, keepdims=True)
        return silu(value * lax.rsqrt(square * (1.0 / C4) + EPSILON) * g4)

    def fine_rows(p, a, b, k):
        at = span * ROWS
        lanes = slice((2 * a + b) * 128, (2 * a + b + 1) * 128)
        value = rounded(total[p][k][at : at + span, lanes] + bias_up)
        ext = FROWS if a else FROWS + 1
        rows = pl.ds((0 if b else FEXT) + ext, span, stride=2 * FEXT)
        if a:
            s4[p][k, rows, :] = value
        value = act_four(value)
        index = lax.broadcasted_iota(jnp.int32, (span, 1), 0)
        if b:
            inside = jnp.logical_or(index > 0, jnp.logical_not(first_col))
        else:
            inside = jnp.logical_or(index < span - 1, jnp.logical_not(last_col))
        if not a:
            inside = jnp.logical_and(inside, jnp.logical_not(last_row))
        z4[p + 1][k, rows, :] = keep(inside, value)

    top = lax.broadcasted_iota(jnp.int32, (ROWS, 1), 0) > 0
    rows_in = jnp.logical_or(top, jnp.logical_not(first_row))

    def fine_column(p, b, j):
        fx = 2 * j if b else 2 * j + 1
        for k in range(2):
            for a in range(2):
                lanes = slice((2 * a + b) * 128, (2 * a + b + 1) * 128)
                value = rounded(total[p][k][j * ROWS : (j + 1) * ROWS, lanes] + bias_up)
                rows = pl.ds(fx * FEXT + 1 - a, ROWS, stride=2)
                if 1 <= fx <= 2 * COLS:
                    s4[p][k, rows, :] = value
                value = act_four(value)
                if a:
                    value = keep(rows_in, value)
                if fx == 0:
                    value = keep(jnp.logical_not(first_col), value)
                if fx == FINE - 1:
                    value = keep(jnp.logical_not(last_col), value)
                z4[p + 1][k, rows, :] = value
        shift_fine(p + 1, fx)

    def shift_fine(group, fx):
        for dy in range(3):
            rows = slice(fx * FEXT + dy, fx * FEXT + dy + FROWS)
            act4_d[group][dy, fx * FROWS : (fx + 1) * FROWS, :] = pair_of(z4[group], rows, slice(None))

    def fine_steps(p):
        for a in range(2):
            for b in range(2):
                for k in range(2):
                    yield lambda a=a, b=b, k=k: fine_rows(p, a, b, k)
        for j in range(span):
            for b in (1, 0):
                yield lambda b=b, j=j: fine_column(p, b, j)

    def put_cached(fx, row0, joined, first):
        rows = joined.shape[0]
        for t in range(2):
            at = first + t * C4
            value = jnp.concatenate([joined[:, at : at + C4], jnp.zeros((rows, 32), F32)], axis=1)
            z4[0][t, fx * FEXT + row0 : fx * FEXT + row0 + rows, :] = value

    def cached_column(fx):
        if 0 < fx < FINE - 1:
            at = (fx - 1) * COLQ
            start = at // 128 * 128
            first = at - start
            strip = slice(XW + PW + start, XW + PW + start + 256)
            put_cached(fx, 1, wide(q_ref[:, start : start + 256]), first)
            put_cached(fx, 0, above(strip)[1:2], first)
            put_cached(fx, FROWS + 1, below(strip)[0:1], first)
        else:
            lanes = (right if fx else left)(slice(QAT, QAT + 384))
            put_cached(fx, 0, lanes[17:18], 0)
            put_cached(fx, 1, lanes[0:16], 0)
            put_cached(fx, 1 + ROWS, lanes[0:16], COLQ)
            put_cached(fx, FROWS + 1, lanes[18:19], 0)
        shift_fine(0, fx)

    def cached_steps():
        for fx in range(FINE):
            yield lambda fx=fx: cached_column(fx)

    size = COLS * FROWS
    done = [[None, None], [None, None]]

    def conv_four(p, half):
        pieces = []
        for dy in range(3):
            for dx in range(3):
                at = (dx + half * COLS) * FROWS
                pieces += [act4_d[group][dy, at : at + size, :] for group in (p, p + 1)]
        kernel = jnp.concatenate([w4_ref[dy] for dy in range(3)], axis=1)
        done[p][half] = nt_dot(jnp.concatenate(pieces, axis=1), kernel)

    def conv_four_steps(p):
        for half in range(2):
            yield lambda half=half: conv_four(p, half)

    b4 = b4_ref[...]
    bias_four = jnp.concatenate([b4, b4], axis=1)
    first = lane_mask(FROWS, C4)

    def out_column(p, fx):
        rows = slice((fx + 1) * FEXT + 1, (fx + 1) * FEXT + 1 + FROWS)
        other = pltpu.roll(s4[p][1, rows, :], C4, 1)
        skip = jnp.concatenate([jnp.where(first, s4[p][0, rows, :], other), other[:, 0:64]], axis=1)
        at = fx % COLS * FROWS
        value = (done[p][fx // COLS][at : at + FROWS] + bias_four + skip).astype(BF16)
        out_ref[:, fx * 384 + p * 192 : fx * 384 + (p + 1) * 192] = value

    def out_steps(p):
        for fx in range(2 * COLS):
            yield lambda fx=fx: out_column(p, fx)

    weave(coarse_steps(0), coarse_steps(1))
    weave(conv_three_steps(0), coarse_steps(2), cached_steps())
    weave(conv_three_steps(1), result_steps(0))
    weave(conv_up_steps(0))
    weave(fine_steps(0), result_steps(1))
    weave(conv_up_steps(1))
    weave(conv_four_steps(0), fine_steps(1))
    later = list(conv_four_steps(1))
    ends = list(out_steps(1))
    weave(later[:1], out_steps(0))
    weave(later[1:], ends[:10])
    weave(ends[10:])


def split_pairs(flat_ref, parts, pairs, taps, stride):
    low = lane_mask(taps, 64)
    zero = jnp.zeros((taps, 128), F32)
    for pair in pairs:
        v0, v1, v2 = [flat_ref[:, (3 * pair + q) * 128 : (3 * pair + q + 1) * 128].astype(F32) for q in range(3)]
        r1, r2 = pltpu.roll(v1, 64, 1), pltpu.roll(v2, 64, 1)
        at = 2 * pair * stride
        parts[0, at : at + taps, :] = v0
        parts[1, at : at + taps, :] = jnp.where(low, v1, zero)
        parts[0, at + stride : at + stride + taps, :] = jnp.where(low, r1, r2)
        parts[1, at + stride : at + stride + taps, :] = jnp.where(low, r2, zero)


def prep_three_kernel(flat_ref, out_ref, parts):
    split_pairs(flat_ref, parts, range(C3 // 2), 27, 40)
    for tap in range(27):
        both = [parts[q, pl.ds(tap, C3, stride=40), :] for q in range(2)]
        t, place = divmod(tap, 9)
        out_ref[place, :, t * 256 : (t + 1) * 256] = jnp.concatenate(both, axis=1).astype(BF16)


def prep_four_kernel(up_ref, four_ref, up_out, four_out, parts_u, parts_f):
    split_pairs(up_ref, parts_u, range(C4 // 2), 9, 24)
    taps = {}
    for tap in range(9):
        for q in range(2):
            taps[tap, q] = parts_u[q, pl.ds(tap, C4, stride=24), :]
    spans = {(0, 0): (0,), (0, 1): (1, 2), (1, 0): (0, 1), (1, 1): (2,)}
    rest = jnp.zeros((32, 256), BF16)
    for a in range(2):
        for b in range(2):
            at = (2 * a + b) * 128
            for r in range(2):
                for c in range(2):
                    tiles = []
                    for q in range(2):
                        total = None
                        for dy in spans[a, r]:
                            for dx in spans[b, c]:
                                one = taps[3 * dy + dx, q]
                                total = one if total is None else total + one
                        tiles.append(total)
                    lanes = slice((2 * r + c) * 256, (2 * r + c + 1) * 256)
                    up_out[at : at + C4, lanes] = jnp.concatenate(tiles, axis=1).astype(BF16)
                    up_out[at + C4 : at + 128, lanes] = rest
    lane = lax.broadcasted_iota(jnp.int32, (27, 128), 1)
    empty = jnp.zeros((27, 128), F32)
    for four in range(C4 // 4):
        at = 3 * four * 128
        v0, v1, v2 = [four_ref[:, at + q * 128 : at + (q + 1) * 128].astype(F32) for q in range(3)]
        second = jnp.where(lane < 32, pltpu.roll(v0, 32, 1), pltpu.roll(v1, 32, 1))
        third = jnp.where(lane < 64, pltpu.roll(v1, 64, 1), pltpu.roll(v2, 64, 1))
        for m, value in enumerate((v0, second, third, pltpu.roll(v2, 96, 1))):
            at = (4 * four + m) * 40
            parts_f[at : at + 27, :] = jnp.where(lane < C4, value, empty)
    none = jnp.zeros((C4, 128), BF16)
    for place in range(9):
        dy, dx = divmod(place, 3)
        at = dx * 512
        four_out[dy, 0:C4, at + 384 : at + 512] = none
        four_out[dy, C4 : 2 * C4, at : at + 128] = none
        for t in range(3):
            kernel = parts_f[pl.ds(9 * t + place, C4, stride=40), :].astype(BF16)
            four_out[dy, 0:C4, at + t * 128 : at + (t + 1) * 128] = kernel
            four_out[dy, C4 : 2 * C4, at + (t + 1) * 128 : at + (t + 2) * 128] = kernel


def row_strips(refs, low_flag, out_ref):
    at = 0
    for ref in refs:
        rows, width = ref.shape
        out_ref[:, at : at + width] = jnp.where(low_flag, ref[0:2, :], ref[rows - 2 : rows, :])
        at += width


def row_strips_kernel(x_ref, p_ref, q_ref, even_ref, odd_ref, x_own, p_own, q_own, sems):
    own = (x_own, p_own, q_own)
    copies = [
        pltpu.make_async_copy(source, target, sems.at[n])
        for n, (source, target) in enumerate(zip((x_ref, p_ref, q_ref), own))
    ]
    for copy in copies:
        copy.start()
    for copy in copies:
        copy.wait()
    row_odd = lax.rem(lax.axis_index("row"), 2) == 1
    row_strips(own, row_odd, even_ref)
    row_strips(own, jnp.logical_not(row_odd), odd_ref)


def col_strips_kernel(x_ref, p_ref, q_ref, odd_row, even_row, _, out_ref, *, col_size, parity):
    row_odd = lax.rem(lax.axis_index("row"), 2) == 1
    col = lax.axis_index("section") * col_size + lax.axis_index("col")
    take_low = lax.rem(col, 2) == parity
    strips = (
        jnp.where(row_odd, even_row[...], odd_row[...]),
        jnp.where(row_odd, odd_row[...], even_row[...]),
    )

    def put(rows, at, low, high):
        out_ref[rows, at : at + low.shape[1]] = jnp.where(take_low, low, high)

    start = 0
    for ref, at, width, lanes in (
        (x_ref, 0, XW, 2 * COLX), (p_ref, 2 * COLX, PW, 2 * COLP), (q_ref, QAT, QW, COLQ)
    ):
        high = width - lanes
        if ref is q_ref:
            for half in range(2):
                rows = slice(half * ROWS, (half + 1) * ROWS)
                put(slice(0, ROWS), at + half * lanes, ref[rows, 0:lanes], ref[rows, high:width])
        else:
            put(slice(0, ROWS), at, ref[:, 0:lanes], ref[:, high:width])
        for place, strip in enumerate(strips):
            rows = slice(ROWS + 2 * place, ROWS + 2 * place + 2)
            put(rows, at, strip[:, start : start + lanes], strip[:, start + high : start + width])
            if ref is q_ref:
                out_ref[rows, at + lanes : at + 2 * lanes] = jnp.zeros((2, lanes), BF16)
        start += width


def call(kernel, operands, outputs, scratch, megabytes, moved=0, unread=0, space=pl.ANY):
    cost = pl.CostEstimate(flops=moved, bytes_accessed=moved, transcendentals=0) if moved else None
    vmem = pl.BlockSpec(memory_space=pltpu.VMEM)
    shapes = [jax.ShapeDtypeStruct(shape, BF16) for shape in outputs]
    got = pl.pallas_call(
        kernel,
        out_shape=shapes,
        in_specs=[vmem] * (len(operands) - unread) + [pl.BlockSpec(memory_space=space)] * unread,
        out_specs=[vmem] * len(outputs),
        scratch_shapes=scratch,
        cost_estimate=cost,
        compiler_params=pltpu.CompilerParams(vmem_limit_bytes=megabytes * 1024 * 1024),
    )(*operands)
    return got[0] if len(outputs) == 1 else got


def swap_pairs(count, start):
    out = []
    for low in range(start, count - 1, 2):
        out += [(low, low + 1), (low + 1, low)]
    return out


def shards(
    section_input,
    cache_three,
    gain_three,
    bias_three,
    weight_three,
    weight_up,
    bias_up,
    cache_four,
    gain_four,
    weight_four,
    bias_four,
):
    row_count = lax.axis_size("row")
    col_size = lax.axis_size("col")
    col_count = lax.axis_size("section") * col_size
    tile = (section_input, cache_three, cache_four)

    row_strip = (2, XW + PW + QW)
    own = [pltpu.VMEM(block.shape, BF16) for block in tile]
    even_strip, odd_strip = call(
        row_strips_kernel,
        tile,
        [row_strip] * 2,
        [*own, pltpu.SemaphoreType.DMA((3,))],
        62, unread=3, space=pltpu.HBM,
    )
    even_row = lax.ppermute(even_strip, "row", swap_pairs(row_count, 0))
    odd_row = lax.ppermute(odd_strip, "row", swap_pairs(row_count, 1))

    w3 = call(
        prep_three_kernel,
        (weight_three,),
        [(9, C3, 3 * 256)],
        [pltpu.VMEM((2, 40 * C3, 128), F32)],
        16, 8_000_000,
    )
    wu, w4 = call(
        prep_four_kernel,
        (weight_up, weight_four),
        [(4 * 128, 4 * 256), (3, 2 * C4, 3 * 512)],
        [
            pltpu.VMEM((2, 24 * C4, 128), F32),
            pltpu.VMEM((40 * C4, 128), F32),
        ],
        16, 8_000_000,
    )

    col_strip = (ROWS + 4, QAT + 2 * COLQ)

    def swap_columns(parity):
        def col_kernel(*refs):
            col_strips_kernel(*refs, col_size=col_size, parity=1 - parity)

        strip = call(col_kernel, (*tile, odd_row, even_row, w3), [col_strip], [], 4, unread=1)
        return lax.ppermute(strip, ("section", "col"), swap_pairs(col_count, parity))

    even_col = swap_columns(0)
    odd_col = swap_columns(1)

    def kernel(*refs):
        main_kernel(*refs, row_count=row_count, col_count=col_count, col_size=col_size)

    operands = (
        *tile, odd_row, even_row, even_col, odd_col,
        gain_three.reshape(1, C3), bias_three.reshape(1, C3), w3, wu, bias_up.reshape(1, C4),
        gain_four.reshape(1, C4), w4, bias_four.reshape(1, C4),
    )
    scratch = [pltpu.VMEM((3, 16 * EXT, 128), F32)] * 3
    scratch += [pltpu.VMEM((2, (2 * WIDE + 4) * EXT, 128), F32)] * 3
    scratch += [pltpu.VMEM((3, 2 * WIDE * ROWS, 256), BF16)] * 3
    scratch += [pltpu.VMEM((18, 2 * 16, 256), BF16)] * 3
    scratch += [pltpu.VMEM((2, (2 * MID + 5) * EXT, 128), F32)] * 2
    scratch += [pltpu.VMEM((2, 2 * MID * ROWS, 256), BF16)] * 2
    scratch += [pltpu.VMEM((4, 2 * 16, 256), BF16)] * 2
    scratch += [pltpu.VMEM((2, FINE * FEXT, 128), F32)] * 3
    scratch += [pltpu.VMEM((2, FINE * FEXT, 128), F32)] * 2
    scratch += [pltpu.VMEM((3, FINE * FROWS, 256), BF16)] * 3
    return call(kernel, operands, [(FROWS, 2 * COLS * FRAMES * C4)], scratch, 32)


def solution(mesh):
    tiled = P("row", ("section", "col"))
    return jax.shard_map(
        shards,
        mesh=mesh,
        in_specs=(tiled, tiled, P(), P(), P(), P(), P(), tiled, P(), P(), P()),
        out_specs=tiled,
        check_vma=False,
    )
```

```python
import functools
import types

import jax
import jax.numpy as jnp
from jax import lax
from jax.experimental import pallas as pl
from jax.experimental.pallas import tpu as pltpu
from jax.sharding import PartitionSpec as P

EPSILON = 1e-06
BF16 = jnp.bfloat16
F32 = jnp.float32

ROWS = 16
COLS = 10
C3 = 192
C4 = 96
FRAMES = 4
WIDE = COLS + 4
MID = COLS + 2
EXT = 24
FINE = 2 * COLS + 2
FROWS = 2 * ROWS
FEXT = 40
XW = COLS * FRAMES * C3
PW = COLS * 2 * C3
QW = 2 * COLS * 2 * C4
COLX = FRAMES * C3
COLP = 2 * C3
COLQ = 2 * C4
QAT = 2 * COLX + 2 * COLP


def nt_dot(lhs, rhs):
    return lax.dot_general(lhs, rhs, (((1,), (1,)), ((), ())), preferred_element_type=F32)


def silu(value):
    half = 0.5 * value
    return half + half * jnp.tanh(half)


def lane_mask(rows, below):
    return lax.broadcasted_iota(jnp.int32, (rows, 128), 1) < below


def split_pair(v0, v1, v2):
    low = lane_mask(v0.shape[0], 64)
    r1 = pltpu.roll(v1, 64, 1)
    r2 = pltpu.roll(v2, 64, 1)
    zero = jnp.zeros_like(v1)
    return (v0, jnp.where(low, v1, zero)), (jnp.where(low, r1, r2), jnp.where(low, r2, zero))


def norm_pair(v0, v1, v2, gains):
    low = lane_mask(v0.shape[0], 64)
    sq1 = v1 * v1
    zero = jnp.zeros_like(v1)
    sum_a = jnp.sum(v0 * v0 + jnp.where(low, sq1, zero), axis=1, keepdims=True)
    sum_b = jnp.sum(v2 * v2 + jnp.where(low, zero, sq1), axis=1, keepdims=True)
    inv_a = lax.rsqrt(sum_a * (1.0 / C3) + EPSILON)
    inv_b = lax.rsqrt(sum_b * (1.0 / C3) + EPSILON)
    return (
        silu(v0 * inv_a * gains[0]),
        silu(v1 * jnp.where(low, inv_a, inv_b) * gains[1]),
        silu(v2 * inv_b * gains[2]),
    )


def weave(*streams):
    lists = []
    for stream in streams:
        lists.append(list(stream))
    order = []
    for place, steps in enumerate(lists):
        order += [((n + 0.5) / len(steps), place, step) for n, step in enumerate(steps)]
    for _, _, step in sorted(order, key=lambda entry: entry[:2]):
        step()


FIRST = ("raw1", "act0", "act1", "actd0", "actd1")
SHARED = (*FIRST, "raw2", "act2", "actd2", "res0", "res1", "resd0", "resd1")
INNER = (2, COLS - 2)
RIMS = ((0, 2), (COLS, 2))


def stages(refs, row_count, col_count, col_size):
    x_ref, p_ref, q_ref = refs.get("x"), refs.get("p"), refs.get("q")
    odd_row, even_row = refs.get("odd_row"), refs.get("even_row")
    even_col, odd_col = refs.get("even_col"), refs.get("odd_col")
    w3_ref, wu_ref, w4_ref = refs.get("w3"), refs.get("wu"), refs.get("w4")
    out_ref = refs.get("out")

    def several(name, count):
        return [refs.get(name + str(n)) for n in range(count)]

    raw, act, act_d, halo_d = several("raw", 3), several("act", 3), several("actd", 3), several("halo", 3)
    res, res_d, res_h = several("res", 2), several("resd", 2), several("resh", 2)
    z4, s4, act4_d = several("z", 3), several("s", 2), several("fine", 3)
    row = lax.axis_index("row")
    col = lax.axis_index("section") * col_size + lax.axis_index("col")
    row_odd = lax.rem(row, 2) == 1
    col_odd = lax.rem(col, 2) == 1
    first_row, last_row = row == 0, row == row_count - 1
    first_col, last_col = col == 0, col == col_count - 1

    def wide(value):
        return value.astype(F32)

    def pick(flag, one, other, *index):
        return wide(jnp.where(flag, one[index], other[index]))

    def above(lanes):
        return pick(row_odd, even_row, odd_row, slice(0, 2), lanes)

    def below(lanes):
        return pick(row_odd, odd_row, even_row, slice(0, 2), lanes)

    def left(lanes):
        return pick(col_odd, even_col, odd_col, slice(0, ROWS + 4), lanes)

    def right(lanes):
        return pick(col_odd, odd_col, even_col, slice(0, ROWS + 4), lanes)

    def keep(inside, value):
        return jnp.where(inside, value, jnp.zeros_like(value))

    def rounded(value):
        return value.astype(BF16).astype(F32)

    def pair_of(ref, *index):
        return jnp.concatenate([ref[(0,) + index], ref[(1,) + index]], axis=1).astype(BF16)

    g3 = refs["g3"][...]
    gains = (
        g3[:, 0:128],
        jnp.concatenate([g3[:, 128:192], g3[:, 0:64]], axis=1),
        g3[:, 64:192],
    )

    def load_column(group, jj):
        base = jj * EXT
        for q in range(3):
            if 2 <= jj < WIDE - 2:
                at = (jj - 2) * COLX + (3 * (group - 1) + q) * 128
                if group == 0:
                    at = (jj - 2) * COLP + q * 128
                src, strip_at = (x_ref, at) if group else (p_ref, XW + at)
                strip = slice(strip_at, strip_at + 128)
                raw[group][q, base : base + 16, :] = wide(src[:, at : at + 128])
                raw[group][q, base + 16 : base + 18, :] = above(strip)
                raw[group][q, base + 18 : base + 20, :] = below(strip)
            else:
                side, lane = (left, jj) if jj < 2 else (right, jj - WIDE + 2)
                at = lane * COLX + (3 * (group - 1) + q) * 128
                if group == 0:
                    at = 2 * COLX + lane * COLP + q * 128
                raw[group][q, base : base + 20, :] = side(slice(at, at + 128))
        tiles = [raw[group][q, base : base + EXT, :] for q in range(3)]
        if group:
            tiles = norm_pair(*tiles, gains)
        for half, pair in enumerate(split_pair(*tiles)):
            at = (half * WIDE + jj) * EXT
            for q in range(2):
                act[group][q, at : at + 2, :] = pair[q][16:18]
                act[group][q, at + 2 : at + 18, :] = pair[q][0:16]
                act[group][q, at + 18 : at + 20, :] = pair[q][18:20]

    def shift_column(group, jj):
        for half in range(2):
            slab = half * WIDE + jj
            for dy in range(3):
                rows = slice(slab * EXT + 1 + dy, slab * EXT + 1 + dy + ROWS)
                act_d[group][dy, slab * ROWS : (slab + 1) * ROWS, :] = pair_of(act[group], rows, slice(None))

    def gather_rows(group, place):
        dx, ext = place // 6, (0, 1, 2, 17, 18, 19)[place % 6]
        for half in range(2):
            rows = pl.ds((half * WIDE + dx) * EXT + ext, 16, stride=EXT)
            halo_d[group][place, half * 16 : (half + 1) * 16, :] = pair_of(act[group], rows, slice(None))

    def coarse_steps(group, columns):
        for jj in columns:
            yield lambda jj=jj: (load_column(group, jj), shift_column(group, jj))

    def row_steps(group):
        for place in range(18):
            yield lambda place=place: gather_rows(group, place)

    center = {}
    edges = {}

    def conv_three(frames, runs):
        kernels = []
        pieces = []
        for dy in range(3):
            for dx in range(3):
                kernels.append(w3_ref[3 * dy + dx])
                for t in range(3):
                    parts = []
                    for p, k in frames:
                        group, half = p + (k + t) // 2, (k + t) % 2
                        for start, count in runs:
                            at = (half * WIDE + start + dx) * ROWS
                            parts.append(act_d[group][dy, at : at + count * ROWS, :])
                        for side in range(2):
                            place = 6 * dx + 3 * side + dy
                            parts.append(halo_d[group][place, half * 16 : (half + 1) * 16, :])
                    pieces.append(jnp.concatenate(parts, axis=0))
        got = nt_dot(jnp.concatenate(pieces, axis=1), jnp.concatenate(kernels, axis=1))
        at = 0
        for p, k in frames:
            for start, count in runs:
                for jm in range(start, start + count):
                    center[p, k, jm] = got[at : at + ROWS]
                    at += ROWS
            for side in range(2):
                edges[p, k, side] = got[at : at + 16]
                at += 16

    def conv_three_steps(runs, *batches):
        for frames in batches:
            yield lambda frames=frames: conv_three(frames, runs)

    b3 = refs["b3"][...] if "b3" in refs else None

    def put_res(p, rows, value):
        res[p][0, rows, :] = value[:, 0:128]
        rest = jnp.zeros((value.shape[0], 64), F32)
        res[p][1, rows, :] = jnp.concatenate([value[:, 128:192], rest], axis=1)

    def result_column(p, jm):
        at = (jm + 1) * EXT
        tiles = [raw[p + 1][q, at : at + ROWS, :] for q in range(3)]
        for k, skip in enumerate(split_pair(*tiles)):
            slab = k * MID + jm
            value = center[p, k, jm] + b3
            value = rounded(value + jnp.concatenate([skip[0], skip[1][:, 0:64]], axis=1))
            if jm == 0:
                value = keep(jnp.logical_not(first_col), value)
            if jm == MID - 1:
                value = keep(jnp.logical_not(last_col), value)
            put_res(p, pl.ds(slab * EXT + 1, ROWS), value)

    def result_rows(p, side, start, count):
        inside = jnp.logical_not(last_row if side else first_row)
        column = lax.broadcasted_iota(jnp.int32, (count, 1), 0) + start
        if start == 0:
            inside = jnp.logical_and(inside, jnp.logical_or(column > 0, jnp.logical_not(first_col)))
        if start + count == MID:
            inside = jnp.logical_and(inside, jnp.logical_or(column < MID - 1, jnp.logical_not(last_col)))
        rows = pl.ds((start + 1) * EXT + (18 if side else 17), count, stride=EXT)
        tiles = [raw[p + 1][q, rows, :] for q in range(3)]
        for k, skip in enumerate(split_pair(*tiles)):
            value = edges[p, k, side][start : start + count] + b3
            value = rounded(value + jnp.concatenate([skip[0], skip[1][:, 0:64]], axis=1))
            at = (k * MID + start) * EXT + (17 if side else 0)
            put_res(p, pl.ds(at, count, stride=EXT), keep(inside, value))

    def shift_result(p, jm):
        for k in range(2):
            slab = k * MID + jm
            for r in range(2):
                rows = slice(slab * EXT + r, slab * EXT + r + ROWS)
                res_d[p][r, slab * ROWS : (slab + 1) * ROWS, :] = pair_of(res[p], rows, slice(None))

    def gather_result(p, place):
        r, c = divmod(place, 2)
        for k in range(2):
            rows = pl.ds((k * MID + c) * EXT + ROWS + r, 16, stride=EXT)
            res_h[p][place, k * 16 : (k + 1) * 16, :] = pair_of(res[p], rows, slice(None))

    def result_steps(p, runs):
        for start, count in runs:
            for side in range(2):
                yield lambda side=side, start=start, count=count: result_rows(p, side, start, count)
            for jm in range(start, start + count):
                yield lambda jm=jm: (result_column(p, jm), shift_result(p, jm))

    def gather_steps(p):
        for place in range(4):
            yield lambda place=place: gather_result(p, place)

    span = COLS + 1
    total = [[None, None], [None, None]]

    def conv_up(p, k):
        pieces = []
        for r in range(2):
            for c in range(2):
                at = (k * MID + c) * ROWS
                own = res_d[p][r, at : at + span * ROWS, :]
                last = res_h[p][2 * r + c, k * 16 : (k + 1) * 16, :]
                pieces.append(jnp.concatenate([own, last], axis=0))
        total[p][k] = nt_dot(jnp.concatenate(pieces, axis=1), wu_ref[...])

    def conv_up_steps(p):
        for k in range(2):
            yield lambda k=k: conv_up(p, k)

    def padded(name):
        return jnp.concatenate([refs[name][...], jnp.zeros((1, 32), F32)], axis=1)

    bias_up = padded("bu") if "bu" in refs else None
    g4 = padded("g4") if "g4" in refs else None

    def act_four(value):
        square = jnp.sum(value * value, axis=1, keepdims=True)
        return silu(value * lax.rsqrt(square * (1.0 / C4) + EPSILON) * g4)

    def fine_rows(p, a, b, k):
        at = span * ROWS
        lanes = slice((2 * a + b) * 128, (2 * a + b + 1) * 128)
        value = rounded(total[p][k][at : at + span, lanes] + bias_up)
        ext = FROWS if a else FROWS + 1
        rows = pl.ds((0 if b else FEXT) + ext, span, stride=2 * FEXT)
        if a:
            s4[p][k, rows, :] = value
        value = act_four(value)
        index = lax.broadcasted_iota(jnp.int32, (span, 1), 0)
        if b:
            inside = jnp.logical_or(index > 0, jnp.logical_not(first_col))
        else:
            inside = jnp.logical_or(index < span - 1, jnp.logical_not(last_col))
        if not a:
            inside = jnp.logical_and(inside, jnp.logical_not(last_row))
        z4[p + 1][k, rows, :] = keep(inside, value)

    top = lax.broadcasted_iota(jnp.int32, (ROWS, 1), 0) > 0
    rows_in = jnp.logical_or(top, jnp.logical_not(first_row))

    def fine_column(p, b, j):
        fx = 2 * j if b else 2 * j + 1
        for k in range(2):
            for a in range(2):
                lanes = slice((2 * a + b) * 128, (2 * a + b + 1) * 128)
                value = rounded(total[p][k][j * ROWS : (j + 1) * ROWS, lanes] + bias_up)
                rows = pl.ds(fx * FEXT + 1 - a, ROWS, stride=2)
                if 1 <= fx <= 2 * COLS:
                    s4[p][k, rows, :] = value
                value = act_four(value)
                if a:
                    value = keep(rows_in, value)
                if fx == 0:
                    value = keep(jnp.logical_not(first_col), value)
                if fx == FINE - 1:
                    value = keep(jnp.logical_not(last_col), value)
                z4[p + 1][k, rows, :] = value
        shift_fine(p + 1, fx)

    def shift_fine(group, fx):
        for dy in range(3):
            rows = slice(fx * FEXT + dy, fx * FEXT + dy + FROWS)
            act4_d[group][dy, fx * FROWS : (fx + 1) * FROWS, :] = pair_of(z4[group], rows, slice(None))

    def fine_steps(p):
        for a in range(2):
            for b in range(2):
                for k in range(2):
                    yield lambda a=a, b=b, k=k: fine_rows(p, a, b, k)
        for j in range(span):
            for b in (1, 0):
                yield lambda b=b, j=j: fine_column(p, b, j)

    def put_cached(fx, row0, joined, first):
        rows = joined.shape[0]
        for t in range(2):
            at = first + t * C4
            value = jnp.concatenate([joined[:, at : at + C4], jnp.zeros((rows, 32), F32)], axis=1)
            z4[0][t, fx * FEXT + row0 : fx * FEXT + row0 + rows, :] = value

    def cached_column(fx):
        if 0 < fx < FINE - 1:
            at = (fx - 1) * COLQ
            start = at // 128 * 128
            first = at - start
            strip = slice(XW + PW + start, XW + PW + start + 256)
            put_cached(fx, 1, wide(q_ref[:, start : start + 256]), first)
            put_cached(fx, 0, above(strip)[1:2], first)
            put_cached(fx, FROWS + 1, below(strip)[0:1], first)
        else:
            lanes = (right if fx else left)(slice(QAT, QAT + 384))
            put_cached(fx, 0, lanes[17:18], 0)
            put_cached(fx, 1, lanes[0:16], 0)
            put_cached(fx, 1 + ROWS, lanes[0:16], COLQ)
            put_cached(fx, FROWS + 1, lanes[18:19], 0)
        shift_fine(0, fx)

    def cached_steps():
        for fx in range(FINE):
            yield lambda fx=fx: cached_column(fx)

    size = COLS * FROWS
    done = [[None, None], [None, None]]

    def conv_four(p, half):
        pieces = []
        for dy in range(3):
            for dx in range(3):
                at = (dx + half * COLS) * FROWS
                pieces += [act4_d[group][dy, at : at + size, :] for group in (p, p + 1)]
        kernel = jnp.concatenate([w4_ref[dy] for dy in range(3)], axis=1)
        done[p][half] = nt_dot(jnp.concatenate(pieces, axis=1), kernel)

    def conv_four_steps(p):
        for half in range(2):
            yield lambda half=half: conv_four(p, half)

    bias_four = jnp.concatenate([refs["b4"][...]] * 2, axis=1) if "b4" in refs else None
    first = lane_mask(FROWS, C4)

    def out_column(p, fx):
        rows = slice((fx + 1) * FEXT + 1, (fx + 1) * FEXT + 1 + FROWS)
        other = pltpu.roll(s4[p][1, rows, :], C4, 1)
        skip = jnp.concatenate([jnp.where(first, s4[p][0, rows, :], other), other[:, 0:64]], axis=1)
        at = fx % COLS * FROWS
        value = (done[p][fx // COLS][at : at + FROWS] + bias_four + skip).astype(BF16)
        out_ref[:, fx * 384 + p * 192 : fx * 384 + (p + 1) * 192] = value

    def out_steps(p):
        for fx in range(2 * COLS):
            yield lambda fx=fx: out_column(p, fx)

    return types.SimpleNamespace(**locals())


OWN = range(2, WIDE - 2)


def first_inner_kernel(names, sizes, *all_refs):
    refs = dict(zip(names, all_refs))
    col = lax.axis_index("section") * sizes[2] + lax.axis_index("col")

    @pl.when(col == sizes[1] // 2)
    def _():
        do = stages(refs, *sizes)
        weave(do.coarse_steps(0, OWN), do.coarse_steps(1, OWN))


def inner_kernel(names, sizes, *all_refs):
    refs = dict(zip(names, all_refs))
    col = lax.axis_index("section") * sizes[2] + lax.axis_index("col")

    @pl.when(col != sizes[1] // 2)
    def _():
        do = stages(refs, *sizes)
        weave(do.coarse_steps(0, OWN), do.coarse_steps(1, OWN))

    do = stages(refs, *sizes)
    weave(do.row_steps(0), do.row_steps(1))
    weave(do.conv_three_steps([INNER], [(0, 0), (0, 1)]), do.coarse_steps(2, OWN))
    weave(do.row_steps(2))
    weave(do.conv_three_steps([INNER], [(1, 0), (1, 1)]), do.result_steps(0, [INNER]))
    weave(do.result_steps(1, [INNER]))


def main_kernel(names, sizes, *all_refs):
    do = stages(dict(zip(names, all_refs)), *sizes)
    sides = (0, 1, WIDE - 2, WIDE - 1)
    weave(*[do.coarse_steps(group, sides) for group in range(3)])
    weave(*[do.row_steps(group) for group in range(3)])
    weave(do.conv_three_steps(RIMS, [(0, 0), (0, 1)], [(1, 0), (1, 1)]), do.cached_steps())
    weave(do.result_steps(0, RIMS))
    weave(do.gather_steps(0))
    weave(do.conv_up_steps(0), do.result_steps(1, RIMS))
    weave(do.gather_steps(1))
    weave(do.conv_up_steps(1), do.fine_steps(0))
    weave(do.conv_four_steps(0), do.fine_steps(1))
    later = list(do.conv_four_steps(1))
    ends = list(do.out_steps(1))
    weave(later[:1], do.out_steps(0))
    weave(later[1:], ends[:10])
    weave(ends[10:])


def split_pairs(flat_ref, parts, pairs, taps, stride):
    low = lane_mask(taps, 64)
    zero = jnp.zeros((taps, 128), F32)
    for pair in pairs:
        v0, v1, v2 = [flat_ref[:, (3 * pair + q) * 128 : (3 * pair + q + 1) * 128].astype(F32) for q in range(3)]
        r1, r2 = pltpu.roll(v1, 64, 1), pltpu.roll(v2, 64, 1)
        at = 2 * pair * stride
        parts[0, at : at + taps, :] = v0
        parts[1, at : at + taps, :] = jnp.where(low, v1, zero)
        parts[0, at + stride : at + stride + taps, :] = jnp.where(low, r1, r2)
        parts[1, at + stride : at + stride + taps, :] = jnp.where(low, r2, zero)


def prep_three_kernel(flat_ref, out_ref, parts):
    split_pairs(flat_ref, parts, range(C3 // 2), 27, 40)
    for tap in range(27):
        both = [parts[q, pl.ds(tap, C3, stride=40), :] for q in range(2)]
        t, place = divmod(tap, 9)
        out_ref[place, :, t * 256 : (t + 1) * 256] = jnp.concatenate(both, axis=1).astype(BF16)


def prep_four_kernel(up_ref, four_ref, up_out, four_out, parts_u, parts_f):
    split_pairs(up_ref, parts_u, range(C4 // 2), 9, 24)
    taps = {}
    for tap in range(9):
        for q in range(2):
            taps[tap, q] = parts_u[q, pl.ds(tap, C4, stride=24), :]
    spans = {(0, 0): (0,), (0, 1): (1, 2), (1, 0): (0, 1), (1, 1): (2,)}
    rest = jnp.zeros((32, 256), BF16)
    for a in range(2):
        for b in range(2):
            at = (2 * a + b) * 128
            for r in range(2):
                for c in range(2):
                    tiles = []
                    for q in range(2):
                        total = None
                        for dy in spans[a, r]:
                            for dx in spans[b, c]:
                                one = taps[3 * dy + dx, q]
                                total = one if total is None else total + one
                        tiles.append(total)
                    lanes = slice((2 * r + c) * 256, (2 * r + c + 1) * 256)
                    up_out[at : at + C4, lanes] = jnp.concatenate(tiles, axis=1).astype(BF16)
                    up_out[at + C4 : at + 128, lanes] = rest
    lane = lax.broadcasted_iota(jnp.int32, (27, 128), 1)
    empty = jnp.zeros((27, 128), F32)
    for four in range(C4 // 4):
        at = 3 * four * 128
        v0, v1, v2 = [four_ref[:, at + q * 128 : at + (q + 1) * 128].astype(F32) for q in range(3)]
        second = jnp.where(lane < 32, pltpu.roll(v0, 32, 1), pltpu.roll(v1, 32, 1))
        third = jnp.where(lane < 64, pltpu.roll(v1, 64, 1), pltpu.roll(v2, 64, 1))
        for m, value in enumerate((v0, second, third, pltpu.roll(v2, 96, 1))):
            at = (4 * four + m) * 40
            parts_f[at : at + 27, :] = jnp.where(lane < C4, value, empty)
    none = jnp.zeros((C4, 128), BF16)
    for place in range(9):
        dy, dx = divmod(place, 3)
        at = dx * 512
        four_out[dy, 0:C4, at + 384 : at + 512] = none
        four_out[dy, C4 : 2 * C4, at : at + 128] = none
        for t in range(3):
            kernel = parts_f[pl.ds(9 * t + place, C4, stride=40), :].astype(BF16)
            four_out[dy, 0:C4, at + t * 128 : at + (t + 1) * 128] = kernel
            four_out[dy, C4 : 2 * C4, at + (t + 1) * 128 : at + (t + 2) * 128] = kernel


def row_strips(refs, low_flag, out_ref):
    at = 0
    for ref in refs:
        rows, width = ref.shape
        out_ref[:, at : at + width] = jnp.where(low_flag, ref[0:2, :], ref[rows - 2 : rows, :])
        at += width


def row_strips_kernel(x_ref, p_ref, q_ref, even_ref, odd_ref, x_own, p_own, q_own, sems):
    own = (x_own, p_own, q_own)
    copies = [
        pltpu.make_async_copy(source, target, sems.at[n])
        for n, (source, target) in enumerate(zip((x_ref, p_ref, q_ref), own))
    ]
    for copy in copies:
        copy.start()
    for copy in copies:
        copy.wait()
    row_odd = lax.rem(lax.axis_index("row"), 2) == 1
    row_strips(own, row_odd, even_ref)
    row_strips(own, jnp.logical_not(row_odd), odd_ref)


def col_strips_kernel(x_ref, p_ref, q_ref, odd_row, even_row, _, out_ref, *, col_size, parity):
    row_odd = lax.rem(lax.axis_index("row"), 2) == 1
    col = lax.axis_index("section") * col_size + lax.axis_index("col")
    take_low = lax.rem(col, 2) == parity
    strips = (
        jnp.where(row_odd, even_row[...], odd_row[...]),
        jnp.where(row_odd, odd_row[...], even_row[...]),
    )

    def put(rows, at, low, high):
        out_ref[rows, at : at + low.shape[1]] = jnp.where(take_low, low, high)

    start = 0
    for ref, at, width, lanes in (
        (x_ref, 0, XW, 2 * COLX), (p_ref, 2 * COLX, PW, 2 * COLP), (q_ref, QAT, QW, COLQ)
    ):
        high = width - lanes
        if ref is q_ref:
            for half in range(2):
                rows = slice(half * ROWS, (half + 1) * ROWS)
                put(slice(0, ROWS), at + half * lanes, ref[rows, 0:lanes], ref[rows, high:width])
        else:
            put(slice(0, ROWS), at, ref[:, 0:lanes], ref[:, high:width])
        for place, strip in enumerate(strips):
            rows = slice(ROWS + 2 * place, ROWS + 2 * place + 2)
            put(rows, at, strip[:, start : start + lanes], strip[:, start + high : start + width])
            if ref is q_ref:
                out_ref[rows, at + lanes : at + 2 * lanes] = jnp.zeros((2, lanes), BF16)
        start += width


def call(kernel, operands, outputs, scratch, megabytes, moved=0, unread=0, space=pl.ANY, aliases=None):
    cost = pl.CostEstimate(flops=moved, bytes_accessed=moved, transcendentals=0) if moved else None
    vmem = pl.BlockSpec(memory_space=pltpu.VMEM)
    shapes = [
        shape if isinstance(shape, jax.ShapeDtypeStruct) else jax.ShapeDtypeStruct(shape, BF16)
        for shape in outputs
    ]
    got = pl.pallas_call(
        kernel,
        out_shape=shapes,
        in_specs=[vmem] * (len(operands) - unread) + [pl.BlockSpec(memory_space=space)] * unread,
        out_specs=[vmem] * len(outputs),
        scratch_shapes=scratch,
        cost_estimate=cost,
        input_output_aliases=aliases or {},
        compiler_params=pltpu.CompilerParams(vmem_limit_bytes=megabytes * 1024 * 1024),
    )(*operands)
    return got[0] if len(outputs) == 1 else got


def swap_pairs(count, start):
    out = []
    for low in range(start, count - 1, 2):
        out += [(low, low + 1), (low + 1, low)]
    return out


def shards(
    section_input,
    cache_three,
    gain_three,
    bias_three,
    weight_three,
    weight_up,
    bias_up,
    cache_four,
    gain_four,
    weight_four,
    bias_four,
):
    row_count = lax.axis_size("row")
    col_size = lax.axis_size("col")
    col_count = lax.axis_size("section") * col_size
    tile = (section_input, cache_three, cache_four)

    row_strip = (2, XW + PW + QW)
    own = [pltpu.VMEM(block.shape, BF16) for block in tile]
    even_strip, odd_strip = call(
        row_strips_kernel,
        tile,
        [row_strip] * 2,
        [*own, pltpu.SemaphoreType.DMA((3,))],
        62, unread=3, space=pltpu.HBM,
    )
    even_row = lax.ppermute(even_strip, "row", swap_pairs(row_count, 0))
    odd_row = lax.ppermute(odd_strip, "row", swap_pairs(row_count, 1))

    w3 = call(
        prep_three_kernel,
        (weight_three,),
        [(9, C3, 3 * 256)],
        [pltpu.VMEM((2, 40 * C3, 128), F32)],
        16, 8_000_000,
    )
    col_strip = (ROWS + 4, QAT + 2 * COLQ)

    def swap_columns(parity, after):
        def col_kernel(*refs):
            col_strips_kernel(*refs, col_size=col_size, parity=1 - parity)

        strip = call(col_kernel, (*tile, odd_row, even_row, after), [col_strip], [], 4, unread=1)
        return lax.ppermute(strip, ("section", "col"), swap_pairs(col_count, parity))

    sizes = (row_count, col_count, col_size)
    rows = (section_input, cache_three, odd_row, even_row)
    params = (gain_three.reshape(1, C3), bias_three.reshape(1, C3), w3)
    names = ("x", "p", "odd_row", "even_row", "g3", "b3", "w3")

    def block(shape, dtype=F32):
        return jax.ShapeDtypeStruct(shape, dtype)

    raw = block((3, 16 * EXT, 128))
    act = block((2, (2 * WIDE + 4) * EXT, 128))
    act_d = block((3, 2 * WIDE * ROWS, 256), BF16)
    res = block((2, (2 * MID + 5) * EXT, 128))
    res_d = block((2, 2 * MID * ROWS, 256), BF16)
    first = [raw, act, act, act_d, act_d]
    rest = [raw, act, act_d, res, res, res_d, res_d]
    halo = pltpu.VMEM((18, 2 * 16, 256), BF16)
    inner_scratch = [pltpu.VMEM(raw.shape, F32), halo, halo, halo]
    scratch_names = ("raw0", "halo0", "halo1", "halo2")

    even_col = swap_columns(0, w3)
    *held, token = call(
        functools.partial(first_inner_kernel, (*names[:-2], *FIRST, "token", "raw0"), sizes),
        (*rows, *params[:1]),
        [*first, (16, 128)],
        inner_scratch[:1],
        8, 2_000_000,
    )
    odd_col = swap_columns(1, token)
    wu, w4 = call(
        prep_four_kernel,
        (weight_up, weight_four),
        [(4 * 128, 4 * 256), (3, 2 * C4, 3 * 512)],
        [
            pltpu.VMEM((2, 24 * C4, 128), F32),
            pltpu.VMEM((40 * C4, 128), F32),
        ],
        16, 8_000_000,
    )

    held = call(
        functools.partial(
            inner_kernel, (*names, *["_" + name for name in FIRST], *SHARED, *scratch_names), sizes
        ),
        (*rows, *params, *held),
        [*first, *rest],
        inner_scratch,
        16, 8_000_000,
        aliases={len(names) + n: n for n in range(len(first))},
    )

    operands = (
        *tile, odd_row, even_row, even_col, odd_col,
        *params, wu, bias_up.reshape(1, C4), gain_four.reshape(1, C4), w4, bias_four.reshape(1, C4),
    )
    names = (
        "x", "p", "q", "odd_row", "even_row", "even_col", "odd_col",
        "g3", "b3", "w3", "wu", "bu", "g4", "w4", "b4",
    )
    scratch = list(inner_scratch)
    scratch += [pltpu.VMEM((4, 2 * 16, 256), BF16)] * 2
    scratch += [pltpu.VMEM((2, FINE * FEXT, 128), F32)] * 3
    scratch += [pltpu.VMEM((2, FINE * FEXT, 128), F32)] * 2
    scratch += [pltpu.VMEM((3, FINE * FROWS, 256), BF16)] * 3
    scratch_names += ("resh0", "resh1", "z0", "z1", "z2", "s0", "s1", "fine0", "fine1", "fine2")
    got = call(
        functools.partial(
            main_kernel, (*names, *["_" + name for name in SHARED], "out", *SHARED, *scratch_names), sizes
        ),
        (*operands, *held),
        [(FROWS, 2 * COLS * FRAMES * C4), *first, *rest],
        scratch,
        24,
        aliases={len(names) + n: n + 1 for n in range(len(SHARED))},
    )
    return got[0]


def solution(mesh):
    tiled = P("row", ("section", "col"))
    return jax.shard_map(
        shards,
        mesh=mesh,
        in_specs=(tiled, tiled, P(), P(), P(), P(), P(), tiled, P(), P(), P()),
        out_specs=tiled,
        check_vma=False,
    )
```

```python
import functools
import types

import jax
import jax.numpy as jnp
from jax import lax
from jax.experimental import pallas as pl
from jax.experimental.pallas import tpu as pltpu
from jax.sharding import PartitionSpec as P

EPSILON = 1e-06
BF16 = jnp.bfloat16
F32 = jnp.float32

ROWS = 16
COLS = 10
C3 = 192
C4 = 96
FRAMES = 4
WIDE = COLS + 4
MID = COLS + 2
EXT = 24
FINE = 2 * COLS + 2
FROWS = 2 * ROWS
FEXT = 40
XW = COLS * FRAMES * C3
PW = COLS * 2 * C3
QW = 2 * COLS * 2 * C4
COLX = FRAMES * C3
COLP = 2 * C3
COLQ = 2 * C4
QAT = 2 * COLX + 2 * COLP


def nt_dot(lhs, rhs):
    return lax.dot_general(lhs, rhs, (((1,), (1,)), ((), ())), preferred_element_type=F32)


def silu(value):
    half = 0.5 * value
    return half + half * jnp.tanh(half)


def lane_mask(rows, below):
    return lax.broadcasted_iota(jnp.int32, (rows, 128), 1) < below


def split_pair(v0, v1, v2):
    low = lane_mask(v0.shape[0], 64)
    r1 = pltpu.roll(v1, 64, 1)
    r2 = pltpu.roll(v2, 64, 1)
    zero = jnp.zeros_like(v1)
    return (v0, jnp.where(low, v1, zero)), (jnp.where(low, r1, r2), jnp.where(low, r2, zero))


def norm_pair(v0, v1, v2, gains):
    low = lane_mask(v0.shape[0], 64)
    sq1 = v1 * v1
    zero = jnp.zeros_like(v1)
    sum_a = jnp.sum(v0 * v0 + jnp.where(low, sq1, zero), axis=1, keepdims=True)
    sum_b = jnp.sum(v2 * v2 + jnp.where(low, zero, sq1), axis=1, keepdims=True)
    inv_a = lax.rsqrt(sum_a * (1.0 / C3) + EPSILON)
    inv_b = lax.rsqrt(sum_b * (1.0 / C3) + EPSILON)
    return (
        silu(v0 * inv_a * gains[0]),
        silu(v1 * jnp.where(low, inv_a, inv_b) * gains[1]),
        silu(v2 * inv_b * gains[2]),
    )


def weave(*streams):
    lists = []
    for stream in streams:
        lists.append(list(stream))
    order = []
    for place, steps in enumerate(lists):
        order += [((n + 0.5) / len(steps), place, step) for n, step in enumerate(steps)]
    for _, _, step in sorted(order, key=lambda entry: entry[:2]):
        step()


FIRST = ("raw1", "act0", "act1", "actd0", "actd1")
SHARED = (*FIRST, "raw2", "act2", "actd2", "res0", "res1", "resd0", "resd1")
INNER = (2, COLS - 2)
RIMS = ((0, 2), (COLS, 2))
RIM_SLOTS = (0, 1, 2, 3, WIDE - 4, WIDE - 3, WIDE - 2, WIDE - 1)


def stages(refs, row_count, col_count, col_size):
    x_ref, p_ref, q_ref = refs.get("x"), refs.get("p"), refs.get("q")
    odd_row, even_row = refs.get("odd_row"), refs.get("even_row")
    even_col, odd_col = refs.get("even_col"), refs.get("odd_col")
    w3_ref, wu_ref, w4_ref = refs.get("w3"), refs.get("wu"), refs.get("w4")
    out_ref = refs.get("out")

    def several(name, count):
        return [refs.get(name + str(n)) for n in range(count)]

    raw, act, act_d, halo_d = several("raw", 3), several("act", 3), several("actd", 3), several("halo", 3)
    rims = several("rim", 3)
    res, res_d, res_h = several("res", 2), several("resd", 2), several("resh", 2)
    z4, s4, act4_d = several("z", 3), several("s", 2), several("fine", 3)
    row = lax.axis_index("row")
    col = lax.axis_index("section") * col_size + lax.axis_index("col")
    row_odd = lax.rem(row, 2) == 1
    col_odd = lax.rem(col, 2) == 1
    first_row, last_row = row == 0, row == row_count - 1
    first_col, last_col = col == 0, col == col_count - 1

    def wide(value):
        return value.astype(F32)

    def pick(flag, one, other, *index):
        return wide(jnp.where(flag, one[index], other[index]))

    def above(lanes):
        return pick(row_odd, even_row, odd_row, slice(0, 2), lanes)

    def below(lanes):
        return pick(row_odd, odd_row, even_row, slice(0, 2), lanes)

    def left(lanes):
        return pick(col_odd, even_col, odd_col, slice(0, ROWS + 4), lanes)

    def right(lanes):
        return pick(col_odd, odd_col, even_col, slice(0, ROWS + 4), lanes)

    def keep(inside, value):
        return jnp.where(inside, value, jnp.zeros_like(value))

    def rounded(value):
        return value.astype(BF16).astype(F32)

    def pair_of(ref, *index):
        return jnp.concatenate([ref[(0,) + index], ref[(1,) + index]], axis=1).astype(BF16)

    g3 = refs["g3"][...]
    gains = (
        g3[:, 0:128],
        jnp.concatenate([g3[:, 128:192], g3[:, 0:64]], axis=1),
        g3[:, 64:192],
    )

    def place_of(jj, rim):
        if rim:
            return rims, len(RIM_SLOTS), RIM_SLOTS.index(jj)
        return act, WIDE, jj

    def load_column(group, jj, rim):
        held, slots, slot = place_of(jj, rim)
        base = jj * EXT
        for q in range(3):
            if 2 <= jj < WIDE - 2:
                at = (jj - 2) * COLX + (3 * (group - 1) + q) * 128
                if group == 0:
                    at = (jj - 2) * COLP + q * 128
                src, strip_at = (x_ref, at) if group else (p_ref, XW + at)
                strip = slice(strip_at, strip_at + 128)
                raw[group][q, base : base + 16, :] = wide(src[:, at : at + 128])
                raw[group][q, base + 16 : base + 18, :] = above(strip)
                raw[group][q, base + 18 : base + 20, :] = below(strip)
            else:
                side, lane = (left, jj) if jj < 2 else (right, jj - WIDE + 2)
                at = lane * COLX + (3 * (group - 1) + q) * 128
                if group == 0:
                    at = 2 * COLX + lane * COLP + q * 128
                raw[group][q, base : base + 20, :] = side(slice(at, at + 128))
        tiles = [raw[group][q, base : base + EXT, :] for q in range(3)]
        if group:
            tiles = norm_pair(*tiles, gains)
        for half, pair in enumerate(split_pair(*tiles)):
            at = (half * slots + slot) * EXT
            for q in range(2):
                held[group][q, at : at + 2, :] = pair[q][16:18]
                held[group][q, at + 2 : at + 18, :] = pair[q][0:16]
                held[group][q, at + 18 : at + 20, :] = pair[q][18:20]

    def copy_column(group, jj):
        slot = RIM_SLOTS.index(jj)
        for half in range(2):
            source, target = (half * WIDE + jj) * EXT, (half * len(RIM_SLOTS) + slot) * EXT
            for q in range(2):
                rims[group][q, target : target + EXT, :] = act[group][q, source : source + EXT, :]

    def shift_column(group, jj, rim):
        held, slots, slot = place_of(jj, rim)
        for half in range(2):
            slab = half * WIDE + jj
            for dy in range(3):
                at = (half * slots + slot) * EXT + 1 + dy
                both = pair_of(held[group], slice(at, at + ROWS), slice(None))
                act_d[group][dy, slab * ROWS : (slab + 1) * ROWS, :] = both

    def gather_rows(group, dx, dy, rim):
        held, slots, start = (rims, len(RIM_SLOTS), 0) if rim else (act, WIDE, INNER[0])
        for half in range(2):
            at = (half * slots + start + dx) * EXT + dy
            tiles = []
            for q in range(2):
                sides = [held[group][q, pl.ds(at + skip, 8, stride=EXT), :] for skip in (0, 17)]
                tiles.append(jnp.concatenate(sides, axis=0))
            both = jnp.concatenate(tiles, axis=1).astype(BF16)
            halo_d[group][3 * dx + dy, half * 16 : (half + 1) * 16, :] = both

    def coarse_steps(group, columns, rim=False):
        for jj in columns:
            yield lambda jj=jj: (load_column(group, jj, rim), shift_column(group, jj, rim))

    def copy_steps(group):
        for jj in RIM_SLOTS[2:6]:
            yield lambda jj=jj: copy_column(group, jj)

    def row_steps(group, rim=False):
        for dx in range(3):
            for dy in range(3):
                yield lambda dx=dx, dy=dy: gather_rows(group, dx, dy, rim)

    center = {}
    edges = {}

    def conv_three(frames, runs):
        kernels = []
        pieces = []
        for dy in range(3):
            for dx in range(3):
                kernels.append(w3_ref[3 * dy + dx])
                for t in range(3):
                    parts = []
                    for p, k in frames:
                        group, half = p + (k + t) // 2, (k + t) % 2
                        for start, count in runs:
                            at = (half * WIDE + start + dx) * ROWS
                            parts.append(act_d[group][dy, at : at + count * ROWS, :])
                        parts.append(halo_d[group][3 * dx + dy, half * 16 : (half + 1) * 16, :])
                    pieces.append(jnp.concatenate(parts, axis=0))
        got = nt_dot(jnp.concatenate(pieces, axis=1), jnp.concatenate(kernels, axis=1))
        at = 0
        for p, k in frames:
            for start, count in runs:
                for jm in range(start, start + count):
                    center[p, k, jm] = got[at : at + ROWS]
                    at += ROWS
            edges[p, k] = got[at : at + 16]
            at += 16

    def conv_three_steps(runs, *batches):
        for frames in batches:
            yield lambda frames=frames: conv_three(frames, runs)

    b3 = refs["b3"][...] if "b3" in refs else None

    def put_res(p, rows, value):
        res[p][0, rows, :] = value[:, 0:128]
        rest = jnp.zeros((value.shape[0], 64), F32)
        res[p][1, rows, :] = jnp.concatenate([value[:, 128:192], rest], axis=1)

    def result_column(p, jm):
        at = (jm + 1) * EXT
        tiles = [raw[p + 1][q, at : at + ROWS, :] for q in range(3)]
        for k, skip in enumerate(split_pair(*tiles)):
            slab = k * MID + jm
            value = center[p, k, jm] + b3
            value = rounded(value + jnp.concatenate([skip[0], skip[1][:, 0:64]], axis=1))
            if jm == 0:
                value = keep(jnp.logical_not(first_col), value)
            if jm == MID - 1:
                value = keep(jnp.logical_not(last_col), value)
            put_res(p, pl.ds(slab * EXT + 1, ROWS), value)

    def result_rows(p, side, start, count):
        inside = jnp.logical_not(last_row if side else first_row)
        column = lax.broadcasted_iota(jnp.int32, (count, 1), 0) + start
        if start == 0:
            inside = jnp.logical_and(inside, jnp.logical_or(column > 0, jnp.logical_not(first_col)))
        if start + count == MID:
            inside = jnp.logical_and(inside, jnp.logical_or(column < MID - 1, jnp.logical_not(last_col)))
        rows = pl.ds((start + 1) * EXT + (18 if side else 17), count, stride=EXT)
        tiles = [raw[p + 1][q, rows, :] for q in range(3)]
        for k, skip in enumerate(split_pair(*tiles)):
            at = 8 * side + (4 if start == COLS else 0)
            value = edges[p, k][at : at + count] + b3
            value = rounded(value + jnp.concatenate([skip[0], skip[1][:, 0:64]], axis=1))
            at = (k * MID + start) * EXT + (17 if side else 0)
            put_res(p, pl.ds(at, count, stride=EXT), keep(inside, value))

    def shift_result(p, jm):
        for k in range(2):
            slab = k * MID + jm
            for r in range(2):
                rows = slice(slab * EXT + r, slab * EXT + r + ROWS)
                res_d[p][r, slab * ROWS : (slab + 1) * ROWS, :] = pair_of(res[p], rows, slice(None))

    def gather_result(p, place):
        r, c = divmod(place, 2)
        for k in range(2):
            rows = pl.ds((k * MID + c) * EXT + ROWS + r, 16, stride=EXT)
            res_h[p][place, k * 16 : (k + 1) * 16, :] = pair_of(res[p], rows, slice(None))

    def result_steps(p, runs):
        for start, count in runs:
            for side in range(2):
                yield lambda side=side, start=start, count=count: result_rows(p, side, start, count)
            for jm in range(start, start + count):
                yield lambda jm=jm: (result_column(p, jm), shift_result(p, jm))

    def gather_steps(p):
        for place in range(4):
            yield lambda place=place: gather_result(p, place)

    span = COLS + 1
    total = [[None, None], [None, None]]

    def conv_up(p, k):
        pieces = []
        for r in range(2):
            for c in range(2):
                at = (k * MID + c) * ROWS
                own = res_d[p][r, at : at + span * ROWS, :]
                last = res_h[p][2 * r + c, k * 16 : (k + 1) * 16, :]
                pieces.append(jnp.concatenate([own, last], axis=0))
        total[p][k] = nt_dot(jnp.concatenate(pieces, axis=1), wu_ref[...])

    def conv_up_steps(p):
        for k in range(2):
            yield lambda k=k: conv_up(p, k)

    def padded(name):
        return jnp.concatenate([refs[name][...], jnp.zeros((1, 32), F32)], axis=1)

    bias_up = padded("bu") if "bu" in refs else None
    g4 = padded("g4") if "g4" in refs else None

    def act_four(value):
        square = jnp.sum(value * value, axis=1, keepdims=True)
        return silu(value * lax.rsqrt(square * (1.0 / C4) + EPSILON) * g4)

    def fine_rows(p, a, b, k):
        at = span * ROWS
        lanes = slice((2 * a + b) * 128, (2 * a + b + 1) * 128)
        value = rounded(total[p][k][at : at + span, lanes] + bias_up)
        ext = FROWS if a else FROWS + 1
        rows = pl.ds((0 if b else FEXT) + ext, span, stride=2 * FEXT)
        if a:
            s4[p][k, rows, :] = value
        value = act_four(value)
        index = lax.broadcasted_iota(jnp.int32, (span, 1), 0)
        if b:
            inside = jnp.logical_or(index > 0, jnp.logical_not(first_col))
        else:
            inside = jnp.logical_or(index < span - 1, jnp.logical_not(last_col))
        if not a:
            inside = jnp.logical_and(inside, jnp.logical_not(last_row))
        z4[p + 1][k, rows, :] = keep(inside, value)

    top = lax.broadcasted_iota(jnp.int32, (ROWS, 1), 0) > 0
    rows_in = jnp.logical_or(top, jnp.logical_not(first_row))

    def fine_column(p, b, j):
        fx = 2 * j if b else 2 * j + 1
        for k in range(2):
            for a in range(2):
                lanes = slice((2 * a + b) * 128, (2 * a + b + 1) * 128)
                value = rounded(total[p][k][j * ROWS : (j + 1) * ROWS, lanes] + bias_up)
                rows = pl.ds(fx * FEXT + 1 - a, ROWS, stride=2)
                if 1 <= fx <= 2 * COLS:
                    s4[p][k, rows, :] = value
                value = act_four(value)
                if a:
                    value = keep(rows_in, value)
                if fx == 0:
                    value = keep(jnp.logical_not(first_col), value)
                if fx == FINE - 1:
                    value = keep(jnp.logical_not(last_col), value)
                z4[p + 1][k, rows, :] = value
        shift_fine(p + 1, fx)

    def shift_fine(group, fx):
        for dy in range(3):
            rows = slice(fx * FEXT + dy, fx * FEXT + dy + FROWS)
            act4_d[group][dy, fx * FROWS : (fx + 1) * FROWS, :] = pair_of(z4[group], rows, slice(None))

    def fine_steps(p):
        for a in range(2):
            for b in range(2):
                for k in range(2):
                    yield lambda a=a, b=b, k=k: fine_rows(p, a, b, k)
        for j in range(span):
            for b in (1, 0):
                yield lambda b=b, j=j: fine_column(p, b, j)

    def put_cached(fx, row0, joined, first):
        rows = joined.shape[0]
        for t in range(2):
            at = first + t * C4
            value = jnp.concatenate([joined[:, at : at + C4], jnp.zeros((rows, 32), F32)], axis=1)
            z4[0][t, fx * FEXT + row0 : fx * FEXT + row0 + rows, :] = value

    def cached_column(fx):
        if 0 < fx < FINE - 1:
            at = (fx - 1) * COLQ
            start = at // 128 * 128
            first = at - start
            strip = slice(XW + PW + start, XW + PW + start + 256)
            put_cached(fx, 1, wide(q_ref[:, start : start + 256]), first)
            put_cached(fx, 0, above(strip)[1:2], first)
            put_cached(fx, FROWS + 1, below(strip)[0:1], first)
        else:
            lanes = (right if fx else left)(slice(QAT, QAT + 384))
            put_cached(fx, 0, lanes[17:18], 0)
            put_cached(fx, 1, lanes[0:16], 0)
            put_cached(fx, 1 + ROWS, lanes[0:16], COLQ)
            put_cached(fx, FROWS + 1, lanes[18:19], 0)
        shift_fine(0, fx)

    def cached_steps():
        for fx in range(FINE):
            yield lambda fx=fx: cached_column(fx)

    size = COLS * FROWS
    done = [[None, None], [None, None]]

    def conv_four(p, half):
        pieces = []
        for dy in range(3):
            for dx in range(3):
                at = (dx + half * COLS) * FROWS
                pieces += [act4_d[group][dy, at : at + size, :] for group in (p, p + 1)]
        kernel = jnp.concatenate([w4_ref[dy] for dy in range(3)], axis=1)
        done[p][half] = nt_dot(jnp.concatenate(pieces, axis=1), kernel)

    def conv_four_steps(p):
        for half in range(2):
            yield lambda half=half: conv_four(p, half)

    bias_four = jnp.concatenate([refs["b4"][...]] * 2, axis=1) if "b4" in refs else None
    first = lane_mask(FROWS, C4)

    def out_column(p, fx):
        rows = slice((fx + 1) * FEXT + 1, (fx + 1) * FEXT + 1 + FROWS)
        other = pltpu.roll(s4[p][1, rows, :], C4, 1)
        skip = jnp.concatenate([jnp.where(first, s4[p][0, rows, :], other), other[:, 0:64]], axis=1)
        at = fx % COLS * FROWS
        value = (done[p][fx // COLS][at : at + FROWS] + bias_four + skip).astype(BF16)
        out_ref[:, fx * 384 + p * 192 : fx * 384 + (p + 1) * 192] = value

    def out_steps(p):
        for fx in range(2 * COLS):
            yield lambda fx=fx: out_column(p, fx)

    return types.SimpleNamespace(**locals())


OWN = range(2, WIDE - 2)


def first_inner_kernel(names, sizes, *all_refs):
    refs = dict(zip(names, all_refs))
    col = lax.axis_index("section") * sizes[2] + lax.axis_index("col")

    @pl.when(col == sizes[1] // 2)
    def _():
        do = stages(refs, *sizes)
        weave(do.coarse_steps(0, OWN), do.coarse_steps(1, OWN))


def inner_kernel(names, sizes, *all_refs):
    refs = dict(zip(names, all_refs))
    col = lax.axis_index("section") * sizes[2] + lax.axis_index("col")

    @pl.when(col != sizes[1] // 2)
    def _():
        do = stages(refs, *sizes)
        weave(do.coarse_steps(0, OWN), do.coarse_steps(1, OWN))

    do = stages(refs, *sizes)
    weave(do.row_steps(0), do.row_steps(1))
    weave(do.conv_three_steps([INNER], [(0, 0), (0, 1)]), do.coarse_steps(2, OWN))
    weave(do.row_steps(2))
    weave(do.conv_three_steps([INNER], [(1, 0), (1, 1)]), do.result_steps(0, [INNER]))
    weave(do.result_steps(1, [INNER]))


def main_kernel(names, sizes, *all_refs):
    do = stages(dict(zip(names, all_refs)), *sizes)
    sides = (0, 1, WIDE - 2, WIDE - 1)
    weave(*[do.copy_steps(group) for group in range(3)])
    weave(*[do.coarse_steps(group, sides, True) for group in range(3)])
    weave(*[do.row_steps(group, True) for group in range(3)])
    weave(do.conv_three_steps(RIMS, [(0, 0), (0, 1)], [(1, 0), (1, 1)]), do.cached_steps())
    weave(do.result_steps(0, RIMS))
    weave(do.gather_steps(0))
    weave(do.result_steps(1, RIMS))
    weave(do.gather_steps(1))
    weave(do.conv_up_steps(0))
    weave(do.conv_up_steps(1))
    weave(do.fine_steps(0))
    weave(do.conv_four_steps(0), do.fine_steps(1))
    later = list(do.conv_four_steps(1))
    ends = list(do.out_steps(1))
    weave(later[:1], do.out_steps(0))
    weave(later[1:], ends[:10])
    weave(ends[10:])


def split_pairs(flat_ref, parts, pairs, taps, stride):
    low = lane_mask(taps, 64)
    zero = jnp.zeros((taps, 128), F32)
    for pair in pairs:
        v0, v1, v2 = [flat_ref[:, (3 * pair + q) * 128 : (3 * pair + q + 1) * 128].astype(F32) for q in range(3)]
        r1, r2 = pltpu.roll(v1, 64, 1), pltpu.roll(v2, 64, 1)
        at = 2 * pair * stride
        parts[0, at : at + taps, :] = v0
        parts[1, at : at + taps, :] = jnp.where(low, v1, zero)
        parts[0, at + stride : at + stride + taps, :] = jnp.where(low, r1, r2)
        parts[1, at + stride : at + stride + taps, :] = jnp.where(low, r2, zero)


def prep_three_kernel(flat_ref, out_ref, parts):
    split_pairs(flat_ref, parts, range(C3 // 2), 27, 40)
    for tap in range(27):
        both = [parts[q, pl.ds(tap, C3, stride=40), :] for q in range(2)]
        t, place = divmod(tap, 9)
        out_ref[place, :, t * 256 : (t + 1) * 256] = jnp.concatenate(both, axis=1).astype(BF16)


def prep_four_kernel(up_ref, four_ref, up_out, four_out, parts_u, parts_f):
    split_pairs(up_ref, parts_u, range(C4 // 2), 9, 24)
    taps = {}
    for tap in range(9):
        for q in range(2):
            taps[tap, q] = parts_u[q, pl.ds(tap, C4, stride=24), :]
    spans = {(0, 0): (0,), (0, 1): (1, 2), (1, 0): (0, 1), (1, 1): (2,)}
    rest = jnp.zeros((32, 256), BF16)
    for a in range(2):
        for b in range(2):
            at = (2 * a + b) * 128
            for r in range(2):
                for c in range(2):
                    tiles = []
                    for q in range(2):
                        total = None
                        for dy in spans[a, r]:
                            for dx in spans[b, c]:
                                one = taps[3 * dy + dx, q]
                                total = one if total is None else total + one
                        tiles.append(total)
                    lanes = slice((2 * r + c) * 256, (2 * r + c + 1) * 256)
                    up_out[at : at + C4, lanes] = jnp.concatenate(tiles, axis=1).astype(BF16)
                    up_out[at + C4 : at + 128, lanes] = rest
    lane = lax.broadcasted_iota(jnp.int32, (27, 128), 1)
    empty = jnp.zeros((27, 128), F32)
    for four in range(C4 // 4):
        at = 3 * four * 128
        v0, v1, v2 = [four_ref[:, at + q * 128 : at + (q + 1) * 128].astype(F32) for q in range(3)]
        second = jnp.where(lane < 32, pltpu.roll(v0, 32, 1), pltpu.roll(v1, 32, 1))
        third = jnp.where(lane < 64, pltpu.roll(v1, 64, 1), pltpu.roll(v2, 64, 1))
        for m, value in enumerate((v0, second, third, pltpu.roll(v2, 96, 1))):
            at = (4 * four + m) * 40
            parts_f[at : at + 27, :] = jnp.where(lane < C4, value, empty)
    none = jnp.zeros((C4, 128), BF16)
    for place in range(9):
        dy, dx = divmod(place, 3)
        at = dx * 512
        four_out[dy, 0:C4, at + 384 : at + 512] = none
        four_out[dy, C4 : 2 * C4, at : at + 128] = none
        for t in range(3):
            kernel = parts_f[pl.ds(9 * t + place, C4, stride=40), :].astype(BF16)
            four_out[dy, 0:C4, at + t * 128 : at + (t + 1) * 128] = kernel
            four_out[dy, C4 : 2 * C4, at + (t + 1) * 128 : at + (t + 2) * 128] = kernel


def row_strips(refs, low_flag, out_ref):
    at = 0
    for ref in refs:
        rows, width = ref.shape
        out_ref[:, at : at + width] = jnp.where(low_flag, ref[0:2, :], ref[rows - 2 : rows, :])
        at += width


def row_strips_kernel(x_ref, p_ref, q_ref, even_ref, odd_ref, x_own, p_own, q_own, sems):
    own = (x_own, p_own, q_own)
    copies = [
        pltpu.make_async_copy(source, target, sems.at[n])
        for n, (source, target) in enumerate(zip((x_ref, p_ref, q_ref), own))
    ]
    for copy in copies:
        copy.start()
    for copy in copies:
        copy.wait()
    row_odd = lax.rem(lax.axis_index("row"), 2) == 1
    row_strips(own, row_odd, even_ref)
    row_strips(own, jnp.logical_not(row_odd), odd_ref)


def col_strips_kernel(x_ref, p_ref, q_ref, odd_row, even_row, _, out_ref, *, col_size, parity):
    row_odd = lax.rem(lax.axis_index("row"), 2) == 1
    col = lax.axis_index("section") * col_size + lax.axis_index("col")
    take_low = lax.rem(col, 2) == parity
    strips = (
        jnp.where(row_odd, even_row[...], odd_row[...]),
        jnp.where(row_odd, odd_row[...], even_row[...]),
    )

    def put(rows, at, low, high):
        out_ref[rows, at : at + low.shape[1]] = jnp.where(take_low, low, high)

    start = 0
    for ref, at, width, lanes in (
        (x_ref, 0, XW, 2 * COLX), (p_ref, 2 * COLX, PW, 2 * COLP), (q_ref, QAT, QW, COLQ)
    ):
        high = width - lanes
        if ref is q_ref:
            for half in range(2):
                rows = slice(half * ROWS, (half + 1) * ROWS)
                put(slice(0, ROWS), at + half * lanes, ref[rows, 0:lanes], ref[rows, high:width])
        else:
            put(slice(0, ROWS), at, ref[:, 0:lanes], ref[:, high:width])
        for place, strip in enumerate(strips):
            rows = slice(ROWS + 2 * place, ROWS + 2 * place + 2)
            put(rows, at, strip[:, start : start + lanes], strip[:, start + high : start + width])
            if ref is q_ref:
                out_ref[rows, at + lanes : at + 2 * lanes] = jnp.zeros((2, lanes), BF16)
        start += width


def call(kernel, operands, outputs, scratch, megabytes, moved=0, unread=0, space=pl.ANY, aliases=None):
    cost = pl.CostEstimate(flops=moved, bytes_accessed=moved, transcendentals=0) if moved else None
    vmem = pl.BlockSpec(memory_space=pltpu.VMEM)
    shapes = [
        shape if isinstance(shape, jax.ShapeDtypeStruct) else jax.ShapeDtypeStruct(shape, BF16)
        for shape in outputs
    ]
    got = pl.pallas_call(
        kernel,
        out_shape=shapes,
        in_specs=[vmem] * (len(operands) - unread) + [pl.BlockSpec(memory_space=space)] * unread,
        out_specs=[vmem] * len(outputs),
        scratch_shapes=scratch,
        cost_estimate=cost,
        input_output_aliases=aliases or {},
        compiler_params=pltpu.CompilerParams(vmem_limit_bytes=megabytes * 1024 * 1024),
    )(*operands)
    return got[0] if len(outputs) == 1 else got


def swap_pairs(count, start):
    out = []
    for low in range(start, count - 1, 2):
        out += [(low, low + 1), (low + 1, low)]
    return out


def shards(
    section_input,
    cache_three,
    gain_three,
    bias_three,
    weight_three,
    weight_up,
    bias_up,
    cache_four,
    gain_four,
    weight_four,
    bias_four,
):
    row_count = lax.axis_size("row")
    col_size = lax.axis_size("col")
    col_count = lax.axis_size("section") * col_size
    tile = (section_input, cache_three, cache_four)

    row_strip = (2, XW + PW + QW)
    own = [pltpu.VMEM(block.shape, BF16) for block in tile]
    even_strip, odd_strip = call(
        row_strips_kernel,
        tile,
        [row_strip] * 2,
        [*own, pltpu.SemaphoreType.DMA((3,))],
        62, unread=3, space=pltpu.HBM,
    )
    even_row = lax.ppermute(even_strip, "row", swap_pairs(row_count, 0))
    odd_row = lax.ppermute(odd_strip, "row", swap_pairs(row_count, 1))

    w3 = call(
        prep_three_kernel,
        (weight_three,),
        [(9, C3, 3 * 256)],
        [pltpu.VMEM((2, 40 * C3, 128), F32)],
        16, 8_000_000,
    )
    col_strip = (ROWS + 4, QAT + 2 * COLQ)

    def swap_columns(parity, after):
        def col_kernel(*refs):
            col_strips_kernel(*refs, col_size=col_size, parity=1 - parity)

        strip = call(col_kernel, (*tile, odd_row, even_row, after), [col_strip], [], 4, unread=1)
        return lax.ppermute(strip, ("section", "col"), swap_pairs(col_count, parity))

    sizes = (row_count, col_count, col_size)
    rows = (section_input, cache_three, odd_row, even_row)
    params = (gain_three.reshape(1, C3), bias_three.reshape(1, C3), w3)
    names = ("x", "p", "odd_row", "even_row", "g3", "b3", "w3")

    def block(shape, dtype=F32):
        return jax.ShapeDtypeStruct(shape, dtype)

    raw = block((3, 16 * EXT, 128))
    act = block((2, (2 * WIDE + 4) * EXT, 128))
    act_d = block((3, 2 * WIDE * ROWS, 256), BF16)
    res = block((2, (2 * MID + 5) * EXT, 128))
    res_d = block((2, 2 * MID * ROWS, 256), BF16)
    first = [raw, act, act, act_d, act_d]
    rest = [raw, act, act_d, res, res, res_d, res_d]
    halo = pltpu.VMEM((9, 2 * 16, 256), BF16)
    inner_scratch = [pltpu.VMEM(raw.shape, F32), halo, halo, halo]
    scratch_names = ("raw0", "halo0", "halo1", "halo2")

    even_col = swap_columns(0, w3)
    *held, token = call(
        functools.partial(first_inner_kernel, (*names[:-2], *FIRST, "token", "raw0"), sizes),
        (*rows, *params[:1]),
        [*first, (16, 128)],
        inner_scratch[:1],
        8, 2_000_000,
    )
    odd_col = swap_columns(1, token)
    wu, w4 = call(
        prep_four_kernel,
        (weight_up, weight_four),
        [(4 * 128, 4 * 256), (3, 2 * C4, 3 * 512)],
        [
            pltpu.VMEM((2, 24 * C4, 128), F32),
            pltpu.VMEM((40 * C4, 128), F32),
        ],
        16, 8_000_000,
    )

    held = call(
        functools.partial(
            inner_kernel, (*names, *["_" + name for name in FIRST], *SHARED, *scratch_names), sizes
        ),
        (*rows, *params, *held),
        [*first, *rest],
        inner_scratch,
        16, 8_000_000,
        aliases={len(names) + n: n for n in range(len(first))},
    )

    operands = (
        *tile, odd_row, even_row, even_col, odd_col,
        *params, wu, bias_up.reshape(1, C4), gain_four.reshape(1, C4), w4, bias_four.reshape(1, C4),
    )
    names = (
        "x", "p", "q", "odd_row", "even_row", "even_col", "odd_col",
        "g3", "b3", "w3", "wu", "bu", "g4", "w4", "b4",
    )
    scratch = list(inner_scratch)
    scratch += [pltpu.VMEM((2, (2 * len(RIM_SLOTS) + 2) * EXT, 128), F32)] * 3
    scratch += [pltpu.VMEM((4, 2 * 16, 256), BF16)] * 2
    scratch += [pltpu.VMEM((2, FINE * FEXT, 128), F32)] * 3
    scratch += [pltpu.VMEM((2, FINE * FEXT, 128), F32)] * 2
    scratch += [pltpu.VMEM((3, FINE * FROWS, 256), BF16)] * 3
    scratch_names += ("rim0", "rim1", "rim2", "resh0", "resh1", "z0", "z1", "z2", "s0", "s1", "fine0", "fine1", "fine2")
    got = call(
        functools.partial(
            main_kernel, (*names, *["_" + name for name in SHARED], "out", *SHARED, *scratch_names), sizes
        ),
        (*operands, *held),
        [(FROWS, 2 * COLS * FRAMES * C4), *first, *rest],
        scratch,
        24,
        aliases={len(names) + n: n + 1 for n in range(len(SHARED))},
    )
    return got[0]


def solution(mesh):
    tiled = P("row", ("section", "col"))
    return jax.shard_map(
        shards,
        mesh=mesh,
        in_specs=(tiled, tiled, P(), P(), P(), P(), P(), tiled, P(), P(), P()),
        out_specs=tiled,
        check_vma=False,
    )
```

```python
import functools
import types

import jax
import jax.numpy as jnp
from jax import lax
from jax.experimental import pallas as pl
from jax.experimental.pallas import tpu as pltpu
from jax.sharding import PartitionSpec as P

EPSILON = 1e-06
BF16 = jnp.bfloat16
F32 = jnp.float32

ROWS = 16
COLS = 10
C3 = 192
C4 = 96
FRAMES = 4
WIDE = COLS + 4
MID = COLS + 2
EXT = 24
FINE = 2 * COLS + 2
FROWS = 2 * ROWS
FEXT = 40
XW = COLS * FRAMES * C3
PW = COLS * 2 * C3
QW = 2 * COLS * 2 * C4
COLX = FRAMES * C3
COLP = 2 * C3
COLQ = 2 * C4
QAT = 2 * COLX + 2 * COLP


def nt_dot(lhs, rhs):
    return lax.dot_general(lhs, rhs, (((1,), (1,)), ((), ())), preferred_element_type=F32)


def silu(value):
    half = 0.5 * value
    return half + half * jnp.tanh(half)


def lane_mask(rows, below):
    return lax.broadcasted_iota(jnp.int32, (rows, 128), 1) < below


def split_pair(v0, v1, v2):
    low = lane_mask(v0.shape[0], 64)
    r1 = pltpu.roll(v1, 64, 1)
    r2 = pltpu.roll(v2, 64, 1)
    zero = jnp.zeros_like(v1)
    return (v0, jnp.where(low, v1, zero)), (jnp.where(low, r1, r2), jnp.where(low, r2, zero))


def norm_pair(v0, v1, v2, gains):
    low = lane_mask(v0.shape[0], 64)
    sq1 = v1 * v1
    zero = jnp.zeros_like(v1)
    sum_a = jnp.sum(v0 * v0 + jnp.where(low, sq1, zero), axis=1, keepdims=True)
    sum_b = jnp.sum(v2 * v2 + jnp.where(low, zero, sq1), axis=1, keepdims=True)
    inv_a = lax.rsqrt(sum_a * (1.0 / C3) + EPSILON)
    inv_b = lax.rsqrt(sum_b * (1.0 / C3) + EPSILON)
    return (
        silu(v0 * inv_a * gains[0]),
        silu(v1 * jnp.where(low, inv_a, inv_b) * gains[1]),
        silu(v2 * inv_b * gains[2]),
    )


def weave(*streams):
    lists = []
    for stream in streams:
        lists.append(list(stream))
    order = []
    for place, steps in enumerate(lists):
        order += [((n + 0.5) / len(steps), place, step) for n, step in enumerate(steps)]
    for _, _, step in sorted(order, key=lambda entry: entry[:2]):
        step()


FIRST = ("raw1", "act0", "act1", "actd0", "actd1")
SHARED = (*FIRST, "raw2", "act2", "actd2", "res0", "res1", "resd0", "resd1")
INNER = (2, COLS - 2)
RIMS = ((0, 2), (COLS, 2))
RIM_SLOTS = (0, 1, 2, 3, WIDE - 4, WIDE - 3, WIDE - 2, WIDE - 1)


def stages(refs, row_count, col_count, col_size):
    x_ref, p_ref, q_ref = refs.get("x"), refs.get("p"), refs.get("q")
    odd_row, even_row = refs.get("odd_row"), refs.get("even_row")
    even_col, odd_col = refs.get("even_col"), refs.get("odd_col")
    w3_ref, wu_ref, w4_ref = refs.get("w3"), refs.get("wu"), refs.get("w4")
    out_ref = refs.get("out")

    def several(name, count):
        return [refs.get(name + str(n)) for n in range(count)]

    raw, act, act_d, halo_d = several("raw", 3), several("act", 3), several("actd", 3), several("halo", 3)
    rims = several("rim", 3)
    res, res_d, res_h = several("res", 2), several("resd", 2), several("resh", 2)
    z4, s4, act4_d = several("z", 3), several("s", 2), several("fine", 3)
    row = lax.axis_index("row")
    col = lax.axis_index("section") * col_size + lax.axis_index("col")
    row_odd = lax.rem(row, 2) == 1
    col_odd = lax.rem(col, 2) == 1
    first_row, last_row = row == 0, row == row_count - 1
    first_col, last_col = col == 0, col == col_count - 1

    def wide(value):
        return value.astype(F32)

    def pick(flag, one, other, *index):
        return wide(jnp.where(flag, one[index], other[index]))

    def above(lanes):
        return pick(row_odd, even_row, odd_row, slice(0, 2), lanes)

    def below(lanes):
        return pick(row_odd, odd_row, even_row, slice(0, 2), lanes)

    def left(lanes):
        return pick(col_odd, even_col, odd_col, slice(0, ROWS + 4), lanes)

    def right(lanes):
        return pick(col_odd, odd_col, even_col, slice(0, ROWS + 4), lanes)

    def keep(inside, value):
        return jnp.where(inside, value, jnp.zeros_like(value))

    def rounded(value):
        return value.astype(BF16).astype(F32)

    def pair_of(ref, *index):
        return jnp.concatenate([ref[(0,) + index], ref[(1,) + index]], axis=1).astype(BF16)

    g3 = refs["g3"][...]
    gains = (
        g3[:, 0:128],
        jnp.concatenate([g3[:, 128:192], g3[:, 0:64]], axis=1),
        g3[:, 64:192],
    )

    def place_of(jj, rim):
        if rim:
            return rims, len(RIM_SLOTS), RIM_SLOTS.index(jj)
        return act, WIDE, jj

    def load_column(group, jj, rim):
        held, slots, slot = place_of(jj, rim)
        base = jj * EXT
        for q in range(3):
            if 2 <= jj < WIDE - 2:
                at = (jj - 2) * COLX + (3 * (group - 1) + q) * 128
                if group == 0:
                    at = (jj - 2) * COLP + q * 128
                src, strip_at = (x_ref, at) if group else (p_ref, XW + at)
                strip = slice(strip_at, strip_at + 128)
                raw[group][q, base : base + 16, :] = wide(src[:, at : at + 128])
                raw[group][q, base + 16 : base + 18, :] = above(strip)
                raw[group][q, base + 18 : base + 20, :] = below(strip)
            else:
                side, lane = (left, jj) if jj < 2 else (right, jj - WIDE + 2)
                at = lane * COLX + (3 * (group - 1) + q) * 128
                if group == 0:
                    at = 2 * COLX + lane * COLP + q * 128
                raw[group][q, base : base + 20, :] = side(slice(at, at + 128))
        tiles = [raw[group][q, base : base + EXT, :] for q in range(3)]
        if group:
            tiles = norm_pair(*tiles, gains)
        for half, pair in enumerate(split_pair(*tiles)):
            at = (half * slots + slot) * EXT
            for q in range(2):
                held[group][q, at : at + 2, :] = pair[q][16:18]
                held[group][q, at + 2 : at + 18, :] = pair[q][0:16]
                held[group][q, at + 18 : at + 20, :] = pair[q][18:20]

    def copy_column(group, jj):
        slot = RIM_SLOTS.index(jj)
        for half in range(2):
            source, target = (half * WIDE + jj) * EXT, (half * len(RIM_SLOTS) + slot) * EXT
            for q in range(2):
                rims[group][q, target : target + EXT, :] = act[group][q, source : source + EXT, :]

    def shift_column(group, jj, rim):
        held, slots, slot = place_of(jj, rim)
        for half in range(2):
            slab = half * WIDE + jj
            for dy in range(3):
                at = (half * slots + slot) * EXT + 1 + dy
                both = pair_of(held[group], slice(at, at + ROWS), slice(None))
                act_d[group][dy, slab * ROWS : (slab + 1) * ROWS, :] = both

    def gather_rows(group, dx, dy, rim):
        held, slots, start = (rims, len(RIM_SLOTS), 0) if rim else (act, WIDE, INNER[0])
        for half in range(2):
            at = (half * slots + start + dx) * EXT + dy
            tiles = []
            for q in range(2):
                sides = [held[group][q, pl.ds(at + skip, 8, stride=EXT), :] for skip in (0, 17)]
                tiles.append(jnp.concatenate(sides, axis=0))
            both = jnp.concatenate(tiles, axis=1).astype(BF16)
            halo_d[group][3 * dx + dy, half * 16 : (half + 1) * 16, :] = both

    def coarse_steps(group, columns, rim=False):
        for jj in columns:
            yield lambda jj=jj: (load_column(group, jj, rim), shift_column(group, jj, rim))

    def copy_steps(group):
        for jj in RIM_SLOTS[2:6]:
            yield lambda jj=jj: copy_column(group, jj)

    def row_steps(group, rim=False):
        for dx in range(3):
            for dy in range(3):
                yield lambda dx=dx, dy=dy: gather_rows(group, dx, dy, rim)

    center = {}
    edges = {}

    def conv_three(frames, runs):
        kernels = []
        pieces = []
        for dy in range(3):
            for dx in range(3):
                kernels.append(w3_ref[3 * dy + dx])
                for t in range(3):
                    parts = []
                    for p, k in frames:
                        group, half = p + (k + t) // 2, (k + t) % 2
                        for start, count in runs:
                            at = (half * WIDE + start + dx) * ROWS
                            parts.append(act_d[group][dy, at : at + count * ROWS, :])
                        parts.append(halo_d[group][3 * dx + dy, half * 16 : (half + 1) * 16, :])
                    pieces.append(jnp.concatenate(parts, axis=0))
        got = nt_dot(jnp.concatenate(pieces, axis=1), jnp.concatenate(kernels, axis=1))
        at = 0
        for p, k in frames:
            for start, count in runs:
                for jm in range(start, start + count):
                    center[p, k, jm] = got[at : at + ROWS]
                    at += ROWS
            edges[p, k] = got[at : at + 16]
            at += 16

    def conv_three_steps(runs, *batches):
        for frames in batches:
            yield lambda frames=frames: conv_three(frames, runs)

    b3 = refs["b3"][...] if "b3" in refs else None

    def put_res(p, rows, value):
        res[p][0, rows, :] = value[:, 0:128]
        rest = jnp.zeros((value.shape[0], 64), F32)
        res[p][1, rows, :] = jnp.concatenate([value[:, 128:192], rest], axis=1)

    def result_column(p, jm):
        at = (jm + 1) * EXT
        tiles = [raw[p + 1][q, at : at + ROWS, :] for q in range(3)]
        for k, skip in enumerate(split_pair(*tiles)):
            slab = k * MID + jm
            value = center[p, k, jm] + b3
            value = rounded(value + jnp.concatenate([skip[0], skip[1][:, 0:64]], axis=1))
            if jm == 0:
                value = keep(jnp.logical_not(first_col), value)
            if jm == MID - 1:
                value = keep(jnp.logical_not(last_col), value)
            put_res(p, pl.ds(slab * EXT + 1, ROWS), value)

    def result_rows(p, side, start, count):
        inside = jnp.logical_not(last_row if side else first_row)
        column = lax.broadcasted_iota(jnp.int32, (count, 1), 0) + start
        if start == 0:
            inside = jnp.logical_and(inside, jnp.logical_or(column > 0, jnp.logical_not(first_col)))
        if start + count == MID:
            inside = jnp.logical_and(inside, jnp.logical_or(column < MID - 1, jnp.logical_not(last_col)))
        rows = pl.ds((start + 1) * EXT + (18 if side else 17), count, stride=EXT)
        tiles = [raw[p + 1][q, rows, :] for q in range(3)]
        for k, skip in enumerate(split_pair(*tiles)):
            at = 8 * side + (4 if start == COLS else 0)
            value = edges[p, k][at : at + count] + b3
            value = rounded(value + jnp.concatenate([skip[0], skip[1][:, 0:64]], axis=1))
            at = (k * MID + start) * EXT + (17 if side else 0)
            put_res(p, pl.ds(at, count, stride=EXT), keep(inside, value))

    def shift_result(p, jm):
        for k in range(2):
            slab = k * MID + jm
            for r in range(2):
                rows = slice(slab * EXT + r, slab * EXT + r + ROWS)
                res_d[p][r, slab * ROWS : (slab + 1) * ROWS, :] = pair_of(res[p], rows, slice(None))

    def gather_result(p, place):
        r, c = divmod(place, 2)
        for k in range(2):
            rows = pl.ds((k * MID + c) * EXT + ROWS + r, 16, stride=EXT)
            res_h[p][place, k * 16 : (k + 1) * 16, :] = pair_of(res[p], rows, slice(None))

    def result_steps(p, runs):
        for start, count in runs:
            for side in range(2):
                yield lambda side=side, start=start, count=count: result_rows(p, side, start, count)
            for jm in range(start, start + count):
                yield lambda jm=jm: (result_column(p, jm), shift_result(p, jm))

    def gather_steps(p):
        for place in range(4):
            yield lambda place=place: gather_result(p, place)

    span = COLS + 1
    total = [{}, {}]

    def conv_up(p, half):
        pieces = []
        for r in range(2):
            for c in range(2):
                parts = []
                for k in range(2):
                    at = (k * MID + c) * ROWS
                    parts.append(res_d[p][r, at : at + span * ROWS, :])
                    parts.append(res_h[p][2 * r + c, k * 16 : (k + 1) * 16, :])
                pieces.append(jnp.concatenate(parts, axis=0))
        got = nt_dot(jnp.concatenate(pieces, axis=1), wu_ref[half * 256 : (half + 1) * 256, :])
        for k in range(2):
            total[p][half, k] = got[k * (span + 1) * ROWS : (k + 1) * (span + 1) * ROWS]

    def conv_up_steps(p):
        for half in range(2):
            yield lambda half=half: conv_up(p, half)

    def padded(name):
        return jnp.concatenate([refs[name][...], jnp.zeros((1, 32), F32)], axis=1)

    bias_up = padded("bu") if "bu" in refs else None
    g4 = padded("g4") if "g4" in refs else None

    def act_four(value):
        square = jnp.sum(value * value, axis=1, keepdims=True)
        return silu(value * lax.rsqrt(square * (1.0 / C4) + EPSILON) * g4)

    def fine_rows(p, a, b, k):
        at = span * ROWS
        lanes = slice(b * 128, (b + 1) * 128)
        value = rounded(total[p][a, k][at : at + span, lanes] + bias_up)
        ext = FROWS if a else FROWS + 1
        rows = pl.ds((0 if b else FEXT) + ext, span, stride=2 * FEXT)
        if a:
            s4[p][k, rows, :] = value
        value = act_four(value)
        index = lax.broadcasted_iota(jnp.int32, (span, 1), 0)
        if b:
            inside = jnp.logical_or(index > 0, jnp.logical_not(first_col))
        else:
            inside = jnp.logical_or(index < span - 1, jnp.logical_not(last_col))
        if not a:
            inside = jnp.logical_and(inside, jnp.logical_not(last_row))
        z4[p + 1][k, rows, :] = keep(inside, value)

    top = lax.broadcasted_iota(jnp.int32, (ROWS, 1), 0) > 0
    rows_in = jnp.logical_or(top, jnp.logical_not(first_row))

    def fine_column(p, b, j):
        fx = 2 * j if b else 2 * j + 1
        for k in range(2):
            for a in range(2):
                lanes = slice(b * 128, (b + 1) * 128)
                value = rounded(total[p][a, k][j * ROWS : (j + 1) * ROWS, lanes] + bias_up)
                rows = pl.ds(fx * FEXT + 1 - a, ROWS, stride=2)
                if 1 <= fx <= 2 * COLS:
                    s4[p][k, rows, :] = value
                value = act_four(value)
                if a:
                    value = keep(rows_in, value)
                if fx == 0:
                    value = keep(jnp.logical_not(first_col), value)
                if fx == FINE - 1:
                    value = keep(jnp.logical_not(last_col), value)
                z4[p + 1][k, rows, :] = value
        shift_fine(p + 1, fx)

    def shift_fine(group, fx):
        for dy in range(3):
            rows = slice(fx * FEXT + dy, fx * FEXT + dy + FROWS)
            act4_d[group][dy, fx * FROWS : (fx + 1) * FROWS, :] = pair_of(z4[group], rows, slice(None))

    def fine_steps(p):
        for a in range(2):
            for b in range(2):
                for k in range(2):
                    yield lambda a=a, b=b, k=k: fine_rows(p, a, b, k)
        for j in range(span):
            for b in (1, 0):
                yield lambda b=b, j=j: fine_column(p, b, j)

    def put_cached(fx, row0, joined, first):
        rows = joined.shape[0]
        for t in range(2):
            at = first + t * C4
            value = jnp.concatenate([joined[:, at : at + C4], jnp.zeros((rows, 32), F32)], axis=1)
            z4[0][t, fx * FEXT + row0 : fx * FEXT + row0 + rows, :] = value

    def cached_column(fx):
        if 0 < fx < FINE - 1:
            at = (fx - 1) * COLQ
            start = at // 128 * 128
            first = at - start
            strip = slice(XW + PW + start, XW + PW + start + 256)
            put_cached(fx, 1, wide(q_ref[:, start : start + 256]), first)
            put_cached(fx, 0, above(strip)[1:2], first)
            put_cached(fx, FROWS + 1, below(strip)[0:1], first)
        else:
            lanes = (right if fx else left)(slice(QAT, QAT + 384))
            put_cached(fx, 0, lanes[17:18], 0)
            put_cached(fx, 1, lanes[0:16], 0)
            put_cached(fx, 1 + ROWS, lanes[0:16], COLQ)
            put_cached(fx, FROWS + 1, lanes[18:19], 0)
        shift_fine(0, fx)

    def cached_steps():
        for fx in range(FINE):
            yield lambda fx=fx: cached_column(fx)

    size = COLS * FROWS
    done = [[None, None], [None, None]]

    def conv_four(p, half):
        pieces = []
        for dy in range(3):
            for dx in range(3):
                at = (dx + half * COLS) * FROWS
                pieces += [act4_d[group][dy, at : at + size, :] for group in (p, p + 1)]
        kernel = jnp.concatenate([w4_ref[dy] for dy in range(3)], axis=1)
        done[p][half] = nt_dot(jnp.concatenate(pieces, axis=1), kernel)

    def conv_four_steps(p):
        for half in range(2):
            yield lambda half=half: conv_four(p, half)

    bias_four = jnp.concatenate([refs["b4"][...]] * 2, axis=1) if "b4" in refs else None
    first = lane_mask(FROWS, C4)

    def out_column(p, fx):
        rows = slice((fx + 1) * FEXT + 1, (fx + 1) * FEXT + 1 + FROWS)
        other = pltpu.roll(s4[p][1, rows, :], C4, 1)
        skip = jnp.concatenate([jnp.where(first, s4[p][0, rows, :], other), other[:, 0:64]], axis=1)
        at = fx % COLS * FROWS
        value = (done[p][fx // COLS][at : at + FROWS] + bias_four + skip).astype(BF16)
        out_ref[:, fx * 384 + p * 192 : fx * 384 + (p + 1) * 192] = value

    def out_steps(p):
        for fx in range(2 * COLS):
            yield lambda fx=fx: out_column(p, fx)

    return types.SimpleNamespace(**locals())


OWN = range(2, WIDE - 2)


def first_inner_kernel(names, sizes, *all_refs):
    refs = dict(zip(names, all_refs))
    col = lax.axis_index("section") * sizes[2] + lax.axis_index("col")

    @pl.when(col == sizes[1] // 2)
    def _():
        do = stages(refs, *sizes)
        weave(do.coarse_steps(0, OWN), do.coarse_steps(1, OWN))


def inner_kernel(names, sizes, *all_refs):
    refs = dict(zip(names, all_refs))
    col = lax.axis_index("section") * sizes[2] + lax.axis_index("col")

    @pl.when(col != sizes[1] // 2)
    def _():
        do = stages(refs, *sizes)
        weave(do.coarse_steps(0, OWN), do.coarse_steps(1, OWN))

    do = stages(refs, *sizes)
    weave(do.row_steps(0), do.row_steps(1))
    weave(do.conv_three_steps([INNER], [(0, 0), (0, 1)]), do.coarse_steps(2, OWN))
    weave(do.row_steps(2))
    weave(do.conv_three_steps([INNER], [(1, 0), (1, 1)]), do.result_steps(0, [INNER]))
    weave(do.result_steps(1, [INNER]))


def main_kernel(names, sizes, *all_refs):
    do = stages(dict(zip(names, all_refs)), *sizes)
    sides = (0, 1, WIDE - 2, WIDE - 1)
    weave(*[do.copy_steps(group) for group in range(3)])
    weave(*[do.coarse_steps(group, sides, True) for group in range(3)])
    weave(*[do.row_steps(group, True) for group in range(3)])
    weave(do.conv_three_steps(RIMS, [(0, 0), (0, 1)], [(1, 0), (1, 1)]), do.cached_steps())
    weave(do.result_steps(0, RIMS))
    weave(do.gather_steps(0))
    weave(do.result_steps(1, RIMS))
    weave(do.gather_steps(1))
    weave(do.conv_up_steps(0))
    weave(do.conv_up_steps(1))
    weave(do.fine_steps(0))
    weave(do.conv_four_steps(0), do.fine_steps(1))
    weave(do.conv_four_steps(1), do.out_steps(0))
    weave(do.out_steps(1))


def split_pairs(flat_ref, parts, pairs, taps, stride):
    low = lane_mask(taps, 64)
    zero = jnp.zeros((taps, 128), F32)
    for pair in pairs:
        v0, v1, v2 = [flat_ref[:, (3 * pair + q) * 128 : (3 * pair + q + 1) * 128].astype(F32) for q in range(3)]
        r1, r2 = pltpu.roll(v1, 64, 1), pltpu.roll(v2, 64, 1)
        at = 2 * pair * stride
        parts[0, at : at + taps, :] = v0
        parts[1, at : at + taps, :] = jnp.where(low, v1, zero)
        parts[0, at + stride : at + stride + taps, :] = jnp.where(low, r1, r2)
        parts[1, at + stride : at + stride + taps, :] = jnp.where(low, r2, zero)


def prep_three_kernel(flat_ref, out_ref, parts):
    split_pairs(flat_ref, parts, range(C3 // 2), 27, 40)
    for tap in range(27):
        both = [parts[q, pl.ds(tap, C3, stride=40), :] for q in range(2)]
        t, place = divmod(tap, 9)
        out_ref[place, :, t * 256 : (t + 1) * 256] = jnp.concatenate(both, axis=1).astype(BF16)


def prep_four_kernel(up_ref, four_ref, up_out, four_out, parts_u, parts_f):
    split_pairs(up_ref, parts_u, range(C4 // 2), 9, 24)
    taps = {}
    for tap in range(9):
        for q in range(2):
            taps[tap, q] = parts_u[q, pl.ds(tap, C4, stride=24), :]
    spans = {(0, 0): (0,), (0, 1): (1, 2), (1, 0): (0, 1), (1, 1): (2,)}
    rest = jnp.zeros((32, 256), BF16)
    for a in range(2):
        for b in range(2):
            at = (2 * a + b) * 128
            for r in range(2):
                for c in range(2):
                    tiles = []
                    for q in range(2):
                        total = None
                        for dy in spans[a, r]:
                            for dx in spans[b, c]:
                                one = taps[3 * dy + dx, q]
                                total = one if total is None else total + one
                        tiles.append(total)
                    lanes = slice((2 * r + c) * 256, (2 * r + c + 1) * 256)
                    up_out[at : at + C4, lanes] = jnp.concatenate(tiles, axis=1).astype(BF16)
                    up_out[at + C4 : at + 128, lanes] = rest
    lane = lax.broadcasted_iota(jnp.int32, (27, 128), 1)
    empty = jnp.zeros((27, 128), F32)
    for four in range(C4 // 4):
        at = 3 * four * 128
        v0, v1, v2 = [four_ref[:, at + q * 128 : at + (q + 1) * 128].astype(F32) for q in range(3)]
        second = jnp.where(lane < 32, pltpu.roll(v0, 32, 1), pltpu.roll(v1, 32, 1))
        third = jnp.where(lane < 64, pltpu.roll(v1, 64, 1), pltpu.roll(v2, 64, 1))
        for m, value in enumerate((v0, second, third, pltpu.roll(v2, 96, 1))):
            at = (4 * four + m) * 40
            parts_f[at : at + 27, :] = jnp.where(lane < C4, value, empty)
    none = jnp.zeros((C4, 128), BF16)
    for place in range(9):
        dy, dx = divmod(place, 3)
        at = dx * 512
        four_out[dy, 0:C4, at + 384 : at + 512] = none
        four_out[dy, C4 : 2 * C4, at : at + 128] = none
        for t in range(3):
            kernel = parts_f[pl.ds(9 * t + place, C4, stride=40), :].astype(BF16)
            four_out[dy, 0:C4, at + t * 128 : at + (t + 1) * 128] = kernel
            four_out[dy, C4 : 2 * C4, at + (t + 1) * 128 : at + (t + 2) * 128] = kernel


def row_strips(refs, low_flag, out_ref):
    at = 0
    for ref in refs:
        rows, width = ref.shape
        out_ref[:, at : at + width] = jnp.where(low_flag, ref[0:2, :], ref[rows - 2 : rows, :])
        at += width


def row_strips_kernel(x_ref, p_ref, q_ref, even_ref, odd_ref, x_own, p_own, q_own, sems):
    own = (x_own, p_own, q_own)
    copies = [
        pltpu.make_async_copy(source, target, sems.at[n])
        for n, (source, target) in enumerate(zip((x_ref, p_ref, q_ref), own))
    ]
    for copy in copies:
        copy.start()
    for copy in copies:
        copy.wait()
    row_odd = lax.rem(lax.axis_index("row"), 2) == 1
    row_strips(own, row_odd, even_ref)
    row_strips(own, jnp.logical_not(row_odd), odd_ref)


def col_strips_kernel(x_ref, p_ref, q_ref, odd_row, even_row, _, out_ref, *, col_size, parity):
    row_odd = lax.rem(lax.axis_index("row"), 2) == 1
    col = lax.axis_index("section") * col_size + lax.axis_index("col")
    take_low = lax.rem(col, 2) == parity
    strips = (
        jnp.where(row_odd, even_row[...], odd_row[...]),
        jnp.where(row_odd, odd_row[...], even_row[...]),
    )

    def put(rows, at, low, high):
        out_ref[rows, at : at + low.shape[1]] = jnp.where(take_low, low, high)

    start = 0
    for ref, at, width, lanes in (
        (x_ref, 0, XW, 2 * COLX), (p_ref, 2 * COLX, PW, 2 * COLP), (q_ref, QAT, QW, COLQ)
    ):
        high = width - lanes
        if ref is q_ref:
            for half in range(2):
                rows = slice(half * ROWS, (half + 1) * ROWS)
                put(slice(0, ROWS), at + half * lanes, ref[rows, 0:lanes], ref[rows, high:width])
        else:
            put(slice(0, ROWS), at, ref[:, 0:lanes], ref[:, high:width])
        for place, strip in enumerate(strips):
            rows = slice(ROWS + 2 * place, ROWS + 2 * place + 2)
            put(rows, at, strip[:, start : start + lanes], strip[:, start + high : start + width])
            if ref is q_ref:
                out_ref[rows, at + lanes : at + 2 * lanes] = jnp.zeros((2, lanes), BF16)
        start += width


def call(kernel, operands, outputs, scratch, megabytes, moved=0, unread=0, space=pl.ANY, aliases=None):
    cost = pl.CostEstimate(flops=moved, bytes_accessed=moved, transcendentals=0) if moved else None
    vmem = pl.BlockSpec(memory_space=pltpu.VMEM)
    shapes = [
        shape if isinstance(shape, jax.ShapeDtypeStruct) else jax.ShapeDtypeStruct(shape, BF16)
        for shape in outputs
    ]
    got = pl.pallas_call(
        kernel,
        out_shape=shapes,
        in_specs=[vmem] * (len(operands) - unread) + [pl.BlockSpec(memory_space=space)] * unread,
        out_specs=[vmem] * len(outputs),
        scratch_shapes=scratch,
        cost_estimate=cost,
        input_output_aliases=aliases or {},
        compiler_params=pltpu.CompilerParams(vmem_limit_bytes=megabytes * 1024 * 1024),
    )(*operands)
    return got[0] if len(outputs) == 1 else got


def swap_pairs(count, start):
    out = []
    for low in range(start, count - 1, 2):
        out += [(low, low + 1), (low + 1, low)]
    return out


def shards(
    section_input,
    cache_three,
    gain_three,
    bias_three,
    weight_three,
    weight_up,
    bias_up,
    cache_four,
    gain_four,
    weight_four,
    bias_four,
):
    row_count = lax.axis_size("row")
    col_size = lax.axis_size("col")
    col_count = lax.axis_size("section") * col_size
    tile = (section_input, cache_three, cache_four)

    row_strip = (2, XW + PW + QW)
    own = [pltpu.VMEM(block.shape, BF16) for block in tile]
    even_strip, odd_strip = call(
        row_strips_kernel,
        tile,
        [row_strip] * 2,
        [*own, pltpu.SemaphoreType.DMA((3,))],
        62, unread=3, space=pltpu.HBM,
    )
    even_row = lax.ppermute(even_strip, "row", swap_pairs(row_count, 0))
    odd_row = lax.ppermute(odd_strip, "row", swap_pairs(row_count, 1))

    w3 = call(
        prep_three_kernel,
        (weight_three,),
        [(9, C3, 3 * 256)],
        [pltpu.VMEM((2, 40 * C3, 128), F32)],
        16, 8_000_000,
    )
    col_strip = (ROWS + 4, QAT + 2 * COLQ)

    def swap_columns(parity, after):
        def col_kernel(*refs):
            col_strips_kernel(*refs, col_size=col_size, parity=1 - parity)

        strip = call(col_kernel, (*tile, odd_row, even_row, after), [col_strip], [], 4, unread=1)
        return lax.ppermute(strip, ("section", "col"), swap_pairs(col_count, parity))

    sizes = (row_count, col_count, col_size)
    rows = (section_input, cache_three, odd_row, even_row)
    params = (gain_three.reshape(1, C3), bias_three.reshape(1, C3), w3)
    names = ("x", "p", "odd_row", "even_row", "g3", "b3", "w3")

    def block(shape, dtype=F32):
        return jax.ShapeDtypeStruct(shape, dtype)

    raw = block((3, 16 * EXT, 128))
    act = block((2, (2 * WIDE + 4) * EXT, 128))
    act_d = block((3, 2 * WIDE * ROWS, 256), BF16)
    res = block((2, (2 * MID + 5) * EXT, 128))
    res_d = block((2, 2 * MID * ROWS, 256), BF16)
    first = [raw, act, act, act_d, act_d]
    rest = [raw, act, act_d, res, res, res_d, res_d]
    halo = pltpu.VMEM((9, 2 * 16, 256), BF16)
    inner_scratch = [pltpu.VMEM(raw.shape, F32), halo, halo, halo]
    scratch_names = ("raw0", "halo0", "halo1", "halo2")

    even_col = swap_columns(0, w3)
    *held, token = call(
        functools.partial(first_inner_kernel, (*names[:-2], *FIRST, "token", "raw0"), sizes),
        (*rows, *params[:1]),
        [*first, (16, 128)],
        inner_scratch[:1],
        8, 2_000_000,
    )
    odd_col = swap_columns(1, token)
    wu, w4 = call(
        prep_four_kernel,
        (weight_up, weight_four),
        [(4 * 128, 4 * 256), (3, 2 * C4, 3 * 512)],
        [
            pltpu.VMEM((2, 24 * C4, 128), F32),
            pltpu.VMEM((40 * C4, 128), F32),
        ],
        16, 8_000_000,
    )

    held = call(
        functools.partial(
            inner_kernel, (*names, *["_" + name for name in FIRST], *SHARED, *scratch_names), sizes
        ),
        (*rows, *params, *held),
        [*first, *rest],
        inner_scratch,
        16, 8_000_000,
        aliases={len(names) + n: n for n in range(len(first))},
    )

    operands = (
        *tile, odd_row, even_row, even_col, odd_col,
        *params, wu, bias_up.reshape(1, C4), gain_four.reshape(1, C4), w4, bias_four.reshape(1, C4),
    )
    names = (
        "x", "p", "q", "odd_row", "even_row", "even_col", "odd_col",
        "g3", "b3", "w3", "wu", "bu", "g4", "w4", "b4",
    )
    scratch = list(inner_scratch)
    scratch += [pltpu.VMEM((2, (2 * len(RIM_SLOTS) + 2) * EXT, 128), F32)] * 3
    scratch += [pltpu.VMEM((4, 2 * 16, 256), BF16)] * 2
    scratch += [pltpu.VMEM((2, FINE * FEXT, 128), F32)] * 3
    scratch += [pltpu.VMEM((2, FINE * FEXT, 128), F32)] * 2
    scratch += [pltpu.VMEM((3, FINE * FROWS, 256), BF16)] * 3
    scratch_names += ("rim0", "rim1", "rim2", "resh0", "resh1", "z0", "z1", "z2", "s0", "s1", "fine0", "fine1", "fine2")
    got = call(
        functools.partial(
            main_kernel, (*names, *["_" + name for name in SHARED], "out", *SHARED, *scratch_names), sizes
        ),
        (*operands, *held),
        [(FROWS, 2 * COLS * FRAMES * C4), *first, *rest],
        scratch,
        24,
        aliases={len(names) + n: n + 1 for n in range(len(SHARED))},
    )
    return got[0]


def solution(mesh):
    tiled = P("row", ("section", "col"))
    return jax.shard_map(
        shards,
        mesh=mesh,
        in_specs=(tiled, tiled, P(), P(), P(), P(), P(), tiled, P(), P(), P()),
        out_specs=tiled,
        check_vma=False,
    )
```

```python
import functools
import types

import jax
import jax.numpy as jnp
from jax import lax
from jax.experimental import pallas as pl
from jax.experimental.pallas import tpu as pltpu
from jax.sharding import PartitionSpec as P

EPSILON = 1e-06
BF16 = jnp.bfloat16
F32 = jnp.float32

ROWS = 16
COLS = 10
C3 = 192
C4 = 96
FRAMES = 4
WIDE = COLS + 4
MID = COLS + 2
EXT = 24
FINE = 2 * COLS + 2
FROWS = 2 * ROWS
FEXT = 40
XW = COLS * FRAMES * C3
PW = COLS * 2 * C3
QW = 2 * COLS * 2 * C4
COLX = FRAMES * C3
COLP = 2 * C3
COLQ = 2 * C4
QAT = 2 * COLX + 2 * COLP


def nt_dot(lhs, rhs):
    return lax.dot_general(lhs, rhs, (((1,), (1,)), ((), ())), preferred_element_type=F32)


def silu(value):
    half = 0.5 * value
    return half + half * jnp.tanh(half)


def lane_mask(rows, below):
    return lax.broadcasted_iota(jnp.int32, (rows, 128), 1) < below


def split_pair(v0, v1, v2):
    low = lane_mask(v0.shape[0], 64)
    r1 = pltpu.roll(v1, 64, 1)
    r2 = pltpu.roll(v2, 64, 1)
    zero = jnp.zeros_like(v1)
    return (v0, jnp.where(low, v1, zero)), (jnp.where(low, r1, r2), jnp.where(low, r2, zero))


def norm_pair(v0, v1, v2, gains):
    low = lane_mask(v0.shape[0], 64)
    sq1 = v1 * v1
    zero = jnp.zeros_like(v1)
    sum_a = jnp.sum(v0 * v0 + jnp.where(low, sq1, zero), axis=1, keepdims=True)
    sum_b = jnp.sum(v2 * v2 + jnp.where(low, zero, sq1), axis=1, keepdims=True)
    inv_a = lax.rsqrt(sum_a * (1.0 / C3) + EPSILON)
    inv_b = lax.rsqrt(sum_b * (1.0 / C3) + EPSILON)
    return (
        silu(v0 * inv_a * gains[0]),
        silu(v1 * jnp.where(low, inv_a, inv_b) * gains[1]),
        silu(v2 * inv_b * gains[2]),
    )


def weave(*streams):
    lists = []
    for stream in streams:
        lists.append(list(stream))
    order = []
    for place, steps in enumerate(lists):
        order += [((n + 0.5) / len(steps), place, step) for n, step in enumerate(steps)]
    for _, _, step in sorted(order, key=lambda entry: entry[:2]):
        step()


FIRST = ("raw1", "act0", "act1", "actd0", "actd1")
SHARED = (*FIRST, "raw2", "act2", "actd2", "res0", "res1", "resd0", "resd1")
INNER = (2, COLS - 2)
RIMS = ((0, 2), (COLS, 2))
RIM_SLOTS = (0, 1, 2, 3, WIDE - 4, WIDE - 3, WIDE - 2, WIDE - 1)


def stages(refs, row_count, col_count, col_size):
    x_ref, p_ref, q_ref = refs.get("x"), refs.get("p"), refs.get("q")
    odd_row, even_row = refs.get("odd_row"), refs.get("even_row")
    even_col, odd_col = refs.get("even_col"), refs.get("odd_col")
    w3_ref, wu_ref, w4_ref = refs.get("w3"), refs.get("wu"), refs.get("w4")
    out_ref = refs.get("out")

    def several(name, count):
        return [refs.get(name + str(n)) for n in range(count)]

    raw, act, act_d, halo_d = several("raw", 3), several("act", 3), several("actd", 3), several("halo", 3)
    rims = several("rim", 3)
    res, res_d, res_h = several("res", 2), several("resd", 2), several("resh", 2)
    z4, s4, act4_d = several("z", 3), several("s", 2), several("fine", 3)
    row = lax.axis_index("row")
    col = lax.axis_index("section") * col_size + lax.axis_index("col")
    row_odd = lax.rem(row, 2) == 1
    col_odd = lax.rem(col, 2) == 1
    first_row, last_row = row == 0, row == row_count - 1
    first_col, last_col = col == 0, col == col_count - 1

    def wide(value):
        return value.astype(F32)

    def pick(flag, one, other, *index):
        return wide(jnp.where(flag, one[index], other[index]))

    def above(lanes):
        return pick(row_odd, even_row, odd_row, slice(0, 2), lanes)

    def below(lanes):
        return pick(row_odd, odd_row, even_row, slice(0, 2), lanes)

    def left(lanes):
        return pick(col_odd, even_col, odd_col, slice(0, ROWS + 4), lanes)

    def right(lanes):
        return pick(col_odd, odd_col, even_col, slice(0, ROWS + 4), lanes)

    def keep(inside, value):
        return jnp.where(inside, value, jnp.zeros_like(value))

    def rounded(value):
        return value.astype(BF16).astype(F32)

    def pair_of(ref, *index):
        return jnp.concatenate([ref[(0,) + index], ref[(1,) + index]], axis=1).astype(BF16)

    g3 = refs["g3"][...]
    gains = (
        g3[:, 0:128],
        jnp.concatenate([g3[:, 128:192], g3[:, 0:64]], axis=1),
        g3[:, 64:192],
    )

    def place_of(jj, rim):
        if rim:
            return rims, len(RIM_SLOTS), RIM_SLOTS.index(jj)
        return act, WIDE, jj

    def load_column(group, jj, rim):
        held, slots, slot = place_of(jj, rim)
        base = jj * EXT
        for q in range(3):
            if 2 <= jj < WIDE - 2:
                at = (jj - 2) * COLX + (3 * (group - 1) + q) * 128
                if group == 0:
                    at = (jj - 2) * COLP + q * 128
                src, strip_at = (x_ref, at) if group else (p_ref, XW + at)
                strip = slice(strip_at, strip_at + 128)
                raw[group][q, base : base + 16, :] = wide(src[:, at : at + 128])
                raw[group][q, base + 16 : base + 18, :] = above(strip)
                raw[group][q, base + 18 : base + 20, :] = below(strip)
            else:
                side, lane = (left, jj) if jj < 2 else (right, jj - WIDE + 2)
                at = lane * COLX + (3 * (group - 1) + q) * 128
                if group == 0:
                    at = 2 * COLX + lane * COLP + q * 128
                raw[group][q, base : base + 20, :] = side(slice(at, at + 128))
        tiles = [raw[group][q, base : base + EXT, :] for q in range(3)]
        if group:
            tiles = norm_pair(*tiles, gains)
        for half, pair in enumerate(split_pair(*tiles)):
            at = (half * slots + slot) * EXT
            for q in range(2):
                held[group][q, at : at + 2, :] = pair[q][16:18]
                held[group][q, at + 2 : at + 18, :] = pair[q][0:16]
                held[group][q, at + 18 : at + 20, :] = pair[q][18:20]

    def copy_column(group, jj):
        slot = RIM_SLOTS.index(jj)
        for half in range(2):
            source, target = (half * WIDE + jj) * EXT, (half * len(RIM_SLOTS) + slot) * EXT
            for q in range(2):
                rims[group][q, target : target + EXT, :] = act[group][q, source : source + EXT, :]

    def shift_column(group, jj, rim):
        held, slots, slot = place_of(jj, rim)
        for half in range(2):
            slab = half * WIDE + jj
            for dy in range(3):
                at = (half * slots + slot) * EXT + 1 + dy
                both = pair_of(held[group], slice(at, at + ROWS), slice(None))
                act_d[group][dy, slab * ROWS : (slab + 1) * ROWS, :] = both

    def gather_rows(group, dx, dy, rim):
        held, slots, start = (rims, len(RIM_SLOTS), 0) if rim else (act, WIDE, INNER[0])
        for half in range(2):
            at = (half * slots + start + dx) * EXT + dy
            tiles = []
            for q in range(2):
                sides = [held[group][q, pl.ds(at + skip, 8, stride=EXT), :] for skip in (0, 17)]
                tiles.append(jnp.concatenate(sides, axis=0))
            both = jnp.concatenate(tiles, axis=1).astype(BF16)
            halo_d[group][3 * dx + dy, half * 16 : (half + 1) * 16, :] = both

    def coarse_steps(group, columns, rim=False):
        for jj in columns:
            yield lambda jj=jj: (load_column(group, jj, rim), shift_column(group, jj, rim))

    def copy_steps(group):
        for jj in RIM_SLOTS[2:6]:
            yield lambda jj=jj: copy_column(group, jj)

    def row_steps(group, rim=False):
        for dx in range(3):
            for dy in range(3):
                yield lambda dx=dx, dy=dy: gather_rows(group, dx, dy, rim)

    center = {}
    edges = {}

    def conv_three(frames, runs):
        kernels = []
        pieces = []
        for dy in range(3):
            for dx in range(3):
                kernels.append(w3_ref[3 * dy + dx])
                for t in range(3):
                    parts = []
                    for p, k in frames:
                        group, half = p + (k + t) // 2, (k + t) % 2
                        for start, count in runs:
                            at = (half * WIDE + start + dx) * ROWS
                            parts.append(act_d[group][dy, at : at + count * ROWS, :])
                        parts.append(halo_d[group][3 * dx + dy, half * 16 : (half + 1) * 16, :])
                    pieces.append(jnp.concatenate(parts, axis=0))
        got = nt_dot(jnp.concatenate(pieces, axis=1), jnp.concatenate(kernels, axis=1))
        at = 0
        for p, k in frames:
            for start, count in runs:
                for jm in range(start, start + count):
                    center[p, k, jm] = got[at : at + ROWS]
                    at += ROWS
            edges[p, k] = got[at : at + 16]
            at += 16

    def conv_three_steps(runs, *batches):
        for frames in batches:
            yield lambda frames=frames: conv_three(frames, runs)

    b3 = refs["b3"][...] if "b3" in refs else None

    def put_res(p, rows, value):
        res[p][0, rows, :] = value[:, 0:128]
        rest = jnp.zeros((value.shape[0], 64), F32)
        res[p][1, rows, :] = jnp.concatenate([value[:, 128:192], rest], axis=1)

    def result_column(p, jm):
        at = (jm + 1) * EXT
        tiles = [raw[p + 1][q, at : at + ROWS, :] for q in range(3)]
        for k, skip in enumerate(split_pair(*tiles)):
            slab = k * MID + jm
            value = center[p, k, jm] + b3
            value = rounded(value + jnp.concatenate([skip[0], skip[1][:, 0:64]], axis=1))
            if jm == 0:
                value = keep(jnp.logical_not(first_col), value)
            if jm == MID - 1:
                value = keep(jnp.logical_not(last_col), value)
            put_res(p, pl.ds(slab * EXT + 1, ROWS), value)

    def result_rows(p, side, start, count):
        inside = jnp.logical_not(last_row if side else first_row)
        column = lax.broadcasted_iota(jnp.int32, (count, 1), 0) + start
        if start == 0:
            inside = jnp.logical_and(inside, jnp.logical_or(column > 0, jnp.logical_not(first_col)))
        if start + count == MID:
            inside = jnp.logical_and(inside, jnp.logical_or(column < MID - 1, jnp.logical_not(last_col)))
        rows = pl.ds((start + 1) * EXT + (18 if side else 17), count, stride=EXT)
        tiles = [raw[p + 1][q, rows, :] for q in range(3)]
        for k, skip in enumerate(split_pair(*tiles)):
            at = 8 * side + (4 if start == COLS else 0)
            value = edges[p, k][at : at + count] + b3
            value = rounded(value + jnp.concatenate([skip[0], skip[1][:, 0:64]], axis=1))
            at = (k * MID + start) * EXT + (17 if side else 0)
            put_res(p, pl.ds(at, count, stride=EXT), keep(inside, value))

    def shift_result(p, jm):
        for k in range(2):
            slab = k * MID + jm
            for r in range(2):
                rows = slice(slab * EXT + r, slab * EXT + r + ROWS)
                res_d[p][r, slab * ROWS : (slab + 1) * ROWS, :] = pair_of(res[p], rows, slice(None))

    def gather_result(p, place):
        r, c = divmod(place, 2)
        for k in range(2):
            rows = pl.ds((k * MID + c) * EXT + ROWS + r, 16, stride=EXT)
            res_h[p][place, k * 16 : (k + 1) * 16, :] = pair_of(res[p], rows, slice(None))

    def result_steps(p, runs):
        for start, count in runs:
            for side in range(2):
                yield lambda side=side, start=start, count=count: result_rows(p, side, start, count)
            for jm in range(start, start + count):
                yield lambda jm=jm: (result_column(p, jm), shift_result(p, jm))

    def gather_steps(p):
        for place in range(4):
            yield lambda place=place: gather_result(p, place)

    span = COLS + 1
    total = [{}, {}]

    def conv_up(p, half):
        pieces = []
        for r in range(2):
            for c in range(2):
                parts = []
                for k in range(2):
                    at = (k * MID + c) * ROWS
                    parts.append(res_d[p][r, at : at + span * ROWS, :])
                    parts.append(res_h[p][2 * r + c, k * 16 : (k + 1) * 16, :])
                pieces.append(jnp.concatenate(parts, axis=0))
        got = nt_dot(jnp.concatenate(pieces, axis=1), wu_ref[half * 256 : (half + 1) * 256, :])
        for k in range(2):
            total[p][half, k] = got[k * (span + 1) * ROWS : (k + 1) * (span + 1) * ROWS]

    def conv_up_steps(p):
        for half in range(2):
            yield lambda half=half: conv_up(p, half)

    def padded(name):
        return jnp.concatenate([refs[name][...], jnp.zeros((1, 32), F32)], axis=1)

    bias_up = padded("bu") if "bu" in refs else None
    g4 = padded("g4") if "g4" in refs else None

    def act_four(value):
        square = jnp.sum(value * value, axis=1, keepdims=True)
        return silu(value * lax.rsqrt(square * (1.0 / C4) + EPSILON) * g4)

    def fine_rows(p, a, b, k):
        at = span * ROWS
        lanes = slice(b * 128, (b + 1) * 128)
        value = rounded(total[p][a, k][at : at + span, lanes] + bias_up)
        ext = FROWS if a else FROWS + 1
        rows = pl.ds((0 if b else FEXT) + ext, span, stride=2 * FEXT)
        if a:
            s4[p][k, rows, :] = value
        value = act_four(value)
        index = lax.broadcasted_iota(jnp.int32, (span, 1), 0)
        if b:
            inside = jnp.logical_or(index > 0, jnp.logical_not(first_col))
        else:
            inside = jnp.logical_or(index < span - 1, jnp.logical_not(last_col))
        if not a:
            inside = jnp.logical_and(inside, jnp.logical_not(last_row))
        z4[p + 1][k, rows, :] = keep(inside, value)

    top = lax.broadcasted_iota(jnp.int32, (ROWS, 1), 0) > 0
    rows_in = jnp.logical_or(top, jnp.logical_not(first_row))

    def fine_column(p, b, j):
        fx = 2 * j if b else 2 * j + 1
        for k in range(2):
            for a in range(2):
                lanes = slice(b * 128, (b + 1) * 128)
                value = rounded(total[p][a, k][j * ROWS : (j + 1) * ROWS, lanes] + bias_up)
                rows = pl.ds(fx * FEXT + 1 - a, ROWS, stride=2)
                if 1 <= fx <= 2 * COLS:
                    s4[p][k, rows, :] = value
                value = act_four(value)
                if a:
                    value = keep(rows_in, value)
                if fx == 0:
                    value = keep(jnp.logical_not(first_col), value)
                if fx == FINE - 1:
                    value = keep(jnp.logical_not(last_col), value)
                z4[p + 1][k, rows, :] = value
        shift_fine(p + 1, fx)

    def shift_fine(group, fx):
        for dy in range(3):
            rows = slice(fx * FEXT + dy, fx * FEXT + dy + FROWS)
            act4_d[group][dy, fx * FROWS : (fx + 1) * FROWS, :] = pair_of(z4[group], rows, slice(None))

    def fine_steps(p):
        for a in range(2):
            for b in range(2):
                for k in range(2):
                    yield lambda a=a, b=b, k=k: fine_rows(p, a, b, k)
        for j in range(span):
            for b in (1, 0):
                yield lambda b=b, j=j: fine_column(p, b, j)

    def put_cached(fx, row0, joined, first):
        rows = joined.shape[0]
        for t in range(2):
            at = first + t * C4
            value = jnp.concatenate([joined[:, at : at + C4], jnp.zeros((rows, 32), F32)], axis=1)
            z4[0][t, fx * FEXT + row0 : fx * FEXT + row0 + rows, :] = value

    def cached_column(fx):
        if 0 < fx < FINE - 1:
            at = (fx - 1) * COLQ
            start = at // 128 * 128
            first = at - start
            strip = slice(XW + PW + start, XW + PW + start + 256)
            put_cached(fx, 1, wide(q_ref[:, start : start + 256]), first)
            put_cached(fx, 0, above(strip)[1:2], first)
            put_cached(fx, FROWS + 1, below(strip)[0:1], first)
        else:
            lanes = (right if fx else left)(slice(QAT, QAT + 384))
            put_cached(fx, 0, lanes[17:18], 0)
            put_cached(fx, 1, lanes[0:16], 0)
            put_cached(fx, 1 + ROWS, lanes[0:16], COLQ)
            put_cached(fx, FROWS + 1, lanes[18:19], 0)
        shift_fine(0, fx)

    def cached_steps():
        for fx in range(FINE):
            yield lambda fx=fx: cached_column(fx)

    size = COLS * FROWS
    done = [[None, None], [None, None]]

    def conv_four(p, half):
        pieces = []
        for dy in range(3):
            for dx in range(3):
                at = (dx + half * COLS) * FROWS
                pieces += [act4_d[group][dy, at : at + size, :] for group in (p, p + 1)]
        kernel = jnp.concatenate([w4_ref[dy] for dy in range(3)], axis=1)
        done[p][half] = nt_dot(jnp.concatenate(pieces, axis=1), kernel)

    def conv_four_steps(p):
        for half in range(2):
            yield lambda half=half: conv_four(p, half)

    bias_four = jnp.concatenate([refs["b4"][...]] * 2, axis=1) if "b4" in refs else None
    first = lane_mask(FROWS, C4)

    def out_column(p, fx):
        rows = slice((fx + 1) * FEXT + 1, (fx + 1) * FEXT + 1 + FROWS)
        other = pltpu.roll(s4[p][1, rows, :], C4, 1)
        skip = jnp.concatenate([jnp.where(first, s4[p][0, rows, :], other), other[:, 0:64]], axis=1)
        at = fx % COLS * FROWS
        value = (done[p][fx // COLS][at : at + FROWS] + bias_four + skip).astype(BF16)
        out_ref[:, fx * 384 + p * 192 : fx * 384 + (p + 1) * 192] = value

    def out_steps(p):
        for fx in range(2 * COLS):
            yield lambda fx=fx: out_column(p, fx)

    return types.SimpleNamespace(**locals())


OWN = range(2, WIDE - 2)
EARLY, LATE = OWN[:6], OWN[6:]


def first_inner_kernel(names, sizes, *all_refs):
    refs = dict(zip(names, all_refs))
    col = lax.axis_index("section") * sizes[2] + lax.axis_index("col")

    @pl.when(col == sizes[1] // 2)
    def _():
        do = stages(refs, *sizes)
        weave(do.coarse_steps(0, OWN), do.coarse_steps(1, EARLY))


def inner_kernel(names, sizes, *all_refs):
    refs = dict(zip(names, all_refs))
    col = lax.axis_index("section") * sizes[2] + lax.axis_index("col")

    @pl.when(col != sizes[1] // 2)
    def _():
        do = stages(refs, *sizes)
        weave(do.coarse_steps(0, OWN), do.coarse_steps(1, EARLY))

    do = stages(refs, *sizes)
    weave(do.coarse_steps(1, LATE), do.row_steps(0))
    weave(do.row_steps(1))
    weave(do.conv_three_steps([INNER], [(0, 0), (0, 1)]), do.coarse_steps(2, OWN))
    weave(do.row_steps(2))
    weave(do.conv_three_steps([INNER], [(1, 0), (1, 1)]), do.result_steps(0, [INNER]))
    weave(do.result_steps(1, [INNER]))


def main_kernel(names, sizes, *all_refs):
    do = stages(dict(zip(names, all_refs)), *sizes)
    sides = (0, 1, WIDE - 2, WIDE - 1)
    weave(*[do.copy_steps(group) for group in range(3)])
    weave(*[do.coarse_steps(group, sides, True) for group in range(3)])
    weave(*[do.row_steps(group, True) for group in range(3)])
    weave(do.conv_three_steps(RIMS, [(0, 0), (0, 1)], [(1, 0), (1, 1)]), do.cached_steps())
    weave(do.result_steps(0, RIMS))
    weave(do.gather_steps(0))
    weave(do.result_steps(1, RIMS))
    weave(do.gather_steps(1))
    weave(do.conv_up_steps(0))
    weave(do.conv_up_steps(1), do.fine_steps(0))
    weave(do.conv_four_steps(0), do.fine_steps(1))
    weave(do.conv_four_steps(1), do.out_steps(0))
    weave(do.out_steps(1))


def split_pairs(flat_ref, parts, pairs, taps, stride):
    low = lane_mask(taps, 64)
    zero = jnp.zeros((taps, 128), F32)
    for pair in pairs:
        v0, v1, v2 = [flat_ref[:, (3 * pair + q) * 128 : (3 * pair + q + 1) * 128].astype(F32) for q in range(3)]
        r1, r2 = pltpu.roll(v1, 64, 1), pltpu.roll(v2, 64, 1)
        at = 2 * pair * stride
        parts[0, at : at + taps, :] = v0
        parts[1, at : at + taps, :] = jnp.where(low, v1, zero)
        parts[0, at + stride : at + stride + taps, :] = jnp.where(low, r1, r2)
        parts[1, at + stride : at + stride + taps, :] = jnp.where(low, r2, zero)


def prep_three_kernel(flat_ref, out_ref, parts):
    split_pairs(flat_ref, parts, range(C3 // 2), 27, 40)
    for tap in range(27):
        both = [parts[q, pl.ds(tap, C3, stride=40), :] for q in range(2)]
        t, place = divmod(tap, 9)
        out_ref[place, :, t * 256 : (t + 1) * 256] = jnp.concatenate(both, axis=1).astype(BF16)


def prep_four_kernel(up_ref, four_ref, up_out, four_out, parts_u, parts_f):
    split_pairs(up_ref, parts_u, range(C4 // 2), 9, 24)
    taps = {}
    for tap in range(9):
        for q in range(2):
            taps[tap, q] = parts_u[q, pl.ds(tap, C4, stride=24), :]
    spans = {(0, 0): (0,), (0, 1): (1, 2), (1, 0): (0, 1), (1, 1): (2,)}
    rest = jnp.zeros((32, 256), BF16)
    for a in range(2):
        for b in range(2):
            at = (2 * a + b) * 128
            for r in range(2):
                for c in range(2):
                    tiles = []
                    for q in range(2):
                        total = None
                        for dy in spans[a, r]:
                            for dx in spans[b, c]:
                                one = taps[3 * dy + dx, q]
                                total = one if total is None else total + one
                        tiles.append(total)
                    lanes = slice((2 * r + c) * 256, (2 * r + c + 1) * 256)
                    up_out[at : at + C4, lanes] = jnp.concatenate(tiles, axis=1).astype(BF16)
                    up_out[at + C4 : at + 128, lanes] = rest
    lane = lax.broadcasted_iota(jnp.int32, (27, 128), 1)
    empty = jnp.zeros((27, 128), F32)
    for four in range(C4 // 4):
        at = 3 * four * 128
        v0, v1, v2 = [four_ref[:, at + q * 128 : at + (q + 1) * 128].astype(F32) for q in range(3)]
        second = jnp.where(lane < 32, pltpu.roll(v0, 32, 1), pltpu.roll(v1, 32, 1))
        third = jnp.where(lane < 64, pltpu.roll(v1, 64, 1), pltpu.roll(v2, 64, 1))
        for m, value in enumerate((v0, second, third, pltpu.roll(v2, 96, 1))):
            at = (4 * four + m) * 40
            parts_f[at : at + 27, :] = jnp.where(lane < C4, value, empty)
    none = jnp.zeros((C4, 128), BF16)
    for place in range(9):
        dy, dx = divmod(place, 3)
        at = dx * 512
        four_out[dy, 0:C4, at + 384 : at + 512] = none
        four_out[dy, C4 : 2 * C4, at : at + 128] = none
        for t in range(3):
            kernel = parts_f[pl.ds(9 * t + place, C4, stride=40), :].astype(BF16)
            four_out[dy, 0:C4, at + t * 128 : at + (t + 1) * 128] = kernel
            four_out[dy, C4 : 2 * C4, at + (t + 1) * 128 : at + (t + 2) * 128] = kernel


def row_strips_kernel(x_ref, p_ref, q_ref, even_ref, odd_ref, x_own, p_own, q_own, sems):
    row_odd = lax.rem(lax.axis_index("row"), 2) == 1
    parts = ((p_ref, p_own, XW), (x_ref, x_own, 0), (q_ref, q_own, XW + PW))
    copies = [
        pltpu.make_async_copy(source, own, sems.at[n]) for n, (source, own, _) in enumerate(parts)
    ]
    for copy in copies:
        copy.start()
    for copy, (_, own, at) in zip(copies, parts):
        copy.wait()
        rows, width = own.shape
        low, high = own[0:2, :], own[rows - 2 : rows, :]
        even_ref[:, at : at + width] = jnp.where(row_odd, low, high)
        odd_ref[:, at : at + width] = jnp.where(row_odd, high, low)


def col_strips_kernel(x_ref, p_ref, q_ref, odd_row, even_row, _, out_ref, *, col_size, parity):
    row_odd = lax.rem(lax.axis_index("row"), 2) == 1
    col = lax.axis_index("section") * col_size + lax.axis_index("col")
    take_low = lax.rem(col, 2) == parity
    strips = (
        jnp.where(row_odd, even_row[...], odd_row[...]),
        jnp.where(row_odd, odd_row[...], even_row[...]),
    )

    def put(rows, at, low, high):
        out_ref[rows, at : at + low.shape[1]] = jnp.where(take_low, low, high)

    start = 0
    for ref, at, width, lanes in (
        (x_ref, 0, XW, 2 * COLX), (p_ref, 2 * COLX, PW, 2 * COLP), (q_ref, QAT, QW, COLQ)
    ):
        high = width - lanes
        if ref is q_ref:
            for half in range(2):
                rows = slice(half * ROWS, (half + 1) * ROWS)
                put(slice(0, ROWS), at + half * lanes, ref[rows, 0:lanes], ref[rows, high:width])
        else:
            put(slice(0, ROWS), at, ref[:, 0:lanes], ref[:, high:width])
        for place, strip in enumerate(strips):
            rows = slice(ROWS + 2 * place, ROWS + 2 * place + 2)
            put(rows, at, strip[:, start : start + lanes], strip[:, start + high : start + width])
            if ref is q_ref:
                out_ref[rows, at + lanes : at + 2 * lanes] = jnp.zeros((2, lanes), BF16)
        start += width


def call(kernel, operands, outputs, scratch, megabytes, moved=0, unread=0, space=pl.ANY, aliases=None):
    cost = pl.CostEstimate(flops=moved, bytes_accessed=moved, transcendentals=0) if moved else None
    vmem = pl.BlockSpec(memory_space=pltpu.VMEM)
    shapes = [
        shape if isinstance(shape, jax.ShapeDtypeStruct) else jax.ShapeDtypeStruct(shape, BF16)
        for shape in outputs
    ]
    got = pl.pallas_call(
        kernel,
        out_shape=shapes,
        in_specs=[vmem] * (len(operands) - unread) + [pl.BlockSpec(memory_space=space)] * unread,
        out_specs=[vmem] * len(outputs),
        scratch_shapes=scratch,
        cost_estimate=cost,
        input_output_aliases=aliases or {},
        compiler_params=pltpu.CompilerParams(vmem_limit_bytes=megabytes * 1024 * 1024),
    )(*operands)
    return got[0] if len(outputs) == 1 else got


def swap_pairs(count, start):
    out = []
    for low in range(start, count - 1, 2):
        out += [(low, low + 1), (low + 1, low)]
    return out


def shards(
    section_input,
    cache_three,
    gain_three,
    bias_three,
    weight_three,
    weight_up,
    bias_up,
    cache_four,
    gain_four,
    weight_four,
    bias_four,
):
    row_count = lax.axis_size("row")
    col_size = lax.axis_size("col")
    col_count = lax.axis_size("section") * col_size
    tile = (section_input, cache_three, cache_four)

    row_strip = (2, XW + PW + QW)
    own = [pltpu.VMEM(block.shape, BF16) for block in tile]
    even_strip, odd_strip = call(
        row_strips_kernel,
        tile,
        [row_strip] * 2,
        [*own, pltpu.SemaphoreType.DMA((3,))],
        62, unread=3, space=pltpu.HBM,
    )
    even_row = lax.ppermute(even_strip, "row", swap_pairs(row_count, 0))
    odd_row = lax.ppermute(odd_strip, "row", swap_pairs(row_count, 1))

    w3 = call(
        prep_three_kernel,
        (weight_three,),
        [(9, C3, 3 * 256)],
        [pltpu.VMEM((2, 40 * C3, 128), F32)],
        16, 8_000_000,
    )
    col_strip = (ROWS + 4, QAT + 2 * COLQ)

    def swap_columns(parity, after):
        def col_kernel(*refs):
            col_strips_kernel(*refs, col_size=col_size, parity=1 - parity)

        strip = call(col_kernel, (*tile, odd_row, even_row, after), [col_strip], [], 4, unread=1)
        return lax.ppermute(strip, ("section", "col"), swap_pairs(col_count, parity))

    sizes = (row_count, col_count, col_size)
    rows = (section_input, cache_three, odd_row, even_row)
    params = (gain_three.reshape(1, C3), bias_three.reshape(1, C3), w3)
    names = ("x", "p", "odd_row", "even_row", "g3", "b3", "w3")

    def block(shape, dtype=F32):
        return jax.ShapeDtypeStruct(shape, dtype)

    raw = block((3, 16 * EXT, 128))
    act = block((2, (2 * WIDE + 4) * EXT, 128))
    act_d = block((3, 2 * WIDE * ROWS, 256), BF16)
    res = block((2, (2 * MID + 5) * EXT, 128))
    res_d = block((2, 2 * MID * ROWS, 256), BF16)
    first = [raw, act, act, act_d, act_d]
    rest = [raw, act, act_d, res, res, res_d, res_d]
    halo = pltpu.VMEM((9, 2 * 16, 256), BF16)
    inner_scratch = [pltpu.VMEM(raw.shape, F32), halo, halo, halo]
    scratch_names = ("raw0", "halo0", "halo1", "halo2")

    even_col = swap_columns(0, w3)
    *held, token = call(
        functools.partial(first_inner_kernel, (*names[:-2], *FIRST, "token", "raw0"), sizes),
        (*rows, *params[:1]),
        [*first, (16, 128)],
        inner_scratch[:1],
        8, 2_000_000,
    )
    odd_col = swap_columns(1, token)
    wu, w4 = call(
        prep_four_kernel,
        (weight_up, weight_four),
        [(4 * 128, 4 * 256), (3, 2 * C4, 3 * 512)],
        [
            pltpu.VMEM((2, 24 * C4, 128), F32),
            pltpu.VMEM((40 * C4, 128), F32),
        ],
        16, 8_000_000,
    )

    held = call(
        functools.partial(
            inner_kernel, (*names, *["_" + name for name in FIRST], *SHARED, *scratch_names), sizes
        ),
        (*rows, *params, *held),
        [*first, *rest],
        inner_scratch,
        16, 8_000_000,
        aliases={len(names) + n: n for n in range(len(first))},
    )

    operands = (
        *tile, odd_row, even_row, even_col, odd_col,
        *params, wu, bias_up.reshape(1, C4), gain_four.reshape(1, C4), w4, bias_four.reshape(1, C4),
    )
    names = (
        "x", "p", "q", "odd_row", "even_row", "even_col", "odd_col",
        "g3", "b3", "w3", "wu", "bu", "g4", "w4", "b4",
    )
    scratch = list(inner_scratch)
    scratch += [pltpu.VMEM((2, (2 * len(RIM_SLOTS) + 2) * EXT, 128), F32)] * 3
    scratch += [pltpu.VMEM((4, 2 * 16, 256), BF16)] * 2
    scratch += [pltpu.VMEM((2, FINE * FEXT, 128), F32)] * 3
    scratch += [pltpu.VMEM((2, FINE * FEXT, 128), F32)] * 2
    scratch += [pltpu.VMEM((3, FINE * FROWS, 256), BF16)] * 3
    scratch_names += ("rim0", "rim1", "rim2", "resh0", "resh1", "z0", "z1", "z2", "s0", "s1", "fine0", "fine1", "fine2")
    got = call(
        functools.partial(
            main_kernel, (*names, *["_" + name for name in SHARED], "out", *SHARED, *scratch_names), sizes
        ),
        (*operands, *held),
        [(FROWS, 2 * COLS * FRAMES * C4), *first, *rest],
        scratch,
        24,
        aliases={len(names) + n: n + 1 for n in range(len(SHARED))},
    )
    return got[0]


def solution(mesh):
    tiled = P("row", ("section", "col"))
    return jax.shard_map(
        shards,
        mesh=mesh,
        in_specs=(tiled, tiled, P(), P(), P(), P(), P(), tiled, P(), P(), P()),
        out_specs=tiled,
        check_vma=False,
    )
```

```python
import functools
import types

import jax
import jax.numpy as jnp
from jax import lax
from jax.experimental import pallas as pl
from jax.experimental.pallas import tpu as pltpu
from jax.sharding import PartitionSpec as P

EPSILON = 1e-06
BF16 = jnp.bfloat16
F32 = jnp.float32

ROWS = 16
COLS = 10
C3 = 192
C4 = 96
FRAMES = 4
WIDE = COLS + 4
MID = COLS + 2
EXT = 24
FINE = 2 * COLS + 2
FROWS = 2 * ROWS
FEXT = 40
XW = COLS * FRAMES * C3
PW = COLS * 2 * C3
QW = 2 * COLS * 2 * C4
COLX = FRAMES * C3
COLP = 2 * C3
COLQ = 2 * C4
QAT = 2 * COLX + 2 * COLP


def nt_dot(lhs, rhs):
    return lax.dot_general(lhs, rhs, (((1,), (1,)), ((), ())), preferred_element_type=F32)


def silu(value):
    half = 0.5 * value
    return half + half * jnp.tanh(half)


def lane_mask(rows, below):
    return lax.broadcasted_iota(jnp.int32, (rows, 128), 1) < below


def split_pair(v0, v1, v2):
    low = lane_mask(v0.shape[0], 64)
    r1 = pltpu.roll(v1, 64, 1)
    r2 = pltpu.roll(v2, 64, 1)
    zero = jnp.zeros_like(v1)
    return (v0, jnp.where(low, v1, zero)), (jnp.where(low, r1, r2), jnp.where(low, r2, zero))


def norm_pair(v0, v1, v2, gains):
    low = lane_mask(v0.shape[0], 64)
    sq1 = v1 * v1
    zero = jnp.zeros_like(v1)
    sum_a = jnp.sum(v0 * v0 + jnp.where(low, sq1, zero), axis=1, keepdims=True)
    sum_b = jnp.sum(v2 * v2 + jnp.where(low, zero, sq1), axis=1, keepdims=True)
    inv_a = lax.rsqrt(sum_a * (1.0 / C3) + EPSILON)
    inv_b = lax.rsqrt(sum_b * (1.0 / C3) + EPSILON)
    return (
        silu(v0 * inv_a * gains[0]),
        silu(v1 * jnp.where(low, inv_a, inv_b) * gains[1]),
        silu(v2 * inv_b * gains[2]),
    )


def weave(*streams):
    lists = []
    for stream in streams:
        lists.append(list(stream))
    order = []
    for place, steps in enumerate(lists):
        order += [((n + 0.5) / len(steps), place, step) for n, step in enumerate(steps)]
    for _, _, step in sorted(order, key=lambda entry: entry[:2]):
        step()


FIRST = ("raw1", "act0", "act1", "actd0", "actd1")
SHARED = (*FIRST, "raw2", "act2", "actd2", "res0", "res1", "resd0", "resd1")
INNER = (2, COLS - 2)
RIMS = ((0, 2), (COLS, 2))
RIM_SLOTS = (0, 1, 2, 3, WIDE - 4, WIDE - 3, WIDE - 2, WIDE - 1)


def stages(refs, row_count, col_count, col_size):
    x_ref, p_ref, q_ref = refs.get("x"), refs.get("p"), refs.get("q")
    odd_row, even_row = refs.get("odd_row"), refs.get("even_row")
    even_col, odd_col = refs.get("even_col"), refs.get("odd_col")
    w3_ref, wu_ref, w4_ref = refs.get("w3"), refs.get("wu"), refs.get("w4")
    out_ref = refs.get("out")

    def several(name, count):
        return [refs.get(name + str(n)) for n in range(count)]

    raw, act, act_d, halo_d = several("raw", 3), several("act", 3), several("actd", 3), several("halo", 3)
    rims = several("rim", 3)
    res, res_d, res_h = several("res", 2), several("resd", 2), several("resh", 2)
    z4, s4, act4_d = several("z", 3), several("s", 2), several("fine", 3)
    row = lax.axis_index("row")
    col = lax.axis_index("section") * col_size + lax.axis_index("col")
    row_odd = lax.rem(row, 2) == 1
    col_odd = lax.rem(col, 2) == 1
    first_row, last_row = row == 0, row == row_count - 1
    first_col, last_col = col == 0, col == col_count - 1

    def wide(value):
        return value.astype(F32)

    def pick(flag, one, other, *index):
        return wide(jnp.where(flag, one[index], other[index]))

    def above(lanes):
        return pick(row_odd, even_row, odd_row, slice(0, 2), lanes)

    def below(lanes):
        return pick(row_odd, odd_row, even_row, slice(0, 2), lanes)

    def left(lanes):
        return pick(col_odd, even_col, odd_col, slice(0, ROWS + 4), lanes)

    def right(lanes):
        return pick(col_odd, odd_col, even_col, slice(0, ROWS + 4), lanes)

    def keep(inside, value):
        return jnp.where(inside, value, jnp.zeros_like(value))

    def rounded(value):
        return value.astype(BF16).astype(F32)

    def pair_of(ref, *index):
        return jnp.concatenate([ref[(0,) + index], ref[(1,) + index]], axis=1).astype(BF16)

    g3 = refs["g3"][...]
    gains = (
        g3[:, 0:128],
        jnp.concatenate([g3[:, 128:192], g3[:, 0:64]], axis=1),
        g3[:, 64:192],
    )

    def place_of(jj, rim):
        if rim:
            return rims, len(RIM_SLOTS), RIM_SLOTS.index(jj)
        return act, WIDE, jj

    def load_column(group, jj, rim):
        held, slots, slot = place_of(jj, rim)
        base = jj * EXT
        for q in range(3):
            if 2 <= jj < WIDE - 2:
                at = (jj - 2) * COLX + (3 * (group - 1) + q) * 128
                if group == 0:
                    at = (jj - 2) * COLP + q * 128
                src, strip_at = (x_ref, at) if group else (p_ref, XW + at)
                strip = slice(strip_at, strip_at + 128)
                raw[group][q, base : base + 16, :] = wide(src[:, at : at + 128])
                raw[group][q, base + 16 : base + 18, :] = above(strip)
                raw[group][q, base + 18 : base + 20, :] = below(strip)
            else:
                side, lane = (left, jj) if jj < 2 else (right, jj - WIDE + 2)
                at = lane * COLX + (3 * (group - 1) + q) * 128
                if group == 0:
                    at = 2 * COLX + lane * COLP + q * 128
                raw[group][q, base : base + 20, :] = side(slice(at, at + 128))
        tiles = [raw[group][q, base : base + EXT, :] for q in range(3)]
        if group:
            tiles = norm_pair(*tiles, gains)
        for half, pair in enumerate(split_pair(*tiles)):
            at = (half * slots + slot) * EXT
            for q in range(2):
                held[group][q, at : at + 2, :] = pair[q][16:18]
                held[group][q, at + 2 : at + 18, :] = pair[q][0:16]
                held[group][q, at + 18 : at + 20, :] = pair[q][18:20]

    def copy_column(group, jj):
        slot = RIM_SLOTS.index(jj)
        for half in range(2):
            source, target = (half * WIDE + jj) * EXT, (half * len(RIM_SLOTS) + slot) * EXT
            for q in range(2):
                rims[group][q, target : target + EXT, :] = act[group][q, source : source + EXT, :]

    def shift_column(group, jj, rim):
        held, slots, slot = place_of(jj, rim)
        for half in range(2):
            slab = half * WIDE + jj
            for dy in range(3):
                at = (half * slots + slot) * EXT + 1 + dy
                both = pair_of(held[group], slice(at, at + ROWS), slice(None))
                act_d[group][dy, slab * ROWS : (slab + 1) * ROWS, :] = both

    def gather_rows(group, dx, dy, rim):
        held, slots, start = (rims, len(RIM_SLOTS), 0) if rim else (act, WIDE, INNER[0])
        for half in range(2):
            at = (half * slots + start + dx) * EXT + dy
            tiles = []
            for q in range(2):
                sides = [held[group][q, pl.ds(at + skip, 8, stride=EXT), :] for skip in (0, 17)]
                tiles.append(jnp.concatenate(sides, axis=0))
            both = jnp.concatenate(tiles, axis=1).astype(BF16)
            halo_d[group][3 * dx + dy, half * 16 : (half + 1) * 16, :] = both

    def coarse_steps(group, columns, rim=False):
        for jj in columns:
            yield lambda jj=jj: (load_column(group, jj, rim), shift_column(group, jj, rim))

    def copy_steps(group):
        for jj in RIM_SLOTS[2:6]:
            yield lambda jj=jj: copy_column(group, jj)

    def row_steps(group, rim=False):
        for dx in range(3):
            for dy in range(3):
                yield lambda dx=dx, dy=dy: gather_rows(group, dx, dy, rim)

    center = {}
    edges = {}

    def conv_three(frames, runs):
        kernels = []
        pieces = []
        for dy in range(3):
            for dx in range(3):
                kernels.append(w3_ref[3 * dy + dx])
                for t in range(3):
                    parts = []
                    for p, k in frames:
                        group, half = p + (k + t) // 2, (k + t) % 2
                        for start, count in runs:
                            at = (half * WIDE + start + dx) * ROWS
                            parts.append(act_d[group][dy, at : at + count * ROWS, :])
                        parts.append(halo_d[group][3 * dx + dy, half * 16 : (half + 1) * 16, :])
                    pieces.append(jnp.concatenate(parts, axis=0))
        got = nt_dot(jnp.concatenate(pieces, axis=1), jnp.concatenate(kernels, axis=1))
        at = 0
        for p, k in frames:
            for start, count in runs:
                for jm in range(start, start + count):
                    center[p, k, jm] = got[at : at + ROWS]
                    at += ROWS
            edges[p, k] = got[at : at + 16]
            at += 16

    def conv_three_steps(runs, *batches):
        for frames in batches:
            yield lambda frames=frames: conv_three(frames, runs)

    b3 = refs["b3"][...] if "b3" in refs else None

    def put_res(p, rows, value):
        res[p][0, rows, :] = value[:, 0:128]
        rest = jnp.zeros((value.shape[0], 64), F32)
        res[p][1, rows, :] = jnp.concatenate([value[:, 128:192], rest], axis=1)

    def result_column(p, jm):
        at = (jm + 1) * EXT
        tiles = [raw[p + 1][q, at : at + ROWS, :] for q in range(3)]
        for k, skip in enumerate(split_pair(*tiles)):
            slab = k * MID + jm
            value = center[p, k, jm] + b3
            value = rounded(value + jnp.concatenate([skip[0], skip[1][:, 0:64]], axis=1))
            if jm == 0:
                value = keep(jnp.logical_not(first_col), value)
            if jm == MID - 1:
                value = keep(jnp.logical_not(last_col), value)
            put_res(p, pl.ds(slab * EXT + 1, ROWS), value)

    def result_rows(p, side, start, count):
        inside = jnp.logical_not(last_row if side else first_row)
        column = lax.broadcasted_iota(jnp.int32, (count, 1), 0) + start
        if start == 0:
            inside = jnp.logical_and(inside, jnp.logical_or(column > 0, jnp.logical_not(first_col)))
        if start + count == MID:
            inside = jnp.logical_and(inside, jnp.logical_or(column < MID - 1, jnp.logical_not(last_col)))
        rows = pl.ds((start + 1) * EXT + (18 if side else 17), count, stride=EXT)
        tiles = [raw[p + 1][q, rows, :] for q in range(3)]
        for k, skip in enumerate(split_pair(*tiles)):
            at = 8 * side + (4 if start == COLS else 0)
            value = edges[p, k][at : at + count] + b3
            value = rounded(value + jnp.concatenate([skip[0], skip[1][:, 0:64]], axis=1))
            at = (k * MID + start) * EXT + (17 if side else 0)
            put_res(p, pl.ds(at, count, stride=EXT), keep(inside, value))

    def shift_result(p, jm):
        for k in range(2):
            slab = k * MID + jm
            for r in range(2):
                rows = slice(slab * EXT + r, slab * EXT + r + ROWS)
                res_d[p][r, slab * ROWS : (slab + 1) * ROWS, :] = pair_of(res[p], rows, slice(None))

    def gather_result(p, place):
        r, c = divmod(place, 2)
        for k in range(2):
            rows = pl.ds((k * MID + c) * EXT + ROWS + r, 16, stride=EXT)
            res_h[p][place, k * 16 : (k + 1) * 16, :] = pair_of(res[p], rows, slice(None))

    def result_steps(p, runs):
        for start, count in runs:
            for side in range(2):
                yield lambda side=side, start=start, count=count: result_rows(p, side, start, count)
            for jm in range(start, start + count):
                yield lambda jm=jm: (result_column(p, jm), shift_result(p, jm))

    def gather_steps(p):
        for place in range(4):
            yield lambda place=place: gather_result(p, place)

    span = COLS + 1
    total = [{}, {}]

    def conv_up(p, half):
        pieces = []
        for r in range(2):
            for c in range(2):
                parts = []
                for k in range(2):
                    at = (k * MID + c) * ROWS
                    parts.append(res_d[p][r, at : at + span * ROWS, :])
                    parts.append(res_h[p][2 * r + c, k * 16 : (k + 1) * 16, :])
                pieces.append(jnp.concatenate(parts, axis=0))
        got = nt_dot(jnp.concatenate(pieces, axis=1), wu_ref[half * 256 : (half + 1) * 256, :])
        for k in range(2):
            total[p][half, k] = got[k * (span + 1) * ROWS : (k + 1) * (span + 1) * ROWS]

    def conv_up_steps(p):
        for half in range(2):
            yield lambda half=half: conv_up(p, half)

    def padded(name):
        return jnp.concatenate([refs[name][...], jnp.zeros((1, 32), F32)], axis=1)

    bias_up = padded("bu") if "bu" in refs else None
    g4 = padded("g4") if "g4" in refs else None

    def act_four(value):
        square = jnp.sum(value * value, axis=1, keepdims=True)
        return silu(value * lax.rsqrt(square * (1.0 / C4) + EPSILON) * g4)

    def fine_rows(p, a, b, k):
        at = span * ROWS
        lanes = slice(b * 128, (b + 1) * 128)
        value = rounded(total[p][a, k][at : at + span, lanes] + bias_up)
        ext = FROWS if a else FROWS + 1
        rows = pl.ds((0 if b else FEXT) + ext, span, stride=2 * FEXT)
        if a:
            s4[p][k, rows, :] = value
        value = act_four(value)
        index = lax.broadcasted_iota(jnp.int32, (span, 1), 0)
        if b:
            inside = jnp.logical_or(index > 0, jnp.logical_not(first_col))
        else:
            inside = jnp.logical_or(index < span - 1, jnp.logical_not(last_col))
        if not a:
            inside = jnp.logical_and(inside, jnp.logical_not(last_row))
        z4[p + 1][k, rows, :] = keep(inside, value)

    top = lax.broadcasted_iota(jnp.int32, (ROWS, 1), 0) > 0
    rows_in = jnp.logical_or(top, jnp.logical_not(first_row))

    def fine_column(p, b, j):
        fx = 2 * j if b else 2 * j + 1
        for k in range(2):
            for a in range(2):
                lanes = slice(b * 128, (b + 1) * 128)
                value = rounded(total[p][a, k][j * ROWS : (j + 1) * ROWS, lanes] + bias_up)
                rows = pl.ds(fx * FEXT + 1 - a, ROWS, stride=2)
                if 1 <= fx <= 2 * COLS:
                    s4[p][k, rows, :] = value
                value = act_four(value)
                if a:
                    value = keep(rows_in, value)
                if fx == 0:
                    value = keep(jnp.logical_not(first_col), value)
                if fx == FINE - 1:
                    value = keep(jnp.logical_not(last_col), value)
                z4[p + 1][k, rows, :] = value
        shift_fine(p + 1, fx)

    def shift_fine(group, fx):
        for dy in range(3):
            rows = slice(fx * FEXT + dy, fx * FEXT + dy + FROWS)
            act4_d[group][dy, fx * FROWS : (fx + 1) * FROWS, :] = pair_of(z4[group], rows, slice(None))

    def fine_steps(p):
        for a in range(2):
            for b in range(2):
                for k in range(2):
                    yield lambda a=a, b=b, k=k: fine_rows(p, a, b, k)
        for j in range(span):
            for b in (1, 0):
                yield lambda b=b, j=j: fine_column(p, b, j)

    def put_cached(fx, row0, joined, first):
        rows = joined.shape[0]
        for t in range(2):
            at = first + t * C4
            value = jnp.concatenate([joined[:, at : at + C4], jnp.zeros((rows, 32), F32)], axis=1)
            z4[0][t, fx * FEXT + row0 : fx * FEXT + row0 + rows, :] = value

    def cached_column(fx):
        if 0 < fx < FINE - 1:
            at = (fx - 1) * COLQ
            start = at // 128 * 128
            first = at - start
            strip = slice(XW + PW + start, XW + PW + start + 256)
            put_cached(fx, 1, wide(q_ref[:, start : start + 256]), first)
            put_cached(fx, 0, above(strip)[1:2], first)
            put_cached(fx, FROWS + 1, below(strip)[0:1], first)
        else:
            lanes = (right if fx else left)(slice(QAT, QAT + 384))
            put_cached(fx, 0, lanes[17:18], 0)
            put_cached(fx, 1, lanes[0:16], 0)
            put_cached(fx, 1 + ROWS, lanes[0:16], COLQ)
            put_cached(fx, FROWS + 1, lanes[18:19], 0)
        shift_fine(0, fx)

    def cached_steps():
        for fx in range(FINE):
            yield lambda fx=fx: cached_column(fx)

    done = [{}, {}]

    def conv_four(p, start, count):
        size = count * FROWS
        pieces = []
        for dy in range(3):
            for dx in range(3):
                at = (dx + start) * FROWS
                pieces += [act4_d[group][dy, at : at + size, :] for group in (p, p + 1)]
        kernel = jnp.concatenate([w4_ref[dy] for dy in range(3)], axis=1)
        got = nt_dot(jnp.concatenate(pieces, axis=1), kernel)
        for n in range(count):
            done[p][start + n] = got[n * FROWS : (n + 1) * FROWS]

    def conv_four_steps(p):
        for start, count in ((0, COLS + 2), (COLS + 2, COLS - 2)):
            yield lambda start=start, count=count: conv_four(p, start, count)

    bias_four = jnp.concatenate([refs["b4"][...]] * 2, axis=1) if "b4" in refs else None
    first = lane_mask(FROWS, C4)

    def out_column(p, fx):
        rows = slice((fx + 1) * FEXT + 1, (fx + 1) * FEXT + 1 + FROWS)
        other = pltpu.roll(s4[p][1, rows, :], C4, 1)
        skip = jnp.concatenate([jnp.where(first, s4[p][0, rows, :], other), other[:, 0:64]], axis=1)
        value = (done[p][fx] + bias_four + skip).astype(BF16)
        out_ref[:, fx * 384 + p * 192 : fx * 384 + (p + 1) * 192] = value

    def out_steps(p):
        for fx in range(2 * COLS):
            yield lambda fx=fx: out_column(p, fx)

    return types.SimpleNamespace(**locals())


OWN = range(2, WIDE - 2)
EARLY, LATE = OWN[:6], OWN[6:]


def first_inner_kernel(names, sizes, *all_refs):
    refs = dict(zip(names, all_refs))
    col = lax.axis_index("section") * sizes[2] + lax.axis_index("col")

    @pl.when(col == sizes[1] // 2)
    def _():
        do = stages(refs, *sizes)
        weave(do.coarse_steps(0, OWN), do.coarse_steps(1, EARLY))


def inner_kernel(names, sizes, *all_refs):
    refs = dict(zip(names, all_refs))
    col = lax.axis_index("section") * sizes[2] + lax.axis_index("col")

    @pl.when(col != sizes[1] // 2)
    def _():
        do = stages(refs, *sizes)
        weave(do.coarse_steps(0, OWN), do.coarse_steps(1, EARLY))

    do = stages(refs, *sizes)
    weave(do.coarse_steps(1, LATE), do.row_steps(0))
    weave(do.row_steps(1))
    weave(do.conv_three_steps([INNER], [(0, 0), (0, 1)]), do.coarse_steps(2, OWN))
    weave(do.row_steps(2))
    weave(do.conv_three_steps([INNER], [(1, 0), (1, 1)]), do.result_steps(0, [INNER]))
    weave(do.result_steps(1, [INNER]))


def main_kernel(names, sizes, *all_refs):
    do = stages(dict(zip(names, all_refs)), *sizes)
    sides = (0, 1, WIDE - 2, WIDE - 1)
    weave(*[do.copy_steps(group) for group in range(3)])
    weave(*[do.coarse_steps(group, sides, True) for group in range(3)])
    weave(*[do.row_steps(group, True) for group in range(3)])
    weave(do.conv_three_steps(RIMS, [(0, 0), (0, 1)], [(1, 0), (1, 1)]), do.cached_steps())
    weave(do.result_steps(0, RIMS))
    weave(do.gather_steps(0))
    weave(do.result_steps(1, RIMS))
    weave(do.gather_steps(1))
    weave(do.conv_up_steps(0))
    weave(do.conv_up_steps(1), do.fine_steps(0))
    weave(do.conv_four_steps(0), do.fine_steps(1))
    weave(do.conv_four_steps(1), do.out_steps(0))
    weave(do.out_steps(1))


def split_pairs(flat_ref, parts, pairs, taps, stride):
    low = lane_mask(taps, 64)
    zero = jnp.zeros((taps, 128), F32)
    for pair in pairs:
        v0, v1, v2 = [flat_ref[:, (3 * pair + q) * 128 : (3 * pair + q + 1) * 128].astype(F32) for q in range(3)]
        r1, r2 = pltpu.roll(v1, 64, 1), pltpu.roll(v2, 64, 1)
        at = 2 * pair * stride
        parts[0, at : at + taps, :] = v0
        parts[1, at : at + taps, :] = jnp.where(low, v1, zero)
        parts[0, at + stride : at + stride + taps, :] = jnp.where(low, r1, r2)
        parts[1, at + stride : at + stride + taps, :] = jnp.where(low, r2, zero)


def prep_three_kernel(flat_ref, out_ref, parts):
    split_pairs(flat_ref, parts, range(C3 // 2), 27, 40)
    for tap in range(27):
        both = [parts[q, pl.ds(tap, C3, stride=40), :] for q in range(2)]
        t, place = divmod(tap, 9)
        out_ref[place, :, t * 256 : (t + 1) * 256] = jnp.concatenate(both, axis=1).astype(BF16)


def prep_four_kernel(up_ref, four_ref, up_out, four_out, parts_u, parts_f):
    split_pairs(up_ref, parts_u, range(C4 // 2), 9, 24)
    taps = {}
    for tap in range(9):
        for q in range(2):
            taps[tap, q] = parts_u[q, pl.ds(tap, C4, stride=24), :]
    spans = {(0, 0): (0,), (0, 1): (1, 2), (1, 0): (0, 1), (1, 1): (2,)}
    rest = jnp.zeros((32, 256), BF16)
    for a in range(2):
        for b in range(2):
            at = (2 * a + b) * 128
            for r in range(2):
                for c in range(2):
                    tiles = []
                    for q in range(2):
                        total = None
                        for dy in spans[a, r]:
                            for dx in spans[b, c]:
                                one = taps[3 * dy + dx, q]
                                total = one if total is None else total + one
                        tiles.append(total)
                    lanes = slice((2 * r + c) * 256, (2 * r + c + 1) * 256)
                    up_out[at : at + C4, lanes] = jnp.concatenate(tiles, axis=1).astype(BF16)
                    up_out[at + C4 : at + 128, lanes] = rest
    lane = lax.broadcasted_iota(jnp.int32, (27, 128), 1)
    empty = jnp.zeros((27, 128), F32)
    for four in range(C4 // 4):
        at = 3 * four * 128
        v0, v1, v2 = [four_ref[:, at + q * 128 : at + (q + 1) * 128].astype(F32) for q in range(3)]
        second = jnp.where(lane < 32, pltpu.roll(v0, 32, 1), pltpu.roll(v1, 32, 1))
        third = jnp.where(lane < 64, pltpu.roll(v1, 64, 1), pltpu.roll(v2, 64, 1))
        for m, value in enumerate((v0, second, third, pltpu.roll(v2, 96, 1))):
            at = (4 * four + m) * 40
            parts_f[at : at + 27, :] = jnp.where(lane < C4, value, empty)
    none = jnp.zeros((C4, 128), BF16)
    for place in range(9):
        dy, dx = divmod(place, 3)
        at = dx * 512
        four_out[dy, 0:C4, at + 384 : at + 512] = none
        four_out[dy, C4 : 2 * C4, at : at + 128] = none
        for t in range(3):
            kernel = parts_f[pl.ds(9 * t + place, C4, stride=40), :].astype(BF16)
            four_out[dy, 0:C4, at + t * 128 : at + (t + 1) * 128] = kernel
            four_out[dy, C4 : 2 * C4, at + (t + 1) * 128 : at + (t + 2) * 128] = kernel


def row_strips_kernel(x_ref, p_ref, q_ref, even_ref, odd_ref, x_own, p_own, q_own, sems):
    row_odd = lax.rem(lax.axis_index("row"), 2) == 1
    parts = ((p_ref, p_own, XW), (x_ref, x_own, 0), (q_ref, q_own, XW + PW))
    copies = [
        pltpu.make_async_copy(source, own, sems.at[n]) for n, (source, own, _) in enumerate(parts)
    ]
    for copy in copies:
        copy.start()
    for copy, (_, own, at) in zip(copies, parts):
        copy.wait()
        rows, width = own.shape
        low, high = own[0:2, :], own[rows - 2 : rows, :]
        even_ref[:, at : at + width] = jnp.where(row_odd, low, high)
        odd_ref[:, at : at + width] = jnp.where(row_odd, high, low)


def col_strips_kernel(x_ref, p_ref, q_ref, odd_row, even_row, _, out_ref, *, col_size, parity):
    row_odd = lax.rem(lax.axis_index("row"), 2) == 1
    col = lax.axis_index("section") * col_size + lax.axis_index("col")
    take_low = lax.rem(col, 2) == parity
    strips = (
        jnp.where(row_odd, even_row[...], odd_row[...]),
        jnp.where(row_odd, odd_row[...], even_row[...]),
    )

    def put(rows, at, low, high):
        out_ref[rows, at : at + low.shape[1]] = jnp.where(take_low, low, high)

    start = 0
    for ref, at, width, lanes in (
        (x_ref, 0, XW, 2 * COLX), (p_ref, 2 * COLX, PW, 2 * COLP), (q_ref, QAT, QW, COLQ)
    ):
        high = width - lanes
        if ref is q_ref:
            for half in range(2):
                rows = slice(half * ROWS, (half + 1) * ROWS)
                put(slice(0, ROWS), at + half * lanes, ref[rows, 0:lanes], ref[rows, high:width])
        else:
            put(slice(0, ROWS), at, ref[:, 0:lanes], ref[:, high:width])
        for place, strip in enumerate(strips):
            rows = slice(ROWS + 2 * place, ROWS + 2 * place + 2)
            put(rows, at, strip[:, start : start + lanes], strip[:, start + high : start + width])
            if ref is q_ref:
                out_ref[rows, at + lanes : at + 2 * lanes] = jnp.zeros((2, lanes), BF16)
        start += width


def call(kernel, operands, outputs, scratch, megabytes, moved=0, unread=0, space=pl.ANY, aliases=None):
    cost = pl.CostEstimate(flops=moved, bytes_accessed=moved, transcendentals=0) if moved else None
    vmem = pl.BlockSpec(memory_space=pltpu.VMEM)
    shapes = [
        shape if isinstance(shape, jax.ShapeDtypeStruct) else jax.ShapeDtypeStruct(shape, BF16)
        for shape in outputs
    ]
    got = pl.pallas_call(
        kernel,
        out_shape=shapes,
        in_specs=[vmem] * (len(operands) - unread) + [pl.BlockSpec(memory_space=space)] * unread,
        out_specs=[vmem] * len(outputs),
        scratch_shapes=scratch,
        cost_estimate=cost,
        input_output_aliases=aliases or {},
        compiler_params=pltpu.CompilerParams(vmem_limit_bytes=megabytes * 1024 * 1024),
    )(*operands)
    return got[0] if len(outputs) == 1 else got


def swap_pairs(count, start):
    out = []
    for low in range(start, count - 1, 2):
        out += [(low, low + 1), (low + 1, low)]
    return out


def shards(
    section_input,
    cache_three,
    gain_three,
    bias_three,
    weight_three,
    weight_up,
    bias_up,
    cache_four,
    gain_four,
    weight_four,
    bias_four,
):
    row_count = lax.axis_size("row")
    col_size = lax.axis_size("col")
    col_count = lax.axis_size("section") * col_size
    tile = (section_input, cache_three, cache_four)

    row_strip = (2, XW + PW + QW)
    own = [pltpu.VMEM(block.shape, BF16) for block in tile]
    even_strip, odd_strip = call(
        row_strips_kernel,
        tile,
        [row_strip] * 2,
        [*own, pltpu.SemaphoreType.DMA((3,))],
        62, unread=3, space=pltpu.HBM,
    )
    even_row = lax.ppermute(even_strip, "row", swap_pairs(row_count, 0))
    odd_row = lax.ppermute(odd_strip, "row", swap_pairs(row_count, 1))

    w3 = call(
        prep_three_kernel,
        (weight_three,),
        [(9, C3, 3 * 256)],
        [pltpu.VMEM((2, 40 * C3, 128), F32)],
        16, 8_000_000,
    )
    col_strip = (ROWS + 4, QAT + 2 * COLQ)

    def swap_columns(parity, after):
        def col_kernel(*refs):
            col_strips_kernel(*refs, col_size=col_size, parity=1 - parity)

        strip = call(col_kernel, (*tile, odd_row, even_row, after), [col_strip], [], 4, unread=1)
        return lax.ppermute(strip, ("section", "col"), swap_pairs(col_count, parity))

    sizes = (row_count, col_count, col_size)
    rows = (section_input, cache_three, odd_row, even_row)
    params = (gain_three.reshape(1, C3), bias_three.reshape(1, C3), w3)
    names = ("x", "p", "odd_row", "even_row", "g3", "b3", "w3")

    def block(shape, dtype=F32):
        return jax.ShapeDtypeStruct(shape, dtype)

    raw = block((3, 16 * EXT, 128))
    act = block((2, (2 * WIDE + 4) * EXT, 128))
    act_d = block((3, 2 * WIDE * ROWS, 256), BF16)
    res = block((2, (2 * MID + 5) * EXT, 128))
    res_d = block((2, 2 * MID * ROWS, 256), BF16)
    first = [raw, act, act, act_d, act_d]
    rest = [raw, act, act_d, res, res, res_d, res_d]
    halo = pltpu.VMEM((9, 2 * 16, 256), BF16)
    inner_scratch = [pltpu.VMEM(raw.shape, F32), halo, halo, halo]
    scratch_names = ("raw0", "halo0", "halo1", "halo2")

    even_col = swap_columns(0, w3)
    *held, token = call(
        functools.partial(first_inner_kernel, (*names[:-2], *FIRST, "token", "raw0"), sizes),
        (*rows, *params[:1]),
        [*first, (16, 128)],
        inner_scratch[:1],
        8, 2_000_000,
    )
    odd_col = swap_columns(1, token)
    wu, w4 = call(
        prep_four_kernel,
        (weight_up, weight_four),
        [(4 * 128, 4 * 256), (3, 2 * C4, 3 * 512)],
        [
            pltpu.VMEM((2, 24 * C4, 128), F32),
            pltpu.VMEM((40 * C4, 128), F32),
        ],
        16, 8_000_000,
    )

    held = call(
        functools.partial(
            inner_kernel, (*names, *["_" + name for name in FIRST], *SHARED, *scratch_names), sizes
        ),
        (*rows, *params, *held),
        [*first, *rest],
        inner_scratch,
        16, 8_000_000,
        aliases={len(names) + n: n for n in range(len(first))},
    )

    operands = (
        *tile, odd_row, even_row, even_col, odd_col,
        *params, wu, bias_up.reshape(1, C4), gain_four.reshape(1, C4), w4, bias_four.reshape(1, C4),
    )
    names = (
        "x", "p", "q", "odd_row", "even_row", "even_col", "odd_col",
        "g3", "b3", "w3", "wu", "bu", "g4", "w4", "b4",
    )
    scratch = list(inner_scratch)
    scratch += [pltpu.VMEM((2, (2 * len(RIM_SLOTS) + 2) * EXT, 128), F32)] * 3
    scratch += [pltpu.VMEM((4, 2 * 16, 256), BF16)] * 2
    scratch += [pltpu.VMEM((2, FINE * FEXT, 128), F32)] * 3
    scratch += [pltpu.VMEM((2, FINE * FEXT, 128), F32)] * 2
    scratch += [pltpu.VMEM((3, FINE * FROWS, 256), BF16)] * 3
    scratch_names += ("rim0", "rim1", "rim2", "resh0", "resh1", "z0", "z1", "z2", "s0", "s1", "fine0", "fine1", "fine2")
    got = call(
        functools.partial(
            main_kernel, (*names, *["_" + name for name in SHARED], "out", *SHARED, *scratch_names), sizes
        ),
        (*operands, *held),
        [(FROWS, 2 * COLS * FRAMES * C4), *first, *rest],
        scratch,
        24,
        aliases={len(names) + n: n + 1 for n in range(len(SHARED))},
    )
    return got[0]


def solution(mesh):
    tiled = P("row", ("section", "col"))
    return jax.shard_map(
        shards,
        mesh=mesh,
        in_specs=(tiled, tiled, P(), P(), P(), P(), P(), tiled, P(), P(), P()),
        out_specs=tiled,
        check_vma=False,
    )
```
